32 devices in a mesh: span: 4 (over z), blk: 8 (over y, x, core).
Axes of the slice: x: 2, y: 2, z: 4, core: 2. Of those that a mesh axis runs over, the one named last changes fastest.
Arguments:
- populations: float32 [19, 64, 32, 128], P(None, 'blk', 'span'), may hold values from 0 to 0.5
- thermal: float32 [7, 64, 32, 128], P(None, 'blk', 'span'), may hold values from 0.1 to 0.2
- solid_mask: int32 [64, 32, 128], P('blk', 'span'), may hold values 0 or 1
- metal_temp: float32 [4, 2048], P('span', 'blk'), may hold values from 0.5 to 1.5
- conduction: float32 [1024, 2048], P('span', 'blk'), may hold values from 0 to 1
- wall_count: int32 [4, 8], P('span', 'blk'), may hold values from 256 to 512, as said below
- wall_node: int32 [4, 4096], P('span', 'blk'), may hold values from 0 to 8191
- wall_owner: int32 [4, 4096, 1], P('span', 'blk'), may hold values from 0 to 7; in each aligned block of 512 rows (0 to 511, 512 to 1023, ..., all dimensions but the last counted through in order) at most 96 rows name the same one
- wall_cell: int32 [4, 4096], P('span', 'blk'), may hold values from 0 to 255
Outputs:
- flow_out: float32 [19, 64, 32, 128], P(None, 'blk', 'span')
- heat_out: float32 [7, 64, 32, 128], P(None, 'blk', 'span')
- metal_out: float32 [4, 2048], P('span', 'blk')
The draws below stay inside these ranges and needn't reach their ends.
Inputs may be any that keep to these rules, and one draw needn't show every extreme that they name: `wall_owner`: among the 512 wall entries of one device at most 96 name one owner; in some devices' entries one owner is named exactly 96 times. `wall_count`: some device has all 512 entries live in every draw.
All inputs are finite; a program needn't handle non-finite values. No bound on the sum of `solid_mask` on one device may be relied on, other than what follows from the above.
Results may differ from the reference program's by a relative error of at most 0.0001.
Values sent between devices are 32-bit elements; how exact they have to be, the bound alone decides.
No kernel may reach another device: no remote copies, remote signals or barrier semaphores. Data moves between devices by JAX's collectives and lax.ppermute only.
A program may use at most 64 MiB of HBM per device.

```python
import math
import jax
import jax.numpy as jnp
import numpy as np
from jax import lax

BX = 8
BZ = 8
BY = 128
W_DEV = 512
M = 256
STEPS = 2
NX = 64
NZ = 32
CAP = 96
N_SPAN = 4
N_BLK = 8


FLOW_WEIGHTS = [1.0 / 3.0] + [1.0 / 18.0] * 6 + [1.0 / 36.0] * 12


def draw_populations(key, part):
    key = jax.random.fold_in(key, 11)
    spread = 0.2
    noise = jax.random.uniform(key, (19, NX, NZ, BY), jnp.float32, 1.0 - spread, 1.0 + spread)
    weights = jnp.array(FLOW_WEIGHTS, jnp.float32)[:, None, None, None]
    return weights * noise


def draw_conduction(key, part):
    key = jax.random.fold_in(key, 23)
    reach = 0.6
    rows = jnp.arange(N_SPAN * M)[:, None] % M
    columns = jnp.arange(N_BLK * M)[None, :] % M
    identity = jnp.where(rows == columns, 0.7, 0.0).astype(jnp.float32)
    spread = jax.random.uniform(key, (N_SPAN * M, N_BLK * M), jnp.float32, 0.0, reach) / M
    return identity + spread


def draw_wall_count(key, part):
    key = jax.random.fold_in(key, 37)
    first_key, second_key = jax.random.split(key)
    counts = jax.random.randint(first_key, (N_SPAN * N_BLK,), W_DEV // 2, W_DEV + 1, jnp.int32)
    chosen = jax.random.randint(second_key, (), 0, N_SPAN * N_BLK, jnp.int32)
    counts = counts.at[chosen].set(W_DEV)
    return counts.reshape(N_SPAN, N_BLK)


def plant(result, key, least, high):
    shape = result.shape
    place = [jax.random.randint(jax.random.fold_in(key, axis), (), 0, shape[axis]) for axis in range(len(shape))]
    result = result.at[tuple(place)].set(least)
    longest = shape.index(max(shape))
    place[longest] = (place[longest] + 1) % shape[longest]
    return result.at[tuple(place)].set(high)


def block_scale(stream_key, extent, cuts, low, high):
    gain, own = 1.0, jax.random.fold_in(stream_key, 6)
    for position, blocks in cuts:
        heights = jnp.exp(jax.random.uniform(jax.random.fold_in(own, position), (blocks,), jnp.float32, low / len(cuts), high / len(cuts)))
        gain = gain * jnp.repeat(heights, extent[position] // blocks).reshape([-1 if axis == position else 1 for axis in range(len(extent))])
    return gain


def routed_block(own_key, own, number, rows, number_of, top, most, slope):
    sequence = jax.random.permutation(own_key, number_of)
    heavy_load, common = shares(number_of, rows * top, most, slope, True), shares(number_of, rows * top, most, slope, False)
    places = jnp.arange(number_of)

    def named(lengths, rotation):
        used = int((lengths > 0).sum())
        fixed = max(1, used // 4)
        passed = fixed + (places - fixed + rotation * (used - fixed)) % max(1, number_of - fixed)
        return jnp.zeros((number_of,), jnp.int32).at[sequence[jnp.where(places < fixed, places, passed)]].set(jnp.asarray(lengths, jnp.int32))

    lengths = jnp.where(number % 4 == 0, named(heavy_load, number // 4), named(common, number - number // 4 - 1))
    mixed = jax.random.permutation(jax.random.fold_in(own, 3), number_of)
    donor, taker = mixed[0:number_of // 2 * 2:2], mixed[1:number_of // 2 * 2:2]
    margin = jnp.minimum(lengths[donor] - 1, most - lengths[taker]) // 2
    margin = jnp.where((donor == sequence[0]) | (taker == sequence[0]) | (lengths[taker] == 0), 0, jnp.maximum(margin, 0))
    passed = jax.random.randint(jax.random.fold_in(own, 4), (number_of // 2,), 0, 1 << 20) % (margin + 1)
    lengths = lengths.at[donor].add(-passed).at[taker].add(passed)
    labels = jnp.searchsorted(jnp.cumsum(lengths), jnp.arange(rows * top), side="right").astype(jnp.int32)
    grid = labels.reshape(top, rows).T
    grid = grid[jax.random.permutation(jax.random.fold_in(own, 1), rows)]
    rotation = jax.random.randint(jax.random.fold_in(own, 2), (rows, 1), 0, top)
    return jnp.take_along_axis(grid, (jnp.arange(top)[None, :] + rotation) % top, axis=1)


def shares(count, total, most, lean, full):
    portions = [(1 << 20) // math.isqrt(rank ** lean) + 1 for rank in range(1, count + 1)]
    largest = most if full else min(most, max(-(-total // count), total * portions[0] // sum(portions)))
    least = 1 if total - largest >= count - 1 else 0
    given, spare = [largest] + [least] * (count - 1), total - largest - least * (count - 1)
    while spare > 0:
        movable = [i for i in range(1, count) if given[i] < largest] or [i for i in range(1, count) if given[i] < most]
        whole, remaining = sum([portions[i] for i in movable]), spare
        for i in movable:
            addition = min(most - given[i], max(1, remaining * portions[i] // whole), spare)
            given[i] = given[i] + addition
            spare = spare - addition
    return np.array(given)


def setup_inputs(seed: int = 0) -> dict:
    arg_keys = jax.random.split(jax.random.key(seed), 10)
    populations = draw_populations(jax.random.fold_in(arg_keys[9], 71), 0)
    thermal = jnp.clip(0.1 + 0.1 * jax.random.uniform(arg_keys[1], (7, NX, NZ, BY), jnp.float32) ** block_scale(arg_keys[1], (7, NX, NZ, BY), ((1, 8), (2, 4)), -0.2, 0.2), 0.1, 0.2)
    solid_mask = plant((jax.random.randint(arg_keys[2], (NX, NZ, BY), 0, 5) < 1).astype(jnp.int32), jax.random.fold_in(arg_keys[2], 1), 0, 1)
    metal_temp = jnp.clip(0.5 + 1.0 * jax.random.uniform(arg_keys[3], (N_SPAN, N_BLK * M), jnp.float32) ** block_scale(arg_keys[3], (N_SPAN, N_BLK * M), ((0, 4), (1, 8)), -0.2, 0.2), 0.5, 1.5)
    conduction = draw_conduction(jax.random.fold_in(arg_keys[9], 71), 0)
    wall_count = draw_wall_count(jax.random.fold_in(arg_keys[9], 71), 0)
    wall_node = plant(jax.random.randint(arg_keys[6], (N_SPAN, N_BLK * W_DEV), 0, BX * BZ * BY), jax.random.fold_in(arg_keys[6], 1), 0, (BX * BZ * BY) - 1).astype(jnp.int32)
    wall_owner_keys = jax.random.split(jax.random.fold_in(arg_keys[7], 1), N_SPAN * (N_BLK * W_DEV) // W_DEV)
    wall_owner_turns = jax.random.permutation(jax.random.fold_in(arg_keys[7], 3), N_SPAN * (N_BLK * W_DEV) // W_DEV)
    wall_owner = jax.vmap(lambda own, number: routed_block(jax.random.fold_in(arg_keys[7], 2), own, number, W_DEV, N_BLK, 1, CAP, 2))(wall_owner_keys, wall_owner_turns).reshape((N_SPAN, N_BLK * W_DEV, 1))
    wall_cell = plant(jax.random.randint(arg_keys[8], (N_SPAN, N_BLK * W_DEV), 0, M), jax.random.fold_in(arg_keys[8], 1), 0, M - 1).astype(jnp.int32)
    return dict(populations=populations, thermal=thermal, solid_mask=solid_mask, metal_temp=metal_temp, conduction=conduction, wall_count=wall_count, wall_node=wall_node, wall_owner=wall_owner, wall_cell=wall_cell)


VELOCITY_FLOW = [(0, 0, 0), (1, 0, 0), (-1, 0, 0), (0, 1, 0), (0, -1, 0), (0, 0, 1), (0, 0, -1),
                 (1, 1, 0), (-1, -1, 0), (1, -1, 0), (-1, 1, 0), (1, 0, 1), (-1, 0, -1), (1, 0, -1), (-1, 0, 1),
                 (0, 1, 1), (0, -1, -1), (0, 1, -1), (0, -1, 1)]
WEIGHT_FLOW = [1.0 / 3.0] + [1.0 / 18.0] * 6 + [1.0 / 36.0] * 12
OPPOSITE_FLOW = [0, 2, 1, 4, 3, 6, 5, 8, 7, 10, 9, 12, 11, 14, 13, 16, 15, 18, 17]
VELOCITY_HEAT = VELOCITY_FLOW[:7]
WEIGHT_HEAT = [0.25] + [0.125] * 6
OPPOSITE_HEAT = [0, 2, 1, 4, 3, 6, 5]
RELAX_FLOW = 0.8
RELAX_HEAT = 0.9
WALL_COEFF = 0.5
METAL_GAIN = 0.5


def collide(flow, heat, solid, source):
    density = jnp.sum(flow, axis=0)
    velocity_parts = []
    for axis_pick in range(3):
        positive = sum([flow[component] for component in range(19) if VELOCITY_FLOW[component][axis_pick] == 1])
        negative = sum([flow[component] for component in range(19) if VELOCITY_FLOW[component][axis_pick] == -1])
        velocity_parts.append((positive - negative) / density)
    speed_sq = velocity_parts[0] ** 2 + velocity_parts[1] ** 2 + velocity_parts[2] ** 2
    projections = []
    for velocity in VELOCITY_FLOW:
        projections.append(velocity[0] * velocity_parts[0] + velocity[1] * velocity_parts[1] + velocity[2] * velocity_parts[2])
    flow_eq = jnp.stack([WEIGHT_FLOW[component] * density * (1.0 + 3.0 * projections[component] + 4.5 * projections[component] * projections[component] - 1.5 * speed_sq) for component in range(19)])
    fluid = (solid == 0)[None]
    flow_back = jnp.stack([flow[other] for other in OPPOSITE_FLOW])
    flow_post = jnp.where(fluid, flow - (flow - flow_eq) / RELAX_FLOW, flow_back)
    temper = jnp.sum(heat, axis=0)
    heat_eq = jnp.stack([WEIGHT_HEAT[component] * temper * (1.0 + 4.0 * projections[component]) for component in range(7)])
    heat_back = jnp.stack([heat[other] for other in OPPOSITE_HEAT])
    heat_post = jnp.where(fluid, heat - (heat - heat_eq) / RELAX_HEAT, heat_back)
    heat_post = heat_post + jnp.stack([WEIGHT_HEAT[component] * source for component in range(7)])
    return flow_post, heat_post


def stream_whole(post, velocities):
    return jnp.stack([jnp.roll(post[component], (velocity[0], velocity[2], velocity[1]), axis=(0, 1, 2)) for component, velocity in enumerate(velocities)])


def to_blocks(field):
    shaped = field.reshape(N_BLK, BX, N_SPAN, BZ, BY).transpose(2, 0, 1, 3, 4)
    return shaped.reshape(N_SPAN, N_BLK, BX * BZ * BY)


def from_blocks(blocks):
    shaped = blocks.reshape(N_SPAN, N_BLK, BX, BZ, BY).transpose(1, 2, 0, 3, 4)
    return shaped.reshape(NX, NZ, BY)


def reference(populations, thermal, solid_mask, metal_temp, conduction, wall_count, wall_node, wall_owner, wall_cell):
    nodes = BX * BZ * BY
    flow = populations
    heat = thermal
    metal = metal_temp.reshape(N_SPAN, N_BLK, M)
    tiles = conduction.reshape(N_SPAN, M, N_BLK, M).transpose(0, 2, 1, 3)
    node_list = wall_node.reshape(N_SPAN, N_BLK, W_DEV)
    owner_list = wall_owner.reshape(N_SPAN, N_BLK, W_DEV)
    cell_list = wall_cell.reshape(N_SPAN, N_BLK, W_DEV)
    live = jnp.arange(W_DEV, dtype=jnp.int32)[None, None, :] < wall_count[:, :, None]
    span_ids = jnp.arange(N_SPAN, dtype=jnp.int32)[:, None, None]
    blk_ids = jnp.arange(N_BLK, dtype=jnp.int32)[None, :, None]
    target = ((span_ids * N_BLK + owner_list) * M + cell_list).astype(jnp.int32).reshape(-1)
    node_target = ((span_ids * N_BLK + blk_ids) * nodes + node_list).astype(jnp.int32).reshape(-1)
    for tick in range(STEPS):
        temper = jnp.sum(heat, axis=0)
        wall_temp = jnp.take_along_axis(to_blocks(temper), node_list, axis=2)
        metal_flat = metal.reshape(-1)
        flux = jnp.where(live, WALL_COEFF * (wall_temp - metal_flat[target].reshape(N_SPAN, N_BLK, W_DEV)), 0.0)
        gained = jnp.zeros((N_SPAN * N_BLK * M,), jnp.float32).at[target].add(flux.reshape(-1))
        gained = gained.reshape(N_SPAN, N_BLK, M)
        metal = jnp.einsum("sbij,sbj->sbi", tiles, metal + METAL_GAIN * gained, precision=lax.Precision.HIGHEST)
        source = jnp.zeros((N_SPAN * N_BLK * nodes,), jnp.float32).at[node_target].add(-flux.reshape(-1))
        source = from_blocks(source)
        flow_post, heat_post = collide(flow, heat, solid_mask, source)
        flow = stream_whole(flow_post, VELOCITY_FLOW)
        heat = stream_whole(heat_post, VELOCITY_HEAT)
    return flow, heat, metal.reshape(N_SPAN, N_BLK * M)
```

```python
import functools

import jax
import jax.numpy as jnp
from jax import lax
from jax.experimental import pallas as pl
from jax.experimental.pallas import tpu as pltpu
from jax.sharding import PartitionSpec as P

VELOCITY_FLOW = [
    (0, 0, 0),
    (1, 0, 0),
    (-1, 0, 0),
    (0, 1, 0),
    (0, -1, 0),
    (0, 0, 1),
    (0, 0, -1),
    (1, 1, 0),
    (-1, -1, 0),
    (1, -1, 0),
    (-1, 1, 0),
    (1, 0, 1),
    (-1, 0, -1),
    (1, 0, -1),
    (-1, 0, 1),
    (0, 1, 1),
    (0, -1, -1),
    (0, 1, -1),
    (0, -1, 1),
]
WEIGHT_FLOW = [1.0 / 3.0] + [1.0 / 18.0] * 6 + [1.0 / 36.0] * 12
OPPOSITE = [0, 2, 1, 4, 3, 6, 5, 8, 7, 10, 9, 12, 11, 14, 13, 16, 15, 18, 17]
WEIGHT_HEAT = [0.25] + [0.125] * 6
VELOCITY = VELOCITY_FLOW + VELOCITY_FLOW[:7]
FLOWS, HEATS = 19, 7
ALL = FLOWS + HEATS
RELAX_FLOW = 0.8
RELAX_HEAT = 0.9
WALL_COEFF = 0.5
METAL_GAIN = 0.5

FACE_RIGHT = [(i, 0) for i in range(ALL) if VELOCITY[i][0] >= 0] + [
    (i, 1) for i in range(ALL) if VELOCITY[i][0] == 1
]
FACE_LEFT = [(i, 0) for i in range(ALL) if VELOCITY[i][0] <= 0] + [
    (i, 1) for i in range(ALL) if VELOCITY[i][0] == -1
]
FACES = len(FACE_RIGHT)
UP = [i for i in range(ALL) if VELOCITY[i][2] == 1]
DOWN = [i for i in range(ALL) if VELOCITY[i][2] == -1]
EDGES = len(UP)

ROW_TEMPER, ROW_OWNER, ROW_CELL, ROW_NODE, ROW_SUMS = 2, 6, 10, 14, 24
LANES = 128
F32 = jnp.float32
BF16 = jnp.bfloat16


def params(mebibytes=32):
    return pltpu.CompilerParams(vmem_limit_bytes=mebibytes * 1024 * 1024)


def in_vmem(count):
    return [pl.BlockSpec(memory_space=pltpu.VMEM)] * count


def shape(*dims):
    return jax.ShapeDtypeStruct(dims, F32)


def split(value):
    high = value.astype(BF16)
    rest = value - high.astype(F32)
    middle = rest.astype(BF16)
    low = (rest - middle.astype(F32)).astype(BF16)
    return high, middle, low


def dot(left, right, dims):
    return lax.dot_general(left, right, (dims, ((), ())), preferred_element_type=F32)


def rows_of(row, count):
    return lax.broadcasted_iota(jnp.int32, (count, row.shape[1]), 0) == row


def hot(mask):
    return jnp.where(mask, 1.0, 0.0).astype(BF16)


def look_up(table, row_hot, lane_mask):
    turned = jnp.transpose(table)
    found = sum([dot(part, row_hot, ((1,), (0,))) for part in split(turned)])
    return jnp.sum(jnp.where(lane_mask, found, 0.0), axis=0, keepdims=True)


def add_up(values, row_mask, lane_hot):
    count = row_mask.shape[0]
    stacked = jnp.concatenate(
        [jnp.where(row_mask, part.astype(F32), 0.0) for part in split(values)], axis=0
    ).astype(BF16)
    sums = dot(stacked, lane_hot, ((1,), (1,)))
    return sums[:count] + sums[count : 2 * count] + sums[2 * count :]


def one_row(block):
    return jnp.concatenate([block[r : r + 1] for r in range(block.shape[0])], axis=1)


def put_rows(ref, start, row):
    for r in range(row.shape[1] // LANES):
        ref[start + r : start + r + 1, :] = row[:, r * LANES : (r + 1) * LANES]


def lists_of(packet):
    owner = one_row(packet[ROW_OWNER : ROW_OWNER + 4]).astype(jnp.int32)
    cell = one_row(packet[ROW_CELL : ROW_CELL + 4]).astype(jnp.int32)
    node = one_row(packet[ROW_NODE : ROW_NODE + 4]).astype(jnp.int32)
    return owner, cell, node


def packet_kernel(count_ref, heat_ref, metal_ref, node_ref, owner_ref, cell_ref, out_ref, *, blocks):
    wide, deep, lanes = heat_ref.shape[1:]
    temper = heat_ref[0]
    for k in range(1, HEATS):
        temper = temper + heat_ref[k]
    temper = temper.reshape(wide * deep, lanes)
    node = node_ref[...]
    cell = cell_ref[...]
    entries = node.shape[1]
    live = lax.broadcasted_iota(jnp.int32, (1, entries), 1) < count_ref[0, 0]
    owner = jnp.where(live, owner_ref[...], -1)
    wall = look_up(temper, hot(rows_of(node >> 7, wide * deep)), rows_of(node & 127, lanes))
    cell_hot = hot(rows_of(cell & 127, lanes))
    row_mask = rows_of(owner * 2 + (cell >> 7), 2 * blocks)
    out_ref[0:ROW_SUMS, :] = jnp.zeros((ROW_SUMS, lanes), F32)
    put_rows(out_ref, 0, metal_ref[...])
    put_rows(out_ref, ROW_TEMPER, wall)
    put_rows(out_ref, ROW_OWNER, owner.astype(F32))
    put_rows(out_ref, ROW_CELL, cell.astype(F32))
    put_rows(out_ref, ROW_NODE, node.astype(F32))
    out_ref[ROW_SUMS : ROW_SUMS + 2 * blocks, :] = add_up(wall, row_mask, cell_hot)
    out_ref[ROW_SUMS + 2 * blocks : ROW_SUMS + 4 * blocks, :] = dot(
        hot(row_mask), cell_hot, ((1,), (1,))
    )


def collide_flow(flow, solid):
    density = flow[0]
    for i in range(1, FLOWS):
        density = density + flow[i]
    inverse = 1.0 / density
    speed = []
    for axis in range(3):
        ahead = [flow[i] for i in range(FLOWS) if VELOCITY[i][axis] == 1]
        behind = [flow[i] for i in range(FLOWS) if VELOCITY[i][axis] == -1]
        speed.append((sum(ahead[1:], ahead[0]) - sum(behind[1:], behind[0])) * inverse)
    base = 1.0 - 1.5 * (speed[0] * speed[0] + speed[1] * speed[1] + speed[2] * speed[2])
    scaled = {w: density * (w / RELAX_FLOW) for w in set(WEIGHT_FLOW)}
    keep = 1.0 - 1.0 / RELAX_FLOW
    post = [None] * FLOWS
    rest = scaled[WEIGHT_FLOW[0]] * base + keep * flow[0]
    post[0] = jnp.where(solid, flow[0], rest)
    for i in range(1, FLOWS, 2):
        along = None
        for axis in range(3):
            c = VELOCITY[i][axis]
            if c == 0:
                continue
            term = speed[axis]
            if along is None:
                along = term if c == 1 else -term
            else:
                along = along + term if c == 1 else along - term
        weight = scaled[WEIGHT_FLOW[i]]
        even = weight * (base + 4.5 * along * along)
        odd = weight * (3.0 * along)
        j = OPPOSITE[i]
        post[i] = jnp.where(solid, flow[j], even + odd + keep * flow[i])
        post[j] = jnp.where(solid, flow[i], even - odd + keep * flow[j])
    return post, speed


def collide_heat(heat, temper, speed, solid):
    keep = 1.0 - 1.0 / RELAX_HEAT
    post = [None] * HEATS
    post[0] = jnp.where(
        solid, heat[0], temper * (WEIGHT_HEAT[0] / RELAX_HEAT) + keep * heat[0]
    )
    scaled = temper * (WEIGHT_HEAT[1] / RELAX_HEAT)
    for axis in range(3):
        i = 2 * axis + 1
        j = i + 1
        odd = scaled * (4.0 * speed[axis])
        post[i] = jnp.where(solid, heat[j], scaled + odd + keep * heat[i])
        post[j] = jnp.where(solid, heat[i], scaled - odd + keep * heat[j])
    return post


def collide_kernel(
    place_ref, flow_ref, heat_ref, solid_ref, postf_ref, posth_ref, senda_ref, sendb_ref
):
    wide = flow_ref.shape[1]
    odd = place_ref[0] % 2 == 1
    for x in range(wide):
        flow = [flow_ref[i, x] for i in range(FLOWS)]
        heat = [heat_ref[k, x] for k in range(HEATS)]
        solid = solid_ref[x] != 0
        temper = heat[0]
        for k in range(1, HEATS):
            temper = temper + heat[k]
        post, speed = collide_flow(flow, solid)
        post = post + collide_heat(heat, temper, speed, solid)
        for i in range(FLOWS):
            postf_ref[i, x] = post[i]
        for k in range(HEATS):
            posth_ref[k, x] = post[FLOWS + k]

    def plane(i, x):
        return postf_ref[i, x] if i < FLOWS else posth_ref[i - FLOWS, x]

    def fill(right_ref, left_ref):
        for n, (i, depth) in enumerate(FACE_RIGHT):
            right_ref[n] = plane(i, wide - 1 - depth)
        right_ref[FACES] = solid_ref[wide - 1].astype(F32)
        for n, (i, depth) in enumerate(FACE_LEFT):
            left_ref[n] = plane(i, depth)
        left_ref[FACES] = solid_ref[0].astype(F32)

    @pl.when(odd)
    def _():
        fill(sendb_ref, senda_ref)

    @pl.when(jnp.logical_not(odd))
    def _():
        fill(senda_ref, sendb_ref)


def sides(odd, a_ref, b_ref):
    def low(n):
        return jnp.where(odd, a_ref[n], b_ref[n])

    def high(n):
        return jnp.where(odd, b_ref[n], a_ref[n])

    return low, high


def planes(postf_ref, posth_ref, low, high, wide, source_ref):
    def get(i, x):
        if x < 0:
            value = low(FACE_RIGHT.index((i, -1 - x)))
        elif x >= wide:
            value = high(FACE_LEFT.index((i, x - wide)))
        elif i < FLOWS:
            value = postf_ref[i, x]
        else:
            value = posth_ref[i - FLOWS, x]
        if i >= FLOWS and source_ref is not None:
            value = value + WEIGHT_HEAT[i - FLOWS] * source_ref[x + 2]
        return value

    return get


def wall_flux(table, lists, wall, blocks):
    owner, cell, node = lists
    row = jnp.where(owner < 0, -1, owner * 8 + (cell >> 7))
    row_mask = rows_of(row, blocks * 8)
    at = look_up(table, hot(row_mask), rows_of(cell & 127, LANES))
    return jnp.where(owner < 0, 0.0, WALL_COEFF * (wall - at))


def tile_sums(value, block):
    rows = lax.broadcasted_iota(jnp.int32, value.shape, 0)
    return [
        jnp.sum(jnp.where(rows == 2 * block + h, value, 0.0), axis=0, keepdims=True)
        for h in range(2)
    ]


def conduct(conduction, halves):
    vector = jnp.concatenate(halves, axis=1)
    parts = split(vector)
    rows = lax.broadcasted_iota(jnp.int32, (16, vector.shape[1]), 0)
    stacked = jnp.zeros((16, vector.shape[1]), F32)
    for r, part in enumerate(parts):
        stacked = jnp.where(rows == r, part.astype(F32), stacked)
    stacked = stacked.astype(BF16)
    out = sum([dot(stacked, part, ((1,), (1,))) for part in split(conduction)])
    return out[0:1] + out[1:2] + out[2:3]


def source_kernel(
    place_ref,
    postf_ref,
    posth_ref,
    recva_ref,
    recvb_ref,
    gathered_ref,
    conduction_ref,
    senda_ref,
    sendb_ref,
    metal_ref,
    source_ref,
    *,
    blocks,
):
    wide, deep, lanes = postf_ref.shape[1:]
    block = place_ref[0]
    left = lax.rem(block + blocks - 1, blocks)
    right = lax.rem(block + 1, blocks)
    table = jnp.concatenate([gathered_ref[d, 0:8] for d in range(blocks)], axis=0)
    packets = [gathered_ref[d, 0:ROW_SUMS] for d in (left, block, right)]
    lists = [lists_of(packet) for packet in packets]
    joined = [jnp.concatenate([item[n] for item in lists], axis=1) for n in range(3)]
    wall = jnp.concatenate(
        [one_row(packet[ROW_TEMPER : ROW_TEMPER + 4]) for packet in packets], axis=1
    )
    flux = -wall_flux(table, joined, wall, blocks)
    entries = lists[0][0].shape[1]
    columns = wide * deep
    for n, (first, count, start) in enumerate(
        ((columns - 2 * deep, 2 * deep, 0), (0, columns, 2), (0, 2 * deep, wide + 2))
    ):
        node = lists[n][2]
        source = add_up(
            flux[:, n * entries : (n + 1) * entries],
            rows_of((node >> 7) - first, count),
            hot(rows_of(node & 127, lanes)),
        )
        source_ref[start : start + count // deep] = source.reshape(count // deep, deep, lanes)

    low, high = sides(block % 2 == 1, recva_ref, recvb_ref)
    get = planes(postf_ref, posth_ref, low, high, wide, source_ref)

    def fill(up_ref, down_ref):
        for ref, comps, row in ((up_ref, UP, deep - 1), (down_ref, DOWN, 0)):
            for j in range(wide + 2):
                for n, i in enumerate(comps):
                    value = get(i, j - 1 - VELOCITY[i][0])
                    at = j * EDGES + n
                    ref[at : at + 1, :] = value[row : row + 1, :]

    for ref in (senda_ref, sendb_ref):
        ref[ref.shape[0] - 8 :, :] = jnp.zeros((8, lanes), F32)

    @pl.when(place_ref[1] % 2 == 1)
    def _():
        fill(sendb_ref, senda_ref)

    @pl.when(place_ref[1] % 2 == 0)
    def _():
        fill(senda_ref, sendb_ref)

    sums = gathered_ref[0, ROW_SUMS : ROW_SUMS + 4 * blocks]
    for d in range(1, blocks):
        sums = sums + gathered_ref[d, ROW_SUMS : ROW_SUMS + 4 * blocks]
    total = tile_sums(sums[: 2 * blocks], block)
    count = tile_sums(sums[2 * blocks :], block)
    own = gathered_ref[block, 0:8]
    halves = []
    for h in range(2):
        metal = own[h : h + 1]
        halves.append(metal + METAL_GAIN * WALL_COEFF * (total[h] - count[h] * metal))
    metal_ref[...] = jnp.zeros(metal_ref.shape, F32)
    put_rows(metal_ref, 0, conduct(conduction_ref[...], halves))


def stream(get, edge, deep, i, x):
    cx, cy, cz = VELOCITY[i]
    value = get(i, x - cx)
    if cz != 0:
        rows = lax.broadcasted_iota(jnp.int32, value.shape, 0)
        if cz == 1:
            value = jnp.where(rows == 0, edge(i, x), pltpu.roll(value, 1, 0))
        else:
            value = jnp.where(rows == deep - 1, edge(i, x), pltpu.roll(value, deep - 1, 0))
    if cy != 0:
        value = pltpu.roll(value, cy % value.shape[1], 1)
    return value


def edge_rows(odd, a_ref, b_ref, first):
    def edge(i, x):
        comps = UP if VELOCITY[i][2] == 1 else DOWN
        at = (x - first) * EDGES + comps.index(i)
        a = a_ref[at : at + 1, :]
        b = b_ref[at : at + 1, :]
        if VELOCITY[i][2] == 1:
            return jnp.where(odd, a, b)
        return jnp.where(odd, b, a)

    return edge


def heat_kernel(
    place_ref,
    posth_ref,
    recva_ref,
    recvb_ref,
    source_ref,
    edgea_ref,
    edgeb_ref,
    gathered_ref,
    heat_ref,
    temper_ref,
    wall_ref,
    sums_ref,
    *,
    blocks,
):
    wide, deep, lanes = posth_ref.shape[1:]
    block = place_ref[0]
    left = lax.rem(block + blocks - 1, blocks)
    right = lax.rem(block + 1, blocks)
    low, high = sides(block % 2 == 1, recva_ref, recvb_ref)
    get = planes(None, posth_ref, low, high, wide, source_ref)
    edge = edge_rows(place_ref[1] % 2 == 1, edgea_ref, edgeb_ref, -1)
    for x in range(-1, wide + 1):
        temper = None
        for k in range(HEATS):
            value = stream(get, edge, deep, FLOWS + k, x)
            heat_ref[k, x + 1] = value
            temper = value if temper is None else temper + value
        temper_ref[x + 1] = temper
    columns = wide * deep
    walls = []
    own = None
    for n, (device, first, count, start) in enumerate(
        ((left, columns - deep, deep, 0), (block, 0, columns, 1), (right, 0, deep, wide + 1))
    ):
        owner, cell, node = lists_of(gathered_ref[device, 0:ROW_SUMS])
        table = temper_ref[start : start + count // deep].reshape(count, lanes)
        wall = look_up(
            table, hot(rows_of((node >> 7) - first, count)), rows_of(node & 127, lanes)
        )
        put_rows(wall_ref, 4 * n, wall)
        if n == 1:
            row_mask = rows_of(owner * 2 + (cell >> 7), 2 * blocks)
            sums_ref[...] = add_up(wall, row_mask, hot(rows_of(cell & 127, lanes)))
    wall_ref[12:16] = jnp.zeros((4, lanes), F32)


def flow_kernel(
    place_ref,
    postf_ref,
    recva_ref,
    recvb_ref,
    edgea_ref,
    edgeb_ref,
    heat_ref,
    temper_ref,
    solid_ref,
    outf_ref,
    outh_ref,
):
    wide, deep, lanes = postf_ref.shape[1:]
    low, high = sides(place_ref[0] % 2 == 1, recva_ref, recvb_ref)
    get = planes(postf_ref, None, low, high, wide, None)
    edge = edge_rows(place_ref[1] % 2 == 1, edgea_ref, edgeb_ref, -1)
    for x in range(-1, wide + 1):
        flow = [stream(get, edge, deep, i, x) for i in range(FLOWS)]
        if x < 0:
            solid = low(FACES) != 0
        elif x >= wide:
            solid = high(FACES) != 0
        else:
            solid = solid_ref[x] != 0
        post, speed = collide_flow(flow, solid)
        heat = [heat_ref[k, x + 1] for k in range(HEATS)]
        posth = collide_heat(heat, temper_ref[x + 1], speed, solid)
        for i in range(FLOWS):
            outf_ref[i, x + 1] = post[i]
        for k in range(HEATS):
            outh_ref[k, x + 1] = posth[k]


def edge_kernel(
    place_ref,
    postf_ref,
    posth_ref,
    wall_ref,
    metals_ref,
    gathered_ref,
    senda_ref,
    sendb_ref,
    source_ref,
    *,
    blocks,
):
    wide = postf_ref.shape[1] - 2
    deep, lanes = postf_ref.shape[2:]
    block = place_ref[0]
    left = lax.rem(block + blocks - 1, blocks)
    right = lax.rem(block + 1, blocks)
    table = jnp.concatenate([metals_ref[d] for d in range(blocks)], axis=0)
    lists = [lists_of(gathered_ref[d, 0:ROW_SUMS]) for d in (left, block, right)]
    joined = [jnp.concatenate([item[n] for item in lists], axis=1) for n in range(3)]
    wall = one_row(wall_ref[0:12])
    flux = -wall_flux(table, joined, wall, blocks)
    entries = lists[0][0].shape[1]
    columns = wide * deep
    for n, (first, count, start) in enumerate(
        ((columns - deep, deep, 0), (0, columns, 1), (0, deep, wide + 1))
    ):
        node = lists[n][2]
        source = add_up(
            flux[:, n * entries : (n + 1) * entries],
            rows_of((node >> 7) - first, count),
            hot(rows_of(node & 127, lanes)),
        )
        source_ref[start : start + count // deep] = source.reshape(count // deep, deep, lanes)

    def fill(up_ref, down_ref):
        for ref, comps, row in ((up_ref, UP, deep - 1), (down_ref, DOWN, 0)):
            for x in range(wide):
                for n, i in enumerate(comps):
                    at = x + 1 - VELOCITY[i][0]
                    if i < FLOWS:
                        value = postf_ref[i, at]
                    else:
                        value = posth_ref[i - FLOWS, at]
                        value = value + WEIGHT_HEAT[i - FLOWS] * source_ref[at]
                    where = x * EDGES + n
                    ref[where : where + 1, :] = value[row : row + 1, :]

    @pl.when(place_ref[1] % 2 == 1)
    def _():
        fill(sendb_ref, senda_ref)

    @pl.when(place_ref[1] % 2 == 0)
    def _():
        fill(senda_ref, sendb_ref)


def final_kernel(
    place_ref, postf_ref, posth_ref, source_ref, edgea_ref, edgeb_ref, flow_ref, heat_ref
):
    wide, deep, lanes = flow_ref.shape[1:]

    def get(i, x):
        if i < FLOWS:
            return postf_ref[i, x + 1]
        return posth_ref[i - FLOWS, x + 1] + WEIGHT_HEAT[i - FLOWS] * source_ref[x + 1]

    edge = edge_rows(place_ref[1] % 2 == 1, edgea_ref, edgeb_ref, 0)
    for x in range(wide):
        for i in range(FLOWS):
            flow_ref[i, x] = stream(get, edge, deep, i, x)
        for k in range(HEATS):
            heat_ref[k, x] = stream(get, edge, deep, FLOWS + k, x)


def metal_kernel(place_ref, metal_ref, sums_ref, gathered_ref, conduction_ref, out_ref, *, blocks):
    block = place_ref[0]
    sums = sums_ref[0]
    counts = gathered_ref[0, ROW_SUMS + 2 * blocks : ROW_SUMS + 4 * blocks]
    for d in range(1, blocks):
        sums = sums + sums_ref[d]
        counts = counts + gathered_ref[d, ROW_SUMS + 2 * blocks : ROW_SUMS + 4 * blocks]
    total = tile_sums(sums, block)
    count = tile_sums(counts, block)
    halves = []
    for h in range(2):
        metal = metal_ref[h : h + 1]
        halves.append(metal + METAL_GAIN * WALL_COEFF * (total[h] - count[h] * metal))
    out_ref[...] = conduct(conduction_ref[...], halves)


def swap(value, axis, offset):
    count = lax.axis_size(axis)
    pairs = []
    for first in range(offset, count + offset, 2):
        one, other = first % count, (first + 1) % count
        pairs += [(one, other), (other, one)]
    return lax.ppermute(value, axis, pairs)


def local(
    populations,
    thermal,
    solid_mask,
    metal_temp,
    conduction,
    wall_count,
    wall_node,
    wall_owner,
    wall_cell,
):
    blocks = lax.axis_size("blk")
    wide, deep, lanes = solid_mask.shape
    place = jnp.stack([lax.axis_index("blk"), lax.axis_index("span")]).astype(jnp.int32)
    smem = pl.BlockSpec(memory_space=pltpu.SMEM)
    rows = ROW_SUMS + 4 * blocks

    def call(kernel, count, outs, name, flops=1000000):
        return pl.pallas_call(
            kernel,
            in_specs=[smem] + in_vmem(count),
            out_specs=jax.tree.map(lambda _: in_vmem(1)[0], outs),
            out_shape=outs,
            compiler_params=params(),
            name=name,
        )

    packet = call(
        functools.partial(packet_kernel, blocks=blocks), 5, shape(rows, lanes), "wall_packet"
    )(wall_count, thermal, metal_temp, wall_node, wall_owner.reshape(1, -1), wall_cell)
    gathered = lax.all_gather(packet, "blk")
    postf, posth, senda, sendb = call(
        collide_kernel,
        3,
        (
            shape(FLOWS, wide, deep, lanes),
            shape(HEATS, wide, deep, lanes),
            shape(FACES + 1, deep, lanes),
            shape(FACES + 1, deep, lanes),
        ),
        "collide_first",
    )(place, populations, thermal, solid_mask)
    recva = swap(senda, "blk", 0)
    recvb = swap(sendb, "blk", 1)
    edge_count = -(-(wide + 2) * EDGES // 8) * 8
    edgea, edgeb, metal, source = call(
        functools.partial(source_kernel, blocks=blocks),
        6,
        (
            shape(edge_count, lanes),
            shape(edge_count, lanes),
            shape(8, lanes),
            shape(wide + 4, deep, lanes),
        ),
        "source_first",
    )(place, postf, posth, recva, recvb, gathered, conduction)
    metals = lax.all_gather(metal, "blk")
    edgea = swap(edgea, "span", 0)
    edgeb = swap(edgeb, "span", 1)
    heat, temper, wall, sums = call(
        functools.partial(heat_kernel, blocks=blocks),
        7,
        (
            shape(HEATS, wide + 2, deep, lanes),
            shape(wide + 2, deep, lanes),
            shape(16, lanes),
            shape(2 * blocks, lanes),
        ),
        "heat_second",
    )(place, posth, recva, recvb, source, edgea, edgeb, gathered)
    sums = lax.all_gather(sums, "blk")
    postf, posth = call(
        flow_kernel,
        8,
        (shape(FLOWS, wide + 2, deep, lanes), shape(HEATS, wide + 2, deep, lanes)),
        "collide_second",
    )(place, postf, recva, recvb, edgea, edgeb, heat, temper, solid_mask)
    edgea, edgeb, source = call(
        functools.partial(edge_kernel, blocks=blocks),
        5,
        (
            shape(wide * EDGES, lanes),
            shape(wide * EDGES, lanes),
            shape(wide + 2, deep, lanes),
        ),
        "source_second",
    )(place, postf, posth, wall, metals, gathered)
    edgea = swap(edgea, "span", 0)
    edgeb = swap(edgeb, "span", 1)
    flow, heat = call(
        final_kernel,
        5,
        (shape(FLOWS, wide, deep, lanes), shape(HEATS, wide, deep, lanes)),
        "stream_last",
    )(place, postf, posth, source, edgea, edgeb)
    metal = call(
        functools.partial(metal_kernel, blocks=blocks), 4, shape(1, metal_temp.shape[1]), "metal_last"
    )(place, metal, sums, gathered, conduction)
    return (flow, heat, metal)


def solution(mesh):
    in_specs = (
        P(None, "blk", "span", None),
        P(None, "blk", "span", None),
        P("blk", "span", None),
        P("span", "blk"),
        P("span", "blk"),
        P("span", "blk"),
        P("span", "blk"),
        P("span", "blk", None),
        P("span", "blk"),
    )
    out_specs = (P(None, "blk", "span", None), P(None, "blk", "span", None), P("span", "blk"))
    return jax.shard_map(local, mesh=mesh, in_specs=in_specs, out_specs=out_specs, check_vma=False)
```

```python
import jax
import jax.numpy as jnp
from jax import lax
from jax.experimental import pallas as pl
from jax.experimental.pallas import tpu as pltpu
from jax.sharding import PartitionSpec as P

VELOCITY_FLOW = [
    (0, 0, 0),
    (1, 0, 0),
    (-1, 0, 0),
    (0, 1, 0),
    (0, -1, 0),
    (0, 0, 1),
    (0, 0, -1),
    (1, 1, 0),
    (-1, -1, 0),
    (1, -1, 0),
    (-1, 1, 0),
    (1, 0, 1),
    (-1, 0, -1),
    (1, 0, -1),
    (-1, 0, 1),
    (0, 1, 1),
    (0, -1, -1),
    (0, 1, -1),
    (0, -1, 1),
]
WEIGHT_FLOW = [1.0 / 3.0] + [1.0 / 18.0] * 6 + [1.0 / 36.0] * 12
OPPOSITE = [0, 2, 1, 4, 3, 6, 5, 8, 7, 10, 9, 12, 11, 14, 13, 16, 15, 18, 17]
WEIGHT_HEAT = [0.25] + [0.125] * 6
VELOCITY = VELOCITY_FLOW + VELOCITY_FLOW[:7]
FLOWS, HEATS = 19, 7
ALL = FLOWS + HEATS
RELAX_FLOW = 0.8
RELAX_HEAT = 0.9
WALL_COEFF = 0.5
METAL_GAIN = 0.5

FACE_RIGHT = [(i, 0) for i in range(ALL) if VELOCITY[i][0] >= 0] + [
    (i, 1) for i in range(ALL) if VELOCITY[i][0] == 1
]
FACE_LEFT = [(i, 0) for i in range(ALL) if VELOCITY[i][0] <= 0] + [
    (i, 1) for i in range(ALL) if VELOCITY[i][0] == -1
]
FACES = len(FACE_RIGHT)
UP = [i for i in range(ALL) if VELOCITY[i][2] == 1]
DOWN = [i for i in range(ALL) if VELOCITY[i][2] == -1]
EDGES = len(UP)

SOLID, COUNTS, LISTS = FACES, FACES + 1, FACES + 2
SIDE_PLANES = FACES + 4
LIST_ROWS = 12
LANES = 128
F32 = jnp.float32
BF16 = jnp.bfloat16


def params(mebibytes=32):
    return pltpu.CompilerParams(vmem_limit_bytes=mebibytes * 1024 * 1024)


def in_vmem(count):
    return [pl.BlockSpec(memory_space=pltpu.VMEM)] * count


def shape(*dims):
    return jax.ShapeDtypeStruct(dims, F32)


def split(value):
    high = value.astype(BF16)
    rest = value - high.astype(F32)
    middle = rest.astype(BF16)
    low = (rest - middle.astype(F32)).astype(BF16)
    return high, middle, low


def dot(left, right, dims):
    return lax.dot_general(left, right, (dims, ((), ())), preferred_element_type=F32)


def rows_of(row, count):
    return lax.broadcasted_iota(jnp.int32, (count, row.shape[1]), 0) == row


def hot(mask):
    return jnp.where(mask, 1.0, 0.0).astype(BF16)


def look_up(table, row_hot, lane_mask):
    turned = jnp.transpose(table)
    found = sum([dot(part, row_hot, ((1,), (0,))) for part in split(turned)])
    return jnp.sum(jnp.where(lane_mask, found, 0.0), axis=0, keepdims=True)


def add_up(values, row_mask, lane_hot):
    count = row_mask.shape[0]
    stacked = jnp.concatenate(
        [jnp.where(row_mask, part.astype(F32), 0.0) for part in split(values)], axis=0
    ).astype(BF16)
    sums = dot(stacked, lane_hot, ((1,), (1,)))
    return sums[:count] + sums[count : 2 * count] + sums[2 * count :]


def one_row(block):
    return jnp.concatenate([block[r : r + 1] for r in range(block.shape[0])], axis=1)


def put_rows(ref, start, row):
    for r in range(row.shape[1] // LANES):
        ref[start + r : start + r + 1, :] = row[:, r * LANES : (r + 1) * LANES]


def lists_of(block):
    return [one_row(block[4 * n : 4 * n + 4]).astype(jnp.int32) for n in range(3)]


def packet_kernel(
    count_ref, heat_ref, metal_ref, node_ref, owner_ref, cell_ref, out_ref, list_ref, counts_ref
):
    blocks = out_ref.shape[0]
    wide, deep, lanes = heat_ref.shape[1:]
    temper = heat_ref[0]
    for k in range(1, HEATS):
        temper = temper + heat_ref[k]
    temper = temper.reshape(wide * deep, lanes)
    node = node_ref[...]
    cell = cell_ref[...]
    entries = node.shape[1]
    live = lax.broadcasted_iota(jnp.int32, (1, entries), 1) < count_ref[0, 0]
    owner = jnp.where(live, owner_ref[...], -1)
    list_ref[8:16, :] = jnp.zeros((8, lanes), F32)
    put_rows(list_ref, 0, owner.astype(F32))
    put_rows(list_ref, 4, cell.astype(F32))
    put_rows(list_ref, 8, node.astype(F32))
    put_rows(list_ref, LIST_ROWS, metal_ref[...])
    column_hot = hot(rows_of(node >> 7, wide * deep))
    lane_mask = rows_of(node & 127, lanes)
    wall = look_up(temper, column_hot, lane_mask)
    cell_hot = hot(rows_of(cell & 127, lanes))
    row_mask = rows_of(owner * 2 + (cell >> 7), 2 * blocks)
    sums = add_up(wall, row_mask, cell_hot)
    counts = dot(hot(row_mask), cell_hot, ((1,), (1,)))
    for d in range(blocks):
        put_rows(out_ref.at[d], 0, metal_ref[...])
        out_ref[d, 2:4, :] = sums[2 * d : 2 * d + 2]
        out_ref[d, 4:6, :] = counts[2 * d : 2 * d + 2]
        out_ref[d, 6:8, :] = jnp.zeros((2, lanes), F32)
    at_nodes = dot(
        hot(rows_of(jnp.where(live, node >> 7, -1), wide * deep)), hot(lane_mask), ((1,), (1,))
    )
    counts_ref[...] = at_nodes.reshape(wide, deep, lanes)


def collide_flow(flow, solid):
    density = flow[0]
    for i in range(1, FLOWS):
        density = density + flow[i]
    inverse = 1.0 / density
    speed = []
    for axis in range(3):
        ahead = [flow[i] for i in range(FLOWS) if VELOCITY[i][axis] == 1]
        behind = [flow[i] for i in range(FLOWS) if VELOCITY[i][axis] == -1]
        speed.append((sum(ahead[1:], ahead[0]) - sum(behind[1:], behind[0])) * inverse)
    base = 1.0 - 1.5 * (speed[0] * speed[0] + speed[1] * speed[1] + speed[2] * speed[2])
    scaled = {w: density * (w / RELAX_FLOW) for w in sorted(set(WEIGHT_FLOW))}
    keep = 1.0 - 1.0 / RELAX_FLOW
    post = [None] * FLOWS
    rest = scaled[WEIGHT_FLOW[0]] * base + keep * flow[0]
    post[0] = jnp.where(solid, flow[0], rest)
    for i in range(1, FLOWS, 2):
        along = None
        for axis in range(3):
            c = VELOCITY[i][axis]
            if c == 0:
                continue
            term = speed[axis]
            if along is None:
                along = term if c == 1 else -term
            else:
                along = along + term if c == 1 else along - term
        weight = scaled[WEIGHT_FLOW[i]]
        even = weight * (base + 4.5 * along * along)
        odd = weight * (3.0 * along)
        j = OPPOSITE[i]
        post[i] = jnp.where(solid, flow[j], even + odd + keep * flow[i])
        post[j] = jnp.where(solid, flow[i], even - odd + keep * flow[j])
    return post, speed


def collide_heat(heat, temper, speed, solid):
    keep = 1.0 - 1.0 / RELAX_HEAT
    post = [None] * HEATS
    post[0] = jnp.where(
        solid, heat[0], temper * (WEIGHT_HEAT[0] / RELAX_HEAT) + keep * heat[0]
    )
    scaled = temper * (WEIGHT_HEAT[1] / RELAX_HEAT)
    for axis in range(3):
        i = 2 * axis + 1
        j = i + 1
        odd = scaled * (4.0 * speed[axis])
        post[i] = jnp.where(solid, heat[j], scaled + odd + keep * heat[i])
        post[j] = jnp.where(solid, heat[i], scaled - odd + keep * heat[j])
    return post


def lose(post, counts, temper):
    lost = counts * temper * -WALL_COEFF
    return [post[k] + WEIGHT_HEAT[k] * lost for k in range(HEATS)]


def collide_kernel(
    place_ref,
    flow_ref,
    heat_ref,
    solid_ref,
    counts_ref,
    list_ref,
    postf_ref,
    posth_ref,
    senda_ref,
    sendb_ref,
):
    wide = flow_ref.shape[1]
    odd = place_ref[0] % 2 == 1
    for x in range(wide):
        flow = [flow_ref[i, x] for i in range(FLOWS)]
        heat = [heat_ref[k, x] for k in range(HEATS)]
        solid = solid_ref[x] != 0
        temper = heat[0]
        for k in range(1, HEATS):
            temper = temper + heat[k]
        post, speed = collide_flow(flow, solid)
        posth = lose(collide_heat(heat, temper, speed, solid), counts_ref[x], temper)
        for i in range(FLOWS):
            postf_ref[i, x] = post[i]
        for k in range(HEATS):
            posth_ref[k, x] = posth[k]

    def plane(i, x):
        return postf_ref[i, x] if i < FLOWS else posth_ref[i - FLOWS, x]

    def fill(right_ref, left_ref):
        for ref, faces, edge in ((right_ref, FACE_RIGHT, wide - 1), (left_ref, FACE_LEFT, 0)):
            for n, (i, depth) in enumerate(faces):
                ref[n] = plane(i, abs(edge - depth))
            ref[SOLID] = solid_ref[edge].astype(F32)
            ref[COUNTS] = counts_ref[edge]
            ref[LISTS] = list_ref[0:8]
            ref[LISTS + 1] = list_ref[8:16]

    @pl.when(odd)
    def _():
        fill(sendb_ref, senda_ref)

    @pl.when(jnp.logical_not(odd))
    def _():
        fill(senda_ref, sendb_ref)


def sides(odd, a_ref, b_ref):
    def low(n):
        return jnp.where(odd, a_ref[n], b_ref[n])

    def high(n):
        return jnp.where(odd, b_ref[n], a_ref[n])

    return low, high


def side_lists(get):
    return lists_of(jnp.concatenate([get(LISTS), get(LISTS + 1)], axis=0))


def planes(postf_ref, posth_ref, low, high, wide, source_ref):
    def get(i, x):
        if x < 0:
            value = low(FACE_RIGHT.index((i, -1 - x)))
        elif x >= wide:
            value = high(FACE_LEFT.index((i, x - wide)))
        elif i < FLOWS:
            value = postf_ref[i, x]
        else:
            value = posth_ref[i - FLOWS, x]
        if i >= FLOWS and source_ref is not None:
            value = value + WEIGHT_HEAT[i - FLOWS] * source_ref[x + 2]
        return value

    return get


def metal_at(table, lists, shift=0):
    owner, cell, node = lists
    row = jnp.where(owner < 0, -1, owner * 8 + (cell >> 7) + shift)
    return look_up(table, hot(rows_of(row, table.shape[0])), rows_of(cell & 127, LANES))


def give(metal, row, node, count):
    return add_up(WALL_COEFF * metal, rows_of(row, count), hot(rows_of(node & 127, LANES)))


def join(lists):
    return [jnp.concatenate([item[n] for item in lists], axis=1) for n in range(3)]


def give_planes(table, lists, parts, deep, source_ref):
    metal = metal_at(table, join(lists))
    entries = lists[0][0].shape[1]
    for n, (first, count, start) in enumerate(parts):
        node = lists[n][2]
        source = give(metal[:, n * entries : (n + 1) * entries], (node >> 7) - first, node, count)
        source_ref[start : start + count // deep] = source.reshape(count // deep, deep, LANES)


def conduct(conduction, halves):
    vector = jnp.concatenate(halves, axis=1)
    parts = split(vector)
    rows = lax.broadcasted_iota(jnp.int32, (16, vector.shape[1]), 0)
    stacked = jnp.zeros((16, vector.shape[1]), F32)
    for r, part in enumerate(parts):
        stacked = jnp.where(rows == r, part.astype(F32), stacked)
    stacked = stacked.astype(BF16)
    out = sum([dot(stacked, part, ((1,), (1,))) for part in split(conduction)])
    return out[0:1] + out[1:2] + out[2:3]


def next_metal(conduction, metal, total, count):
    gained = WALL_COEFF * (total - count * metal)
    value = metal + METAL_GAIN * gained
    return conduct(conduction, [value[0:1], value[1:2]])


def source_kernel(
    place_ref,
    postf_ref,
    posth_ref,
    recva_ref,
    recvb_ref,
    list_ref,
    chunks_ref,
    conduction_ref,
    senda_ref,
    sendb_ref,
    metal_ref,
    source_ref,
):
    wide, deep, lanes = postf_ref.shape[1:]
    blocks = chunks_ref.shape[0]
    low, high = sides(place_ref[0] % 2 == 1, recva_ref, recvb_ref)
    table = chunks_ref[...].reshape(blocks * 8, lanes)
    columns = wide * deep
    give_planes(
        table,
        [side_lists(low), lists_of(list_ref[...]), side_lists(high)],
        ((columns - 2 * deep, 2 * deep, 0), (0, columns, 2), (0, 2 * deep, wide + 2)),
        deep,
        source_ref,
    )
    get = planes(postf_ref, posth_ref, low, high, wide, source_ref)
    sums = chunks_ref[0]
    for d in range(1, blocks):
        sums = sums + chunks_ref[d]
    count = sums[4:6]
    metal = next_metal(conduction_ref[...], list_ref[LIST_ROWS : LIST_ROWS + 2], sums[2:4], count)
    metal_ref[...] = jnp.zeros(metal_ref.shape, F32)
    put_rows(metal_ref, 0, metal)
    metal_ref[2:4, :] = count

    def fill(up_ref, down_ref):
        for ref, comps, row in ((up_ref, UP, deep - 1), (down_ref, DOWN, 0)):
            for j in range(wide + 2):
                for n, i in enumerate(comps):
                    value = get(i, j - 1 - VELOCITY[i][0])
                    at = j * EDGES + n
                    ref[at : at + 1, :] = value[row : row + 1, :]
            at = (wide + 2) * EDGES
            put_rows(ref, at, metal)
            ref[at + 2 : at + 2 + LIST_ROWS, :] = list_ref[0:LIST_ROWS]

    for ref in (senda_ref, sendb_ref):
        ref[ref.shape[0] - 8 :, :] = jnp.zeros((8, lanes), F32)

    @pl.when(place_ref[1] % 2 == 1)
    def _():
        fill(sendb_ref, senda_ref)

    @pl.when(place_ref[1] % 2 == 0)
    def _():
        fill(senda_ref, sendb_ref)


def stream(get, edge, deep, i, x):
    cx, cy, cz = VELOCITY[i]
    value = get(i, x - cx)
    if cz != 0:
        rows = lax.broadcasted_iota(jnp.int32, value.shape, 0)
        if cz == 1:
            value = jnp.where(rows == 0, edge(i, x), pltpu.roll(value, 1, 0))
        else:
            value = jnp.where(rows == deep - 1, edge(i, x), pltpu.roll(value, deep - 1, 0))
    if cy != 0:
        value = pltpu.roll(value, cy % value.shape[1], 1)
    return value


def edge_rows(odd, a_ref, b_ref, first):
    def edge(i, x):
        comps = UP if VELOCITY[i][2] == 1 else DOWN
        at = (x - first) * EDGES + comps.index(i)
        a = a_ref[at : at + 1, :]
        b = b_ref[at : at + 1, :]
        if VELOCITY[i][2] == 1:
            return jnp.where(odd, a, b)
        return jnp.where(odd, b, a)

    return edge


def heat_kernel(
    place_ref,
    posth_ref,
    recva_ref,
    recvb_ref,
    source_ref,
    edgea_ref,
    edgeb_ref,
    list_ref,
    metal_ref,
    heat_ref,
    out_ref,
):
    wide, deep, lanes = posth_ref.shape[1:]
    blocks = out_ref.shape[0]
    low, high = sides(place_ref[0] % 2 == 1, recva_ref, recvb_ref)
    get = planes(None, posth_ref, low, high, wide, source_ref)
    odd = place_ref[1] % 2 == 1
    edge = edge_rows(odd, edgea_ref, edgeb_ref, -1)
    tempers = []
    for x in range(-1, wide + 1):
        temper = None
        for k in range(HEATS):
            value = stream(get, edge, deep, FLOWS + k, x)
            heat_ref[k, x + 1] = value
            temper = value if temper is None else temper + value
        if 0 <= x < wide:
            tempers.append(temper)
    columns = wide * deep
    owner, cell, node = lists_of(list_ref[...])
    wall = look_up(
        jnp.concatenate(tempers, axis=0),
        hot(rows_of(node >> 7, columns)),
        rows_of(node & 127, lanes),
    )
    row_mask = rows_of(owner * 2 + (cell >> 7), 2 * blocks)
    sums = add_up(wall, row_mask, hot(rows_of(cell & 127, lanes)))
    at = (wide + 2) * EDGES
    a = edgea_ref[at : at + 2, :]
    b = edgeb_ref[at : at + 2, :]
    for d in range(blocks):
        out_ref[d, 0:2, :] = metal_ref[0:2]
        out_ref[d, 2:4, :] = jnp.where(odd, a, b)
        out_ref[d, 4:6, :] = jnp.where(odd, b, a)
        out_ref[d, 6:8, :] = sums[2 * d : 2 * d + 2]


def flow_kernel(
    place_ref,
    postf_ref,
    recva_ref,
    recvb_ref,
    edgea_ref,
    edgeb_ref,
    heat_ref,
    solid_ref,
    counts_ref,
    outf_ref,
    outh_ref,
    senda_ref,
    sendb_ref,
):
    wide, deep, lanes = postf_ref.shape[1:]
    low, high = sides(place_ref[0] % 2 == 1, recva_ref, recvb_ref)
    get = planes(postf_ref, None, low, high, wide, None)
    edge = edge_rows(place_ref[1] % 2 == 1, edgea_ref, edgeb_ref, -1)
    for x in range(-1, wide + 1):
        flow = [stream(get, edge, deep, i, x) for i in range(FLOWS)]
        if x < 0:
            solid, counts = low(SOLID) != 0, low(COUNTS)
        elif x >= wide:
            solid, counts = high(SOLID) != 0, high(COUNTS)
        else:
            solid, counts = solid_ref[x] != 0, counts_ref[x]
        post, speed = collide_flow(flow, solid)
        heat = [heat_ref[k, x + 1] for k in range(HEATS)]
        temper = heat[0]
        for k in range(1, HEATS):
            temper = temper + heat[k]
        posth = lose(collide_heat(heat, temper, speed, solid), counts, temper)
        for i in range(FLOWS):
            outf_ref[i, x + 1] = post[i]
        for k in range(HEATS):
            outh_ref[k, x + 1] = posth[k]

    def fill(up_ref, down_ref):
        for ref, comps, row in ((up_ref, UP, deep - 1), (down_ref, DOWN, 0)):
            for x in range(wide):
                for n, i in enumerate(comps):
                    at = x + 1 - VELOCITY[i][0]
                    value = outf_ref[i, at] if i < FLOWS else outh_ref[i - FLOWS, at]
                    where = x * EDGES + n
                    ref[where : where + 1, :] = value[row : row + 1, :]

    @pl.when(place_ref[1] % 2 == 1)
    def _():
        fill(sendb_ref, senda_ref)

    @pl.when(place_ref[1] % 2 == 0)
    def _():
        fill(senda_ref, sendb_ref)


def last_metal_kernel(
    place_ref,
    recva_ref,
    recvb_ref,
    list_ref,
    chunks_ref,
    edgea_ref,
    edgeb_ref,
    metal_ref,
    conduction_ref,
    source_ref,
    row_ref,
    out_ref,
):
    blocks = chunks_ref.shape[0]
    wide, deep, lanes = source_ref.shape
    wide = wide - 2
    low, high = sides(place_ref[0] % 2 == 1, recva_ref, recvb_ref)
    table = chunks_ref[...].reshape(blocks * 8, lanes)
    columns = wide * deep
    give_planes(
        table,
        [side_lists(low), lists_of(list_ref[...]), side_lists(high)],
        ((columns - deep, deep, 0), (0, columns, 1), (0, deep, wide + 1)),
        deep,
        source_ref,
    )
    odd = place_ref[1] % 2 == 1
    at = (wide + 2) * EDGES + 2
    a = edgea_ref[at : at + LIST_ROWS, :]
    b = edgeb_ref[at : at + LIST_ROWS, :]
    for n, (block, shift, z) in enumerate(
        ((jnp.where(odd, a, b), 2, deep - 1), (jnp.where(odd, b, a), 4, 0))
    ):
        lists = lists_of(block)
        node = lists[2]
        column = node >> 7
        row = jnp.where(lax.rem(column, deep) == z, lax.div(column, deep), -1)
        row_ref[wide * n : wide * (n + 1), :] = give(
            metal_at(table, lists, shift), row, node, wide
        )
    sums = chunks_ref[0]
    for d in range(1, blocks):
        sums = sums + chunks_ref[d]
    out_ref[...] = next_metal(conduction_ref[...], metal_ref[0:2], sums[6:8], metal_ref[2:4])


def final_kernel(
    place_ref, postf_ref, posth_ref, source_ref, row_ref, edgea_ref, edgeb_ref, flow_ref, heat_ref
):
    wide, deep, lanes = flow_ref.shape[1:]

    def get(i, x):
        if i < FLOWS:
            return postf_ref[i, x + 1]
        return posth_ref[i - FLOWS, x + 1] + WEIGHT_HEAT[i - FLOWS] * source_ref[x + 1]

    sent = edge_rows(place_ref[1] % 2 == 1, edgea_ref, edgeb_ref, 0)

    def edge(i, x):
        value = sent(i, x)
        if i < FLOWS:
            return value
        at = x if VELOCITY[i][2] == 1 else wide + x
        return value + WEIGHT_HEAT[i - FLOWS] * row_ref[at : at + 1, :]

    for x in range(wide):
        for i in range(FLOWS):
            flow_ref[i, x] = stream(get, edge, deep, i, x)
        for k in range(HEATS):
            heat_ref[k, x] = stream(get, edge, deep, FLOWS + k, x)


def swap(value, axis, offset):
    count = lax.axis_size(axis)
    pairs = []
    for first in range(offset, count + offset, 2):
        one, other = first % count, (first + 1) % count
        pairs += [(one, other), (other, one)]
    return lax.ppermute(value, axis, pairs)


def local(
    populations,
    thermal,
    solid_mask,
    metal_temp,
    conduction,
    wall_count,
    wall_node,
    wall_owner,
    wall_cell,
):
    blocks = lax.axis_size("blk")
    wide, deep, lanes = solid_mask.shape
    place = jnp.stack([lax.axis_index("blk"), lax.axis_index("span")]).astype(jnp.int32)
    smem = pl.BlockSpec(memory_space=pltpu.SMEM)

    def call(kernel, name, outs, scalars, *args):
        return pl.pallas_call(
            kernel,
            in_specs=[smem] + in_vmem(len(args)),
            out_specs=jax.tree.map(lambda _: in_vmem(1)[0], outs),
            out_shape=outs,
            compiler_params=params(),
            name=name,
        )(scalars, *args)

    def to_all(chunks):
        return lax.all_to_all(chunks, "blk", 0, 0, tiled=True)

    chunks, lists, counts = call(
        packet_kernel,
        "wall_packet",
        (shape(blocks, 8, lanes), shape(16, lanes), shape(wide, deep, lanes)),
        wall_count,
        thermal,
        metal_temp,
        wall_node,
        wall_owner.reshape(1, -1),
        wall_cell,
    )
    chunks = to_all(chunks)
    side = shape(SIDE_PLANES, deep, lanes)
    postf, posth, senda, sendb = call(
        collide_kernel,
        "collide_first",
        (shape(FLOWS, wide, deep, lanes), shape(HEATS, wide, deep, lanes), side, side),
        place,
        populations,
        thermal,
        solid_mask,
        counts,
        lists,
    )
    recva = swap(senda, "blk", 0)
    recvb = swap(sendb, "blk", 1)
    edge_count = -(-((wide + 2) * EDGES + 2 + LIST_ROWS) // 8) * 8
    edges = shape(edge_count, lanes)
    senda, sendb, metal, source = call(
        source_kernel,
        "source_first",
        (edges, edges, shape(8, lanes), shape(wide + 4, deep, lanes)),
        place,
        postf,
        posth,
        recva,
        recvb,
        lists,
        chunks,
        conduction,
    )
    edgea = swap(senda, "span", 0)
    edgeb = swap(sendb, "span", 1)
    heat, chunks = call(
        heat_kernel,
        "heat_second",
        (shape(HEATS, wide + 2, deep, lanes), shape(blocks, 8, lanes)),
        place,
        posth,
        recva,
        recvb,
        source,
        edgea,
        edgeb,
        lists,
        metal,
    )
    chunks = to_all(chunks)
    edges = shape(wide * EDGES, lanes)
    postf, posth, senda, sendb = call(
        flow_kernel,
        "collide_second",
        (
            shape(FLOWS, wide + 2, deep, lanes),
            shape(HEATS, wide + 2, deep, lanes),
            edges,
            edges,
        ),
        place,
        postf,
        recva,
        recvb,
        edgea,
        edgeb,
        heat,
        solid_mask,
        counts,
    )
    lasta = swap(senda, "span", 0)
    lastb = swap(sendb, "span", 1)
    source, rows, metal = call(
        last_metal_kernel,
        "source_second",
        (
            shape(wide + 2, deep, lanes),
            shape(2 * wide, lanes),
            shape(1, metal_temp.shape[1]),
        ),
        place,
        recva,
        recvb,
        lists,
        chunks,
        edgea,
        edgeb,
        metal,
        conduction,
    )
    flow, heat = call(
        final_kernel,
        "stream_last",
        (shape(FLOWS, wide, deep, lanes), shape(HEATS, wide, deep, lanes)),
        place,
        postf,
        posth,
        source,
        rows,
        lasta,
        lastb,
    )
    return (flow, heat, metal)


def solution(mesh):
    in_specs = (
        P(None, "blk", "span", None),
        P(None, "blk", "span", None),
        P("blk", "span", None),
        P("span", "blk"),
        P("span", "blk"),
        P("span", "blk"),
        P("span", "blk"),
        P("span", "blk", None),
        P("span", "blk"),
    )
    out_specs = (P(None, "blk", "span", None), P(None, "blk", "span", None), P("span", "blk"))
    return jax.shard_map(local, mesh=mesh, in_specs=in_specs, out_specs=out_specs, check_vma=False)
```

```python
import jax
import jax.numpy as jnp
from jax import lax
from jax.experimental import pallas as pl
from jax.experimental.pallas import tpu as pltpu
from jax.sharding import PartitionSpec as P

VELOCITY_FLOW = [
    (0, 0, 0),
    (1, 0, 0),
    (-1, 0, 0),
    (0, 1, 0),
    (0, -1, 0),
    (0, 0, 1),
    (0, 0, -1),
    (1, 1, 0),
    (-1, -1, 0),
    (1, -1, 0),
    (-1, 1, 0),
    (1, 0, 1),
    (-1, 0, -1),
    (1, 0, -1),
    (-1, 0, 1),
    (0, 1, 1),
    (0, -1, -1),
    (0, 1, -1),
    (0, -1, 1),
]
WEIGHT_FLOW = [1.0 / 3.0] + [1.0 / 18.0] * 6 + [1.0 / 36.0] * 12
OPPOSITE = [0, 2, 1, 4, 3, 6, 5, 8, 7, 10, 9, 12, 11, 14, 13, 16, 15, 18, 17]
WEIGHT_HEAT = [0.25] + [0.125] * 6
VELOCITY = VELOCITY_FLOW + VELOCITY_FLOW[:7]
FLOWS, HEATS = 19, 7
ALL = FLOWS + HEATS
RELAX_FLOW = 0.8
RELAX_HEAT = 0.9
WALL_COEFF = 0.5
METAL_GAIN = 0.5

FACE_RIGHT = [(i, 0) for i in range(ALL) if VELOCITY[i][0] >= 0] + [
    (i, 1) for i in range(ALL) if VELOCITY[i][0] == 1
]
FACE_LEFT = [(i, 0) for i in range(ALL) if VELOCITY[i][0] <= 0] + [
    (i, 1) for i in range(ALL) if VELOCITY[i][0] == -1
]
FACES = len(FACE_RIGHT)
UP = [i for i in range(ALL) if VELOCITY[i][2] == 1]
DOWN = [i for i in range(ALL) if VELOCITY[i][2] == -1]
EDGES = len(UP)

SOLID, COUNTS, LISTS = FACES, FACES + 1, FACES + 2
SIDE_PLANES = FACES + 4
LIST_ROWS = 12
LANES = 128
F32 = jnp.float32
BF16 = jnp.bfloat16


def params(mebibytes=32):
    return pltpu.CompilerParams(vmem_limit_bytes=mebibytes * 1024 * 1024)


def in_vmem(count):
    return [pl.BlockSpec(memory_space=pltpu.VMEM)] * count


def shape(*dims):
    return jax.ShapeDtypeStruct(dims, F32)


def split(value):
    high = value.astype(BF16)
    low = (value - high.astype(F32)).astype(BF16)
    return high, low


def split_three(value):
    high = value.astype(BF16)
    rest = value - high.astype(F32)
    middle = rest.astype(BF16)
    low = (rest - middle.astype(F32)).astype(BF16)
    return high, middle, low


def dot(left, right, dims):
    return lax.dot_general(left, right, (dims, ((), ())), preferred_element_type=F32)


def rows_of(row, count):
    return lax.broadcasted_iota(jnp.int32, (count, row.shape[1]), 0) == row


def hot(mask):
    return jnp.where(mask, 1.0, 0.0).astype(BF16)


def pick(rows, row_index, lane_index):
    found = jnp.zeros(lane_index.shape, F32)
    for r, row in enumerate(rows):
        whole = jnp.broadcast_to(row, lane_index.shape)
        value = jnp.take_along_axis(whole, lane_index, axis=1, mode="promise_in_bounds")
        found = jnp.where(row_index == r, value, found)
    return found


def pick_twice(rows, row_index, lane_index):
    first, second = (row_index, lane_index) if len(row_index) == 2 else (row_index * 2, lane_index * 2)
    found = pick(rows, jnp.concatenate(first, axis=0), jnp.concatenate(second, axis=0))
    return [found[4 * n : 4 * n + 4] for n in range(len(row_index))]


def add_up(values, row_mask, lane_hot):
    count = row_mask.shape[0]
    stacked = jnp.concatenate(
        [jnp.where(row_mask, part.astype(F32), 0.0) for part in split(values)], axis=0
    ).astype(BF16)
    sums = dot(stacked, lane_hot, ((1,), (1,)))
    return sums[:count] + sums[count:]


def one_row(block):
    return jnp.concatenate([block[r : r + 1] for r in range(block.shape[0])], axis=1)


def put_rows(ref, start, row):
    for r in range(row.shape[1] // LANES):
        ref[start + r : start + r + 1, :] = row[:, r * LANES : (r + 1) * LANES]


def lists_of(block):
    return [block[4 * n : 4 * n + 4].astype(jnp.int32) for n in range(3)]


def wall_temper(tempers, node):
    rows = [temper[z : z + 1] for temper in tempers for z in range(temper.shape[0])]
    return pick_twice(rows, [node >> 7], [node & 127])[0]


def pack(
    count_ref, heat_ref, metal_ref, node_ref, owner_ref, cell_ref, out_ref, list_ref, counts_ref
):
    blocks = out_ref.shape[0]
    wide, deep, lanes = heat_ref.shape[1:]
    tempers = []
    for x in range(wide):
        temper = heat_ref[0, x]
        for k in range(1, HEATS):
            temper = temper + heat_ref[k, x]
        tempers.append(temper)
    node = node_ref[...]
    cell = cell_ref[...]
    entries = node.shape[1]
    live = lax.broadcasted_iota(jnp.int32, (1, entries), 1) < count_ref[0, 0]
    owner = jnp.where(live, owner_ref[...], -1)
    list_ref[8:16, :] = jnp.zeros((8, lanes), F32)
    put_rows(list_ref, 0, owner.astype(F32))
    put_rows(list_ref, 4, cell.astype(F32))
    put_rows(list_ref, 8, node.astype(F32))
    put_rows(list_ref, LIST_ROWS, metal_ref[...])
    lane_mask = rows_of(node & 127, lanes)
    nodes = list_ref[8:12].astype(jnp.int32)
    wall = one_row(wall_temper(tempers, nodes))
    cell_hot = hot(rows_of(cell & 127, lanes))
    row_mask = rows_of(owner * 2 + (cell >> 7), 2 * blocks)
    sums = add_up(wall, row_mask, cell_hot)
    counts = dot(hot(row_mask), cell_hot, ((1,), (1,)))
    for d in range(blocks):
        put_rows(out_ref.at[d], 0, metal_ref[...])
        out_ref[d, 2:4, :] = sums[2 * d : 2 * d + 2]
        out_ref[d, 4:6, :] = counts[2 * d : 2 * d + 2]
        out_ref[d, 6:8, :] = jnp.zeros((2, lanes), F32)
    at_nodes = dot(
        hot(rows_of(jnp.where(live, node >> 7, -1), wide * deep)), hot(lane_mask), ((1,), (1,))
    )
    counts_ref[...] = at_nodes.reshape(wide, deep, lanes)


def collide_flow(flow, solid):
    density = flow[0]
    for i in range(1, FLOWS):
        density = density + flow[i]
    inverse = 1.0 / density
    speed = []
    for axis in range(3):
        ahead = [flow[i] for i in range(FLOWS) if VELOCITY[i][axis] == 1]
        behind = [flow[i] for i in range(FLOWS) if VELOCITY[i][axis] == -1]
        speed.append((sum(ahead[1:], ahead[0]) - sum(behind[1:], behind[0])) * inverse)
    base = 1.0 - 1.5 * (speed[0] * speed[0] + speed[1] * speed[1] + speed[2] * speed[2])
    scaled = {w: density * (w / RELAX_FLOW) for w in sorted(set(WEIGHT_FLOW))}
    keep = 1.0 - 1.0 / RELAX_FLOW
    post = [None] * FLOWS
    rest = scaled[WEIGHT_FLOW[0]] * base + keep * flow[0]
    post[0] = jnp.where(solid, flow[0], rest)
    for i in range(1, FLOWS, 2):
        along = None
        for axis in range(3):
            c = VELOCITY[i][axis]
            if c == 0:
                continue
            term = speed[axis]
            if along is None:
                along = term if c == 1 else -term
            else:
                along = along + term if c == 1 else along - term
        weight = scaled[WEIGHT_FLOW[i]]
        even = weight * (base + 4.5 * along * along)
        odd = weight * (3.0 * along)
        j = OPPOSITE[i]
        post[i] = jnp.where(solid, flow[j], even + odd + keep * flow[i])
        post[j] = jnp.where(solid, flow[i], even - odd + keep * flow[j])
    return post, speed


def collide_heat(heat, temper, speed, solid):
    keep = 1.0 - 1.0 / RELAX_HEAT
    post = [None] * HEATS
    post[0] = jnp.where(
        solid, heat[0], temper * (WEIGHT_HEAT[0] / RELAX_HEAT) + keep * heat[0]
    )
    scaled = temper * (WEIGHT_HEAT[1] / RELAX_HEAT)
    for axis in range(3):
        i = 2 * axis + 1
        j = i + 1
        odd = scaled * (4.0 * speed[axis])
        post[i] = jnp.where(solid, heat[j], scaled + odd + keep * heat[i])
        post[j] = jnp.where(solid, heat[i], scaled - odd + keep * heat[j])
    return post


def lose(post, counts, temper):
    lost = counts * temper * -WALL_COEFF
    return [post[k] + WEIGHT_HEAT[k] * lost for k in range(HEATS)]


STRIPS = 4


def first_kernel(
    place_ref,
    count_ref,
    flow_hbm,
    heat_hbm,
    solid_hbm,
    metal_hbm,
    node_hbm,
    owner_hbm,
    cell_hbm,
    chunks_ref,
    list_ref,
    counts_ref,
    solid_ref,
    postf_ref,
    posth_ref,
    senda_ref,
    sendb_ref,
    flow_ref,
    heat_ref,
    mask_ref,
    metal_ref,
    node_ref,
    owner_ref,
    cell_ref,
    sems,
):
    wide = flow_ref.shape[1]
    strip = wide // STRIPS
    odd = place_ref[0] % 2 == 1
    small = [
        pltpu.make_async_copy(source, target, sems.at[n])
        for n, (source, target) in enumerate(
            (
                (heat_hbm, heat_ref),
                (node_hbm, node_ref),
                (owner_hbm, owner_ref),
                (cell_hbm, cell_ref),
                (metal_hbm, metal_ref),
                (solid_hbm, mask_ref),
            )
        )
    ]
    strips = [
        pltpu.make_async_copy(
            flow_hbm.at[:, pl.ds(n * strip, strip)],
            flow_ref.at[:, pl.ds(n * strip, strip)],
            sems.at[len(small) + n],
        )
        for n in range(STRIPS)
    ]
    for copy in small + strips:
        copy.start()
    for copy in small:
        copy.wait()
    pack(
        count_ref,
        heat_ref,
        metal_ref,
        node_ref,
        owner_ref,
        cell_ref,
        chunks_ref,
        list_ref,
        counts_ref,
    )
    solid_ref[...] = mask_ref[...].astype(F32)
    for x in range(wide):
        if x % strip == 0:
            strips[x // strip].wait()
        flow = [flow_ref[i, x] for i in range(FLOWS)]
        heat = [heat_ref[k, x] for k in range(HEATS)]
        solid = mask_ref[x] != 0
        temper = heat[0]
        for k in range(1, HEATS):
            temper = temper + heat[k]
        post, speed = collide_flow(flow, solid)
        posth = lose(collide_heat(heat, temper, speed, solid), counts_ref[x], temper)
        for i in range(FLOWS):
            postf_ref[i, x] = post[i]
        for k in range(HEATS):
            posth_ref[k, x] = posth[k]

    def plane(i, x):
        return postf_ref[i, x] if i < FLOWS else posth_ref[i - FLOWS, x]

    def fill(right_ref, left_ref):
        for ref, faces, edge in ((right_ref, FACE_RIGHT, wide - 1), (left_ref, FACE_LEFT, 0)):
            for n, (i, depth) in enumerate(faces):
                ref[n] = plane(i, abs(edge - depth))
            ref[SOLID] = solid_ref[edge]
            ref[COUNTS] = counts_ref[edge]
            ref[LISTS] = list_ref[0:8]
            ref[LISTS + 1] = list_ref[8:16]

    @pl.when(odd)
    def _():
        fill(sendb_ref, senda_ref)

    @pl.when(jnp.logical_not(odd))
    def _():
        fill(senda_ref, sendb_ref)


def sides(odd, a_ref, b_ref):
    def low(n):
        return jnp.where(odd, a_ref[n], b_ref[n])

    def high(n):
        return jnp.where(odd, b_ref[n], a_ref[n])

    return low, high


def side_lists(get):
    return lists_of(jnp.concatenate([get(LISTS), get(LISTS + 1)], axis=0))


def planes(postf_ref, posth_ref, low, high, wide, source_ref):
    def get(i, x):
        if x < 0:
            value = low(FACE_RIGHT.index((i, -1 - x)))
        elif x >= wide:
            value = high(FACE_LEFT.index((i, x - wide)))
        elif i < FLOWS:
            value = postf_ref[i, x]
        else:
            value = posth_ref[i - FLOWS, x]
        if i >= FLOWS and source_ref is not None:
            value = value + WEIGHT_HEAT[i - FLOWS] * source_ref[x + 2]
        return value

    return get


def metal_rows(chunks_ref, shift):
    blocks = chunks_ref.shape[0]
    return [chunks_ref[d, shift + h : shift + h + 1] for d in range(blocks) for h in range(2)]


def metal_at(rows, *lists):
    return pick_twice(
        rows,
        [owner * 2 + (cell >> 7) for owner, cell, node in lists],
        [cell & 127 for owner, cell, node in lists],
    )


def give(metal, row, node, count):
    return add_up(
        WALL_COEFF * one_row(metal),
        rows_of(one_row(row), count),
        hot(rows_of(one_row(node) & 127, LANES)),
    )


def give_planes(metal, node, first, planes, deep):
    count = planes * deep
    return give(metal, (node >> 7) - first * deep, node, count).reshape(planes, deep, LANES)


def conduct(conduction, halves):
    vector = jnp.concatenate(halves, axis=1)
    parts = split_three(vector)
    rows = lax.broadcasted_iota(jnp.int32, (16, vector.shape[1]), 0)
    stacked = jnp.zeros((16, vector.shape[1]), F32)
    for r, part in enumerate(parts):
        stacked = jnp.where(rows == r, part.astype(F32), stacked)
    stacked = stacked.astype(BF16)
    out = sum([dot(stacked, part, ((1,), (1,))) for part in split_three(conduction)])
    return out[0:1] + out[1:2] + out[2:3]


def next_metal(conduction, metal, total, count):
    gained = WALL_COEFF * (total - count * metal)
    value = metal + METAL_GAIN * gained
    return conduct(conduction, [value[0:1], value[1:2]])


def metal_kernel(list_ref, chunks_ref, conduction_ref, metal_ref, source_ref):
    blocks = chunks_ref.shape[0]
    wide, deep, lanes = source_ref.shape
    lists = lists_of(list_ref[...])
    found = metal_at(metal_rows(chunks_ref, 0), lists)[0]
    source_ref[...] = give_planes(found, lists[2], 0, wide, deep)
    sums = chunks_ref[0]
    for d in range(1, blocks):
        sums = sums + chunks_ref[d]
    count = sums[4:6]
    metal = next_metal(conduction_ref[...], list_ref[LIST_ROWS : LIST_ROWS + 2], sums[2:4], count)
    metal_ref[...] = jnp.zeros(metal_ref.shape, F32)
    put_rows(metal_ref, 0, metal)
    metal_ref[2:4, :] = count


def source_kernel(
    place_ref,
    postf_ref,
    posth_ref,
    recva_ref,
    recvb_ref,
    list_ref,
    chunks_ref,
    metal_ref,
    own_ref,
    senda_ref,
    sendb_ref,
    source_ref,
):
    wide, deep, lanes = postf_ref.shape[1:]
    low, high = sides(place_ref[0] % 2 == 1, recva_ref, recvb_ref)
    before, after = side_lists(low), side_lists(high)
    found = metal_at(metal_rows(chunks_ref, 0), before, after)
    source_ref[0:2] = give_planes(found[0], before[2], wide - 2, 2, deep)
    source_ref[2 : wide + 2] = own_ref[...]
    source_ref[wide + 2 :] = give_planes(found[1], after[2], 0, 2, deep)
    get = planes(postf_ref, posth_ref, low, high, wide, source_ref)

    def fill(up_ref, down_ref):
        for ref, comps, row in ((up_ref, UP, deep - 1), (down_ref, DOWN, 0)):
            for j in range(wide + 2):
                for n, i in enumerate(comps):
                    value = get(i, j - 1 - VELOCITY[i][0])
                    at = j * EDGES + n
                    ref[at : at + 1, :] = value[row : row + 1, :]
            at = (wide + 2) * EDGES
            ref[at : at + 2, :] = metal_ref[0:2]
            ref[at + 2 : at + 2 + LIST_ROWS, :] = list_ref[0:LIST_ROWS]

    for ref in (senda_ref, sendb_ref):
        ref[ref.shape[0] - 8 :, :] = jnp.zeros((8, lanes), F32)

    @pl.when(place_ref[1] % 2 == 1)
    def _():
        fill(sendb_ref, senda_ref)

    @pl.when(place_ref[1] % 2 == 0)
    def _():
        fill(senda_ref, sendb_ref)


def stream(get, edge, deep, i, x):
    cx, cy, cz = VELOCITY[i]
    value = get(i, x - cx)
    if cz != 0:
        rows = lax.broadcasted_iota(jnp.int32, value.shape, 0)
        if cz == 1:
            value = jnp.where(rows == 0, edge(i, x), pltpu.roll(value, 1, 0))
        else:
            value = jnp.where(rows == deep - 1, edge(i, x), pltpu.roll(value, deep - 1, 0))
    if cy != 0:
        value = pltpu.roll(value, cy % value.shape[1], 1)
    return value


def edge_rows(odd, a_ref, b_ref, first):
    def edge(i, x):
        comps = UP if VELOCITY[i][2] == 1 else DOWN
        at = (x - first) * EDGES + comps.index(i)
        a = a_ref[at : at + 1, :]
        b = b_ref[at : at + 1, :]
        if VELOCITY[i][2] == 1:
            return jnp.where(odd, a, b)
        return jnp.where(odd, b, a)

    return edge


def heat_kernel(
    place_ref,
    posth_ref,
    recva_ref,
    recvb_ref,
    source_ref,
    edgea_ref,
    edgeb_ref,
    list_ref,
    metal_ref,
    heat_ref,
    out_ref,
):
    wide, deep, lanes = posth_ref.shape[1:]
    blocks = out_ref.shape[0]
    low, high = sides(place_ref[0] % 2 == 1, recva_ref, recvb_ref)
    get = planes(None, posth_ref, low, high, wide, source_ref)
    odd = place_ref[1] % 2 == 1
    edge = edge_rows(odd, edgea_ref, edgeb_ref, -1)
    tempers = []
    for x in range(-1, wide + 1):
        temper = None
        for k in range(HEATS):
            value = stream(get, edge, deep, FLOWS + k, x)
            heat_ref[k, x + 1] = value
            temper = value if temper is None else temper + value
        if 0 <= x < wide:
            tempers.append(temper)
    owner, cell, node = lists_of(list_ref[...])
    wall = one_row(wall_temper(tempers, node))
    owner, cell = one_row(owner), one_row(cell)
    row_mask = rows_of(owner * 2 + (cell >> 7), 2 * blocks)
    sums = add_up(wall, row_mask, hot(rows_of(cell & 127, lanes)))
    at = (wide + 2) * EDGES
    a = edgea_ref[at : at + 2, :]
    b = edgeb_ref[at : at + 2, :]
    for d in range(blocks):
        out_ref[d, 0:2, :] = metal_ref[0:2]
        out_ref[d, 2:4, :] = jnp.where(odd, a, b)
        out_ref[d, 4:6, :] = jnp.where(odd, b, a)
        out_ref[d, 6:8, :] = sums[2 * d : 2 * d + 2]


def flow_kernel(
    place_ref,
    postf_ref,
    recva_ref,
    recvb_ref,
    edgea_ref,
    edgeb_ref,
    heat_ref,
    solid_ref,
    counts_ref,
    outf_ref,
    outh_ref,
    senda_ref,
    sendb_ref,
):
    wide, deep, lanes = postf_ref.shape[1:]
    low, high = sides(place_ref[0] % 2 == 1, recva_ref, recvb_ref)
    get = planes(postf_ref, None, low, high, wide, None)
    edge = edge_rows(place_ref[1] % 2 == 1, edgea_ref, edgeb_ref, -1)
    for x in range(-1, wide + 1):
        flow = [stream(get, edge, deep, i, x) for i in range(FLOWS)]
        if x < 0:
            solid, counts = low(SOLID) != 0, low(COUNTS)
        elif x >= wide:
            solid, counts = high(SOLID) != 0, high(COUNTS)
        else:
            solid, counts = solid_ref[x] != 0, counts_ref[x]
        post, speed = collide_flow(flow, solid)
        heat = [heat_ref[k, x + 1] for k in range(HEATS)]
        temper = heat[0]
        for k in range(1, HEATS):
            temper = temper + heat[k]
        posth = lose(collide_heat(heat, temper, speed, solid), counts, temper)
        for i in range(FLOWS):
            outf_ref[i, x + 1] = post[i]
        for k in range(HEATS):
            outh_ref[k, x + 1] = posth[k]

    def fill(up_ref, down_ref):
        for ref, comps, row in ((up_ref, UP, deep - 1), (down_ref, DOWN, 0)):
            for x in range(wide):
                for n, i in enumerate(comps):
                    at = x + 1 - VELOCITY[i][0]
                    value = outf_ref[i, at] if i < FLOWS else outh_ref[i - FLOWS, at]
                    where = x * EDGES + n
                    ref[where : where + 1, :] = value[row : row + 1, :]

    @pl.when(place_ref[1] % 2 == 1)
    def _():
        fill(sendb_ref, senda_ref)

    @pl.when(place_ref[1] % 2 == 0)
    def _():
        fill(senda_ref, sendb_ref)


def last_metal_kernel(
    place_ref,
    recva_ref,
    recvb_ref,
    list_ref,
    chunks_ref,
    edgea_ref,
    edgeb_ref,
    metal_ref,
    conduction_ref,
    source_ref,
    row_ref,
    out_ref,
):
    blocks = chunks_ref.shape[0]
    wide, deep, lanes = source_ref.shape
    wide = wide - 2
    low, high = sides(place_ref[0] % 2 == 1, recva_ref, recvb_ref)
    own, before, after = lists_of(list_ref[...]), side_lists(low), side_lists(high)
    found = metal_at(metal_rows(chunks_ref, 0), own)[0]
    source_ref[1 : wide + 1] = give_planes(found, own[2], 0, wide, deep)
    found = metal_at(metal_rows(chunks_ref, 0), before, after)
    source_ref[0:1] = give_planes(found[0], before[2], wide - 1, 1, deep)
    source_ref[wide + 1 :] = give_planes(found[1], after[2], 0, 1, deep)
    odd = place_ref[1] % 2 == 1
    at = (wide + 2) * EDGES + 2
    a = edgea_ref[at : at + LIST_ROWS, :]
    b = edgeb_ref[at : at + LIST_ROWS, :]
    for n, (block, shift, z) in enumerate(
        ((jnp.where(odd, a, b), 2, deep - 1), (jnp.where(odd, b, a), 4, 0))
    ):
        lists = lists_of(block)
        node = lists[2]
        column = node >> 7
        row = jnp.where(lax.rem(column, deep) == z, lax.div(column, deep), -1)
        found = metal_at(metal_rows(chunks_ref, shift), lists)[0]
        row_ref[wide * n : wide * (n + 1), :] = give(found, row, node, wide)
    sums = chunks_ref[0]
    for d in range(1, blocks):
        sums = sums + chunks_ref[d]
    out_ref[...] = next_metal(conduction_ref[...], metal_ref[0:2], sums[6:8], metal_ref[2:4])


def final_kernel(
    place_ref,
    postf_ref,
    posth_ref,
    source_ref,
    row_ref,
    metal_ref,
    edgea_ref,
    edgeb_ref,
    flow_hbm,
    heat_hbm,
    metal_hbm,
    flow_ref,
    heat_ref,
    sems,
):
    wide, deep, lanes = flow_ref.shape[1:]
    strip = wide // STRIPS

    def get(i, x):
        if i < FLOWS:
            return postf_ref[i, x + 1]
        return posth_ref[i - FLOWS, x + 1] + WEIGHT_HEAT[i - FLOWS] * source_ref[x + 1]

    sent = edge_rows(place_ref[1] % 2 == 1, edgea_ref, edgeb_ref, 0)

    def edge(i, x):
        value = sent(i, x)
        if i < FLOWS:
            return value
        at = x if VELOCITY[i][2] == 1 else wide + x
        return value + WEIGHT_HEAT[i - FLOWS] * row_ref[at : at + 1, :]

    copies = [pltpu.make_async_copy(metal_ref, metal_hbm, sems.at[2 * STRIPS])]
    copies[0].start()
    for n in range(STRIPS):
        for x in range(n * strip, (n + 1) * strip):
            for i in range(FLOWS):
                flow_ref[i, x] = stream(get, edge, deep, i, x)
            for k in range(HEATS):
                heat_ref[k, x] = stream(get, edge, deep, FLOWS + k, x)
        part = pl.ds(n * strip, strip)
        for m, (source, target) in enumerate(((flow_ref, flow_hbm), (heat_ref, heat_hbm))):
            copy = pltpu.make_async_copy(
                source.at[:, part], target.at[:, part], sems.at[2 * n + m]
            )
            copy.start()
            copies.append(copy)
    for copy in copies:
        copy.wait()


def swap(value, axis, offset):
    count = lax.axis_size(axis)
    pairs = []
    for first in range(offset, count + offset, 2):
        one, other = first % count, (first + 1) % count
        pairs += [(one, other), (other, one)]
    return lax.ppermute(value, axis, pairs)


def local(
    populations,
    thermal,
    solid_mask,
    metal_temp,
    conduction,
    wall_count,
    wall_node,
    wall_owner,
    wall_cell,
):
    blocks = lax.axis_size("blk")
    wide, deep, lanes = solid_mask.shape
    place = jnp.stack([lax.axis_index("blk"), lax.axis_index("span")]).astype(jnp.int32)
    smem = pl.BlockSpec(memory_space=pltpu.SMEM)
    hbm = pl.BlockSpec(memory_space=pltpu.HBM)

    def call(kernel, name, outs, scalars, *args, far=0, scratch=(), out_spec=None):
        near = len(args) - far
        held = [pltpu.with_memory_space_constraint(arg, pltpu.HBM) for arg in args[near:]]
        out_spec = out_spec or in_vmem(1)[0]
        return pl.pallas_call(
            kernel,
            in_specs=[smem] * len(scalars) + in_vmem(near) + [hbm] * far,
            out_specs=jax.tree.map(lambda _: out_spec, outs),
            out_shape=outs,
            scratch_shapes=scratch,
            compiler_params=params(),
            name=name,
        )(*scalars, *args[:near], *held)

    def to_all(chunks):
        return lax.all_to_all(chunks, "blk", 0, 0, tiled=True)

    side = shape(SIDE_PLANES, deep, lanes)
    field = shape(wide, deep, lanes)
    flows, heats = shape(FLOWS, wide, deep, lanes), shape(HEATS, wide, deep, lanes)
    chunks, lists, counts, solid, postf, posth, senda, sendb = call(
        first_kernel,
        "collide_first",
        (shape(blocks, 8, lanes), shape(16, lanes), field, field, flows, heats, side, side),
        (place, wall_count),
        populations,
        thermal,
        solid_mask,
        metal_temp,
        wall_node,
        wall_owner.reshape(1, -1),
        wall_cell,
        far=7,
        scratch=[
            pltpu.VMEM(flows.shape, F32),
            pltpu.VMEM(heats.shape, F32),
            pltpu.VMEM(field.shape, jnp.int32),
            pltpu.VMEM(metal_temp.shape, F32),
            pltpu.VMEM(wall_node.shape, jnp.int32),
            pltpu.VMEM(wall_node.shape, jnp.int32),
            pltpu.VMEM(wall_node.shape, jnp.int32),
            pltpu.SemaphoreType.DMA((6 + STRIPS,)),
        ],
    )
    chunks = to_all(chunks)
    recva = swap(senda, "blk", 0)
    recvb = swap(sendb, "blk", 1)
    edge_count = -(-((wide + 2) * EDGES + 2 + LIST_ROWS) // 8) * 8
    edges = shape(edge_count, lanes)
    metal, own = call(
        metal_kernel,
        "metal_first",
        (shape(8, lanes), shape(wide, deep, lanes)),
        (),
        lists,
        chunks,
        conduction,
    )
    senda, sendb, source = call(
        source_kernel,
        "source_first",
        (edges, edges, shape(wide + 4, deep, lanes)),
        (place,),
        postf,
        posth,
        recva,
        recvb,
        lists,
        chunks,
        metal,
        own,
    )
    edgea = swap(senda, "span", 0)
    edgeb = swap(sendb, "span", 1)
    heat, chunks = call(
        heat_kernel,
        "heat_second",
        (shape(HEATS, wide + 2, deep, lanes), shape(blocks, 8, lanes)),
        (place,),
        posth,
        recva,
        recvb,
        source,
        edgea,
        edgeb,
        lists,
        metal,
    )
    chunks = to_all(chunks)
    edges = shape(wide * EDGES, lanes)
    postf, posth, senda, sendb = call(
        flow_kernel,
        "collide_second",
        (
            shape(FLOWS, wide + 2, deep, lanes),
            shape(HEATS, wide + 2, deep, lanes),
            edges,
            edges,
        ),
        (place,),
        postf,
        recva,
        recvb,
        edgea,
        edgeb,
        heat,
        solid,
        counts,
    )
    lasta = swap(senda, "span", 0)
    lastb = swap(sendb, "span", 1)
    source, rows, metal = call(
        last_metal_kernel,
        "source_second",
        (
            shape(wide + 2, deep, lanes),
            shape(2 * wide, lanes),
            shape(1, metal_temp.shape[1]),
        ),
        (place,),
        recva,
        recvb,
        lists,
        chunks,
        edgea,
        edgeb,
        metal,
        conduction,
    )
    return call(
        final_kernel,
        "stream_last",
        (flows, heats, shape(*metal_temp.shape)),
        (place,),
        postf,
        posth,
        source,
        rows,
        metal,
        lasta,
        lastb,
        scratch=[
            pltpu.VMEM(flows.shape, F32),
            pltpu.VMEM(heats.shape, F32),
            pltpu.SemaphoreType.DMA((2 * STRIPS + 1,)),
        ],
        out_spec=hbm,
    )


def solution(mesh):
    in_specs = (
        P(None, "blk", "span", None),
        P(None, "blk", "span", None),
        P("blk", "span", None),
        P("span", "blk"),
        P("span", "blk"),
        P("span", "blk"),
        P("span", "blk"),
        P("span", "blk", None),
        P("span", "blk"),
    )
    out_specs = (P(None, "blk", "span", None), P(None, "blk", "span", None), P("span", "blk"))
    return jax.shard_map(local, mesh=mesh, in_specs=in_specs, out_specs=out_specs, check_vma=False)
```

```python
import jax
import jax.numpy as jnp
from jax import lax
from jax.experimental import pallas as pl
from jax.experimental.pallas import tpu as pltpu
from jax.sharding import PartitionSpec as P

VELOCITY_FLOW = [
    (0, 0, 0),
    (1, 0, 0),
    (-1, 0, 0),
    (0, 1, 0),
    (0, -1, 0),
    (0, 0, 1),
    (0, 0, -1),
    (1, 1, 0),
    (-1, -1, 0),
    (1, -1, 0),
    (-1, 1, 0),
    (1, 0, 1),
    (-1, 0, -1),
    (1, 0, -1),
    (-1, 0, 1),
    (0, 1, 1),
    (0, -1, -1),
    (0, 1, -1),
    (0, -1, 1),
]
WEIGHT_FLOW = [1.0 / 3.0] + [1.0 / 18.0] * 6 + [1.0 / 36.0] * 12
OPPOSITE = [0, 2, 1, 4, 3, 6, 5, 8, 7, 10, 9, 12, 11, 14, 13, 16, 15, 18, 17]
WEIGHT_HEAT = [0.25] + [0.125] * 6
VELOCITY = VELOCITY_FLOW + VELOCITY_FLOW[:7]
FLOWS, HEATS = 19, 7
ALL = FLOWS + HEATS
RELAX_FLOW = 0.8
RELAX_HEAT = 0.9
WALL_COEFF = 0.5
METAL_GAIN = 0.5

FACE_RIGHT = [(i, 0) for i in range(ALL) if VELOCITY[i][0] >= 0] + [
    (i, 1) for i in range(ALL) if VELOCITY[i][0] == 1
]
FACE_LEFT = [(i, 0) for i in range(ALL) if VELOCITY[i][0] <= 0] + [
    (i, 1) for i in range(ALL) if VELOCITY[i][0] == -1
]
FACES = len(FACE_RIGHT)
UP = [i for i in range(ALL) if VELOCITY[i][2] == 1]
DOWN = [i for i in range(ALL) if VELOCITY[i][2] == -1]
EDGES = len(UP)
SOLID, COUNTS, LISTS = FACES, FACES + 1, FACES + 2
SIDE_PLANES = FACES + 4
LIST_ROWS = 12
LANES = 128
F32 = jnp.float32
BF16 = jnp.bfloat16


def params(mebibytes=32):
    return pltpu.CompilerParams(vmem_limit_bytes=mebibytes * 1024 * 1024)


def in_vmem(count):
    return [pl.BlockSpec(memory_space=pltpu.VMEM)] * count


def shape(*dims):
    return jax.ShapeDtypeStruct(dims, F32)


def split(value):
    high = value.astype(BF16)
    low = (value - high.astype(F32)).astype(BF16)
    return high, low


def split_three(value):
    high = value.astype(BF16)
    rest = value - high.astype(F32)
    middle = rest.astype(BF16)
    low = (rest - middle.astype(F32)).astype(BF16)
    return high, middle, low


def dot(left, right, dims):
    return lax.dot_general(left, right, (dims, ((), ())), preferred_element_type=F32)


def rows_of(row, count):
    return lax.broadcasted_iota(jnp.int32, (count, row.shape[1]), 0) == row


def hot(mask):
    return jnp.where(mask, 1.0, 0.0).astype(BF16)


def pick(rows, row_index, lane_index):
    found = jnp.zeros(lane_index.shape, F32)
    for r, row in enumerate(rows):
        whole = jnp.broadcast_to(row, lane_index.shape)
        value = jnp.take_along_axis(whole, lane_index, axis=1, mode="promise_in_bounds")
        found = jnp.where(row_index == r, value, found)
    return found


def pick_twice(rows, row_index, lane_index):
    first, second = (row_index, lane_index) if len(row_index) == 2 else (row_index * 2, lane_index * 2)
    found = pick(rows, jnp.concatenate(first, axis=0), jnp.concatenate(second, axis=0))
    return [found[4 * n : 4 * n + 4] for n in range(len(row_index))]


def add_up(values, row_mask, lane_hot):
    count = row_mask.shape[0]
    stacked = jnp.concatenate(
        [jnp.where(row_mask, part.astype(F32), 0.0) for part in split(values)], axis=0
    ).astype(BF16)
    sums = dot(stacked, lane_hot, ((1,), (1,)))
    return sums[:count] + sums[count:]


def one_row(block):
    return jnp.concatenate([block[r : r + 1] for r in range(block.shape[0])], axis=1)


def put_rows(ref, start, row):
    for r in range(row.shape[1] // LANES):
        ref[start + r : start + r + 1, :] = row[:, r * LANES : (r + 1) * LANES]


def lists_of(block):
    return [block[4 * n : 4 * n + 4].astype(jnp.int32) for n in range(3)]


def wall_temper(tempers, node):
    rows = [temper[z : z + 1] for temper in tempers for z in range(temper.shape[0])]
    return pick_twice(rows, [node >> 7], [node & 127])[0]


def pack(
    count_ref, heat_ref, metal_ref, node_ref, owner_ref, cell_ref, out_ref, list_ref, counts_ref
):
    blocks = out_ref.shape[0]
    wide, deep, lanes = heat_ref.shape[1:]
    tempers = []
    for x in range(wide):
        temper = heat_ref[0, x]
        for k in range(1, HEATS):
            temper = temper + heat_ref[k, x]
        tempers.append(temper)
    node = node_ref[...]
    cell = cell_ref[...]
    entries = node.shape[1]
    live = lax.broadcasted_iota(jnp.int32, (1, entries), 1) < count_ref[0, 0]
    owner = jnp.where(live, owner_ref[...], -1)
    list_ref[8:16, :] = jnp.zeros((8, lanes), F32)
    put_rows(list_ref, 0, owner.astype(F32))
    put_rows(list_ref, 4, cell.astype(F32))
    put_rows(list_ref, 8, node.astype(F32))
    put_rows(list_ref, LIST_ROWS, metal_ref[...])
    lane_mask = rows_of(node & 127, lanes)
    nodes = list_ref[8:12].astype(jnp.int32)
    wall = one_row(wall_temper(tempers, nodes))
    cell_hot = hot(rows_of(cell & 127, lanes))
    row_mask = rows_of(owner * 2 + (cell >> 7), 2 * blocks)
    sums = add_up(wall, row_mask, cell_hot)
    counts = dot(hot(row_mask), cell_hot, ((1,), (1,)))
    for d in range(blocks):
        put_rows(out_ref.at[d], 0, metal_ref[...])
        out_ref[d, 2:4, :] = sums[2 * d : 2 * d + 2]
        out_ref[d, 4:6, :] = counts[2 * d : 2 * d + 2]
        out_ref[d, 6:8, :] = jnp.zeros((2, lanes), F32)
    at_nodes = dot(
        hot(rows_of(jnp.where(live, node >> 7, -1), wide * deep)), hot(lane_mask), ((1,), (1,))
    )
    counts_ref[...] = at_nodes.reshape(wide, deep, lanes)


def tree(values):
    while len(values) > 1:
        values = [sum(values[n : n + 2][1:], values[n]) for n in range(0, len(values), 2)]
    return values[0]


def collide_flow(flow, solid):
    pairs = range(1, FLOWS, 2)
    gap = {i: flow[i] - flow[i + 1] for i in pairs}
    density = tree([flow[0]] + [flow[i] + flow[i + 1] for i in pairs])
    inverse = 1.0 / density
    speed = []
    for axis in range(3):
        terms = [
            gap[i] if VELOCITY[i][axis] == 1 else -gap[i] for i in pairs if VELOCITY[i][axis] != 0
        ]
        speed.append(tree(terms) * inverse)
    base = 1.0 - 1.5 * (speed[0] * speed[0] + speed[1] * speed[1] + speed[2] * speed[2])
    scaled = {w: density * (w / RELAX_FLOW) for w in sorted(set(WEIGHT_FLOW))}
    keep = 1.0 - 1.0 / RELAX_FLOW
    post = [None] * FLOWS
    rest = scaled[WEIGHT_FLOW[0]] * base + keep * flow[0]
    post[0] = jnp.where(solid, flow[0], rest)
    for i in pairs:
        along = None
        for axis in range(3):
            c = VELOCITY[i][axis]
            if c == 0:
                continue
            term = speed[axis]
            if along is None:
                along = term if c == 1 else -term
            else:
                along = along + term if c == 1 else along - term
        weight = scaled[WEIGHT_FLOW[i]]
        even = weight * (base + 4.5 * along * along)
        odd = weight * (3.0 * along)
        j = OPPOSITE[i]
        post[i] = jnp.where(solid, flow[j], even + odd + keep * flow[i])
        post[j] = jnp.where(solid, flow[i], even - odd + keep * flow[j])
    return post, speed


def collide_heat(heat, temper, speed, solid):
    keep = 1.0 - 1.0 / RELAX_HEAT
    post = [None] * HEATS
    post[0] = jnp.where(
        solid, heat[0], temper * (WEIGHT_HEAT[0] / RELAX_HEAT) + keep * heat[0]
    )
    scaled = temper * (WEIGHT_HEAT[1] / RELAX_HEAT)
    for axis in range(3):
        i = 2 * axis + 1
        j = i + 1
        odd = scaled * (4.0 * speed[axis])
        post[i] = jnp.where(solid, heat[j], scaled + odd + keep * heat[i])
        post[j] = jnp.where(solid, heat[i], scaled - odd + keep * heat[j])
    return post


def lose(post, counts, temper):
    lost = counts * temper * -WALL_COEFF
    return [post[k] + WEIGHT_HEAT[k] * lost for k in range(HEATS)]


STRIPS = 4


def first_kernel(
    count_ref,
    flow_hbm,
    heat_hbm,
    solid_hbm,
    metal_hbm,
    node_hbm,
    owner_hbm,
    cell_hbm,
    chunks_ref,
    list_ref,
    counts_ref,
    solid_ref,
    postf_ref,
    posth_ref,
    senda_ref,
    sendb_ref,
    flow_ref,
    heat_ref,
    mask_ref,
    metal_ref,
    node_ref,
    owner_ref,
    cell_ref,
    sems,
):
    wide = flow_ref.shape[1]
    strip = wide // STRIPS
    odd = lax.axis_index("blk") % 2 == 1
    small = [
        pltpu.make_async_copy(source, target, sems.at[n])
        for n, (source, target) in enumerate(
            (
                (heat_hbm, heat_ref),
                (node_hbm, node_ref),
                (owner_hbm, owner_ref),
                (cell_hbm, cell_ref),
                (metal_hbm, metal_ref),
                (solid_hbm, mask_ref),
            )
        )
    ]
    strips = [
        pltpu.make_async_copy(
            flow_hbm.at[:, pl.ds(n * strip, strip)],
            flow_ref.at[:, pl.ds(n * strip, strip)],
            sems.at[len(small) + n],
        )
        for n in range(STRIPS)
    ]
    for copy in small + strips:
        copy.start()
    for copy in small:
        copy.wait()
    pack(
        count_ref,
        heat_ref,
        metal_ref,
        node_ref,
        owner_ref,
        cell_ref,
        chunks_ref,
        list_ref,
        counts_ref,
    )
    solid_ref[...] = mask_ref[...].astype(F32)
    for x in range(wide):
        if x % strip == 0:
            strips[x // strip].wait()
        flow = [flow_ref[i, x] for i in range(FLOWS)]
        heat = [heat_ref[k, x] for k in range(HEATS)]
        solid = mask_ref[x] != 0
        temper = heat[0]
        for k in range(1, HEATS):
            temper = temper + heat[k]
        post, speed = collide_flow(flow, solid)
        posth = lose(collide_heat(heat, temper, speed, solid), counts_ref[x], temper)
        for i in range(FLOWS):
            postf_ref[i, x] = post[i]
        for k in range(HEATS):
            posth_ref[k, x] = posth[k]

    def plane(i, x):
        return postf_ref[i, x] if i < FLOWS else posth_ref[i - FLOWS, x]

    def fill(right_ref, left_ref):
        for ref, faces, edge in ((right_ref, FACE_RIGHT, wide - 1), (left_ref, FACE_LEFT, 0)):
            for n, (i, depth) in enumerate(faces):
                ref[n] = plane(i, abs(edge - depth))
            ref[SOLID] = solid_ref[edge]
            ref[COUNTS] = counts_ref[edge]
            ref[LISTS] = list_ref[0:8]
            ref[LISTS + 1] = list_ref[8:16]

    @pl.when(odd)
    def _():
        fill(sendb_ref, senda_ref)

    @pl.when(jnp.logical_not(odd))
    def _():
        fill(senda_ref, sendb_ref)


def sides(odd, a_ref, b_ref):
    def low(n):
        return jnp.where(odd, a_ref[n], b_ref[n])

    def high(n):
        return jnp.where(odd, b_ref[n], a_ref[n])

    return low, high


def side_lists(get):
    return lists_of(jnp.concatenate([get(LISTS), get(LISTS + 1)], axis=0))


def planes(postf_ref, posth_ref, low, high, wide, source_ref):
    def get(i, x):
        if x < 0:
            value = low(FACE_RIGHT.index((i, -1 - x)))
        elif x >= wide:
            value = high(FACE_LEFT.index((i, x - wide)))
        elif i < FLOWS:
            value = postf_ref[i, x]
        else:
            value = posth_ref[i - FLOWS, x]
        if i >= FLOWS and source_ref is not None:
            value = value + WEIGHT_HEAT[i - FLOWS] * source_ref[x + 2]
        return value

    return get


def metal_rows(chunks_ref, shift):
    blocks = chunks_ref.shape[0]
    return [chunks_ref[d, shift + h : shift + h + 1] for d in range(blocks) for h in range(2)]


def metal_at(rows, *lists):
    return pick_twice(
        rows,
        [owner * 2 + (cell >> 7) for owner, cell, node in lists],
        [cell & 127 for owner, cell, node in lists],
    )


def give(metal, row, node, count):
    return add_up(
        WALL_COEFF * one_row(metal),
        rows_of(one_row(row), count),
        hot(rows_of(one_row(node) & 127, LANES)),
    )


def give_planes(metal, node, first, planes, deep):
    count = planes * deep
    return give(metal, (node >> 7) - first * deep, node, count).reshape(planes, deep, LANES)


def conduct(conduction, halves):
    vector = jnp.concatenate(halves, axis=1)
    parts = split_three(vector)
    rows = lax.broadcasted_iota(jnp.int32, (16, vector.shape[1]), 0)
    stacked = jnp.zeros((16, vector.shape[1]), F32)
    for r, part in enumerate(parts):
        stacked = jnp.where(rows == r, part.astype(F32), stacked)
    stacked = stacked.astype(BF16)
    out = sum([dot(stacked, part, ((1,), (1,))) for part in split_three(conduction)])
    return out[0:1] + out[1:2] + out[2:3]


def next_metal(conduction, metal, total, count):
    gained = WALL_COEFF * (total - count * metal)
    value = metal + METAL_GAIN * gained
    return conduct(conduction, [value[0:1], value[1:2]])


def source_kernel(
    postf_ref,
    posth_ref,
    recva_ref,
    recvb_ref,
    list_ref,
    chunks_ref,
    conduction_ref,
    senda_ref,
    sendb_ref,
    metal_ref,
    source_ref,
):
    wide, deep, lanes = postf_ref.shape[1:]
    blocks = chunks_ref.shape[0]
    sums = chunks_ref[0]
    for d in range(1, blocks):
        sums = sums + chunks_ref[d]
    count = sums[4:6]
    metal = next_metal(conduction_ref[...], list_ref[LIST_ROWS : LIST_ROWS + 2], sums[2:4], count)
    metal_ref[...] = jnp.zeros(metal_ref.shape, F32)
    put_rows(metal_ref, 0, metal)
    metal_ref[2:4, :] = count
    own = lists_of(list_ref[...])
    found = metal_at(metal_rows(chunks_ref, 0), own)[0]
    source_ref[2 : wide + 2] = give_planes(found, own[2], 0, wide, deep)
    low, high = sides(lax.axis_index("blk") % 2 == 1, recva_ref, recvb_ref)
    before, after = side_lists(low), side_lists(high)
    found = metal_at(metal_rows(chunks_ref, 0), before, after)
    source_ref[0:2] = give_planes(found[0], before[2], wide - 2, 2, deep)
    source_ref[wide + 2 :] = give_planes(found[1], after[2], 0, 2, deep)
    get = planes(postf_ref, posth_ref, low, high, wide, source_ref)

    def fill(up_ref, down_ref):
        for ref, comps, row in ((up_ref, UP, deep - 1), (down_ref, DOWN, 0)):
            for j in range(wide + 2):
                for n, i in enumerate(comps):
                    value = get(i, j - 1 - VELOCITY[i][0])
                    at = j * EDGES + n
                    ref[at : at + 1, :] = value[row : row + 1, :]
            at = (wide + 2) * EDGES
            put_rows(ref, at, metal)
            ref[at + 2 : at + 2 + LIST_ROWS, :] = list_ref[0:LIST_ROWS]

    for ref in (senda_ref, sendb_ref):
        ref[ref.shape[0] - 8 :, :] = jnp.zeros((8, lanes), F32)

    @pl.when(lax.axis_index("span") % 2 == 1)
    def _():
        fill(sendb_ref, senda_ref)

    @pl.when(lax.axis_index("span") % 2 == 0)
    def _():
        fill(senda_ref, sendb_ref)


def stream(get, edge, deep, i, x):
    cx, cy, cz = VELOCITY[i]
    value = get(i, x - cx)
    if cz != 0:
        rows = lax.broadcasted_iota(jnp.int32, value.shape, 0)
        if cz == 1:
            value = jnp.where(rows == 0, edge(i, x), pltpu.roll(value, 1, 0))
        else:
            value = jnp.where(rows == deep - 1, edge(i, x), pltpu.roll(value, deep - 1, 0))
    if cy != 0:
        value = pltpu.roll(value, cy % value.shape[1], 1)
    return value


def edge_rows(odd, a_ref, b_ref, first):
    def edge(i, x):
        comps = UP if VELOCITY[i][2] == 1 else DOWN
        at = (x - first) * EDGES + comps.index(i)
        a = a_ref[at : at + 1, :]
        b = b_ref[at : at + 1, :]
        if VELOCITY[i][2] == 1:
            return jnp.where(odd, a, b)
        return jnp.where(odd, b, a)

    return edge


def step_kernel(
    postf_ref,
    posth_ref,
    recva_ref,
    recvb_ref,
    source_ref,
    edgea_ref,
    edgeb_ref,
    list_ref,
    metal_ref,
    solid_ref,
    counts_ref,
    chunks_hbm,
    outf_ref,
    outh_ref,
    senda_ref,
    sendb_ref,
    out_ref,
    sem,
):
    wide, deep, lanes = posth_ref.shape[1:]
    blocks = out_ref.shape[0]
    low, high = sides(lax.axis_index("blk") % 2 == 1, recva_ref, recvb_ref)
    get = planes(None, posth_ref, low, high, wide, source_ref)
    odd = lax.axis_index("span") % 2 == 1
    edge = edge_rows(odd, edgea_ref, edgeb_ref, -1)
    tempers = []
    for x in range(-1, wide + 1):
        temper = None
        for k in range(HEATS):
            value = stream(get, edge, deep, FLOWS + k, x)
            outh_ref[k, x + 1] = value
            temper = value if temper is None else temper + value
        if 0 <= x < wide:
            tempers.append(temper)
    owner, cell, node = lists_of(list_ref[...])
    wall = one_row(wall_temper(tempers, node))
    owner, cell = one_row(owner), one_row(cell)
    row_mask = rows_of(owner * 2 + (cell >> 7), 2 * blocks)
    sums = add_up(wall, row_mask, hot(rows_of(cell & 127, lanes)))
    at = (wide + 2) * EDGES
    a = edgea_ref[at : at + 2, :]
    b = edgeb_ref[at : at + 2, :]
    for d in range(blocks):
        out_ref[d, 0:2, :] = metal_ref[0:2]
        out_ref[d, 2:4, :] = jnp.where(odd, a, b)
        out_ref[d, 4:6, :] = jnp.where(odd, b, a)
        out_ref[d, 6:8, :] = sums[2 * d : 2 * d + 2]
    copy = pltpu.make_async_copy(out_ref, chunks_hbm, sem)
    copy.start()
    get = planes(postf_ref, None, low, high, wide, None)
    for x in range(-1, wide + 1):
        flow = [stream(get, edge, deep, i, x) for i in range(FLOWS)]
        if x < 0:
            solid, counts = low(SOLID) != 0, low(COUNTS)
        elif x >= wide:
            solid, counts = high(SOLID) != 0, high(COUNTS)
        else:
            solid, counts = solid_ref[x] != 0, counts_ref[x]
        post, speed = collide_flow(flow, solid)
        heat = [outh_ref[k, x + 1] for k in range(HEATS)]
        temper = heat[0]
        for k in range(1, HEATS):
            temper = temper + heat[k]
        posth = lose(collide_heat(heat, temper, speed, solid), counts, temper)
        for i in range(FLOWS):
            outf_ref[i, x + 1] = post[i]
        for k in range(HEATS):
            outh_ref[k, x + 1] = posth[k]

    def fill(up_ref, down_ref):
        for ref, comps, row in ((up_ref, UP, deep - 1), (down_ref, DOWN, 0)):
            for x in range(wide):
                for n, i in enumerate(comps):
                    at = x + 1 - VELOCITY[i][0]
                    value = outf_ref[i, at] if i < FLOWS else outh_ref[i - FLOWS, at]
                    cy = VELOCITY[i][1]
                    value = pltpu.roll(value, cy % lanes, 1) if cy else value
                    ref[n, x] = value[row : row + 1, :]

    @pl.when(lax.axis_index("span") % 2 == 1)
    def _():
        fill(sendb_ref, senda_ref)

    @pl.when(lax.axis_index("span") % 2 == 0)
    def _():
        fill(senda_ref, sendb_ref)

    copy.wait()


def shift(value, i):
    cx, cy, cz = VELOCITY[i]
    if cz != 0:
        value = pltpu.roll(value, cz % value.shape[0], 0)
    if cy != 0:
        value = pltpu.roll(value, cy % value.shape[1], 1)
    return value


def stream_kernel(postf_ref, flow_hbm, flow_ref, sems):
    wide = flow_ref.shape[1]
    copies = []
    for n, i in enumerate(range(FLOWS)):
        for x in range(wide):
            flow_ref[i, x] = shift(postf_ref[i, x + 1 - VELOCITY[i][0]], i)
        if i % 4 == 3 or i == FLOWS - 1:
            part = pl.ds(i - i % 4, i % 4 + 1)
            copy = pltpu.make_async_copy(
                flow_ref.at[part], flow_hbm.at[part], sems.at[len(copies)]
            )
            copy.start()
            copies.append(copy)
    for copy in copies:
        copy.wait()


def heat_kernel(
    posth_ref,
    recva_ref,
    recvb_ref,
    list_ref,
    chunks_ref,
    edgea_ref,
    edgeb_ref,
    metal_ref,
    conduction_ref,
    heat_hbm,
    metal_hbm,
    row_ref,
    heat_ref,
    out_ref,
    sems,
):
    blocks = chunks_ref.shape[0]
    wide, deep, lanes = heat_ref.shape[1:]
    odd = lax.axis_index("span") % 2 == 1
    sums = chunks_ref[0]
    for d in range(1, blocks):
        sums = sums + chunks_ref[d]
    out_ref[...] = next_metal(conduction_ref[...], metal_ref[0:2], sums[6:8], metal_ref[2:4])
    copies = [pltpu.make_async_copy(out_ref, metal_hbm, sems.at[0])]
    copies[0].start()

    low, high = sides(lax.axis_index("blk") % 2 == 1, recva_ref, recvb_ref)
    own, before, after = lists_of(list_ref[...]), side_lists(low), side_lists(high)
    inner = metal_at(metal_rows(chunks_ref, 0), own)[0]
    found = metal_at(metal_rows(chunks_ref, 0), before, after)
    source = [give_planes(found[0], before[2], wide - 1, 1, deep)]
    source.append(give_planes(inner, own[2], 0, wide, deep))
    source.append(give_planes(found[1], after[2], 0, 1, deep))
    source = jnp.concatenate(source, axis=0)
    for k in range(HEATS):
        i = FLOWS + k
        for x in range(wide):
            at = x + 1 - VELOCITY[i][0]
            heat_ref[k, x] = shift(posth_ref[k, at] + WEIGHT_HEAT[k] * source[at], i)
    copies.append(pltpu.make_async_copy(heat_ref, heat_hbm, sems.at[1]))
    copies[1].start()

    at = (wide + 2) * EDGES + 2
    a = edgea_ref[at : at + LIST_ROWS, :]
    b = edgeb_ref[at : at + LIST_ROWS, :]
    for n, (block, moved, z) in enumerate(
        ((jnp.where(odd, a, b), 2, deep - 1), (jnp.where(odd, b, a), 4, 0))
    ):
        lists = lists_of(block)
        column = lists[2] >> 7
        row = jnp.where(lax.rem(column, deep) == z, lax.div(column, deep), -1)
        found = metal_at(metal_rows(chunks_ref, moved), lists)[0]
        row_ref[n * wide : (n + 1) * wide] = give(found, row, lists[2], wide)
    for copy in copies:
        copy.wait()


def edge_kernel(
    row_ref,
    lasta_ref,
    lastb_ref,
    flow_in,
    heat_in,
    flow_hbm,
    heat_hbm,
    rows_ref,
    sems,
):
    wide, deep, lanes = flow_hbm.shape[1:]

    def fill(low_ref, high_ref):
        copies = []
        for m, (ref, comps, z) in enumerate(((low_ref, UP, 0), (high_ref, DOWN, deep - 1))):
            for n, i in enumerate(comps):
                if i < FLOWS:
                    source, target = ref.at[n], flow_hbm.at[i]
                else:
                    source, target = rows_ref.at[m], heat_hbm.at[i - FLOWS]
                    for x in range(wide):
                        given = row_ref[m * wide + x : m * wide + x + 1, :]
                        rows_ref[m, x] = ref[n, x] + WEIGHT_HEAT[i - FLOWS] * given
                copy = pltpu.make_async_copy(
                    source, target.at[:, z : z + 1, :], sems.at[m * EDGES + n]
                )
                copy.start()
                copies.append(copy)
        for copy in copies:
            copy.wait()

    @pl.when(lax.axis_index("span") % 2 == 1)
    def _():
        fill(lasta_ref, lastb_ref)

    @pl.when(lax.axis_index("span") % 2 == 0)
    def _():
        fill(lastb_ref, lasta_ref)


def swap(value, axis, offset):
    count = lax.axis_size(axis)
    pairs = []
    for first in range(offset, count + offset, 2):
        one, other = first % count, (first + 1) % count
        pairs += [(one, other), (other, one)]
    return lax.ppermute(value, axis, pairs)


def local(
    populations,
    thermal,
    solid_mask,
    metal_temp,
    conduction,
    wall_count,
    wall_node,
    wall_owner,
    wall_cell,
):
    blocks = lax.axis_size("blk")
    wide, deep, lanes = solid_mask.shape
    smem = pl.BlockSpec(memory_space=pltpu.SMEM)
    hbm = pl.BlockSpec(memory_space=pltpu.HBM)
    near_spec = pl.BlockSpec(memory_space=pltpu.VMEM)

    def call(kernel, name, outs, scalars, *args, far=0, scratch=(), out_spec=None, alias=None):
        near = len(args) - far
        held = [pltpu.with_memory_space_constraint(arg, pltpu.HBM) for arg in args[near:]]
        out_spec = out_spec or jax.tree.map(lambda _: near_spec, outs)
        return pl.pallas_call(
            kernel,
            in_specs=[smem] * len(scalars) + in_vmem(near) + [hbm] * far,
            out_specs=out_spec,
            out_shape=outs,
            scratch_shapes=scratch,
            input_output_aliases=alias or {},
            compiler_params=params(),
            name=name,
        )(*scalars, *args[:near], *held)

    def to_all(chunks):
        return lax.all_to_all(chunks, "blk", 0, 0, tiled=True)

    side = shape(SIDE_PLANES, deep, lanes)
    field = shape(wide, deep, lanes)
    flows, heats = shape(FLOWS, wide, deep, lanes), shape(HEATS, wide, deep, lanes)
    chunks, lists, counts, solid, postf, posth, senda, sendb = call(
        first_kernel,
        "collide_first",
        (shape(blocks, 8, lanes), shape(16, lanes), field, field, flows, heats, side, side),
        (wall_count,),
        populations,
        thermal,
        solid_mask,
        metal_temp,
        wall_node,
        wall_owner.reshape(1, -1),
        wall_cell,
        far=7,
        scratch=[
            pltpu.VMEM(flows.shape, F32),
            pltpu.VMEM(heats.shape, F32),
            pltpu.VMEM(field.shape, jnp.int32),
            pltpu.VMEM(metal_temp.shape, F32),
            pltpu.VMEM(wall_node.shape, jnp.int32),
            pltpu.VMEM(wall_node.shape, jnp.int32),
            pltpu.VMEM(wall_node.shape, jnp.int32),
            pltpu.SemaphoreType.DMA((6 + STRIPS,)),
        ],
    )
    chunks = to_all(chunks)
    recva = swap(senda, "blk", 0)
    recvb = swap(sendb, "blk", 1)
    edge_count = -(-((wide + 2) * EDGES + 2 + LIST_ROWS) // 8) * 8
    edges = shape(edge_count, lanes)
    senda, sendb, metal, source = call(
        source_kernel,
        "source_first",
        (edges, edges, shape(8, lanes), shape(wide + 4, deep, lanes)),
        (),
        postf,
        posth,
        recva,
        recvb,
        lists,
        chunks,
        conduction,
    )
    edgea = swap(senda, "span", 0)
    edgeb = swap(sendb, "span", 1)
    edges = shape(EDGES, wide, 1, lanes)
    chunk = shape(blocks, 8, lanes)
    chunks, postf, posth, senda, sendb = call(
        step_kernel,
        "collide_second",
        (
            chunk,
            shape(FLOWS, wide + 2, deep, lanes),
            shape(HEATS, wide + 2, deep, lanes),
            edges,
            edges,
        ),
        (),
        postf,
        posth,
        recva,
        recvb,
        source,
        edgea,
        edgeb,
        lists,
        metal,
        solid,
        counts,
        scratch=[pltpu.VMEM(chunk.shape, F32), pltpu.SemaphoreType.DMA],
        out_spec=(hbm,) + (near_spec,) * 4,
    )
    chunks = to_all(chunks)
    lasta = swap(senda, "span", 0)
    lastb = swap(sendb, "span", 1)
    part = call(
        stream_kernel,
        "stream_flow",
        flows,
        (),
        postf,
        scratch=[pltpu.VMEM(flows.shape, F32), pltpu.SemaphoreType.DMA((-(-FLOWS // 4),))],
        out_spec=hbm,
    )
    heat, metal, rows = call(
        heat_kernel,
        "stream_heat",
        (heats, shape(*metal_temp.shape), shape(2 * wide, lanes)),
        (),
        posth,
        recva,
        recvb,
        lists,
        chunks,
        edgea,
        edgeb,
        metal,
        conduction,
        scratch=[
            pltpu.VMEM(heats.shape, F32),
            pltpu.VMEM(metal_temp.shape, F32),
            pltpu.SemaphoreType.DMA((2,)),
        ],
        out_spec=(hbm, hbm, near_spec),
    )
    flow, heat = call(
        edge_kernel,
        "stream_edges",
        (flows, heats),
        (),
        rows,
        lasta,
        lastb,
        part,
        heat,
        far=2,
        scratch=[
            pltpu.VMEM((2, wide, 1, lanes), F32),
            pltpu.SemaphoreType.DMA((2 * EDGES,)),
        ],
        out_spec=(hbm, hbm),
        alias={3: 0, 4: 1},
    )
    return (flow, heat, metal)


def solution(mesh):
    in_specs = (
        P(None, "blk", "span", None),
        P(None, "blk", "span", None),
        P("blk", "span", None),
        P("span", "blk"),
        P("span", "blk"),
        P("span", "blk"),
        P("span", "blk"),
        P("span", "blk", None),
        P("span", "blk"),
    )
    out_specs = (P(None, "blk", "span", None), P(None, "blk", "span", None), P("span", "blk"))
    return jax.shard_map(local, mesh=mesh, in_specs=in_specs, out_specs=out_specs, check_vma=False)
```

```python
import jax
import jax.numpy as jnp
from jax import lax
from jax.experimental import pallas as pl
from jax.experimental.pallas import tpu as pltpu
from jax.sharding import PartitionSpec as P

VELOCITY_FLOW = [
    (0, 0, 0),
    (1, 0, 0),
    (-1, 0, 0),
    (0, 1, 0),
    (0, -1, 0),
    (0, 0, 1),
    (0, 0, -1),
    (1, 1, 0),
    (-1, -1, 0),
    (1, -1, 0),
    (-1, 1, 0),
    (1, 0, 1),
    (-1, 0, -1),
    (1, 0, -1),
    (-1, 0, 1),
    (0, 1, 1),
    (0, -1, -1),
    (0, 1, -1),
    (0, -1, 1),
]
WEIGHT_FLOW = [1.0 / 3.0] + [1.0 / 18.0] * 6 + [1.0 / 36.0] * 12
OPPOSITE = [0, 2, 1, 4, 3, 6, 5, 8, 7, 10, 9, 12, 11, 14, 13, 16, 15, 18, 17]
WEIGHT_HEAT = [0.25] + [0.125] * 6
VELOCITY = VELOCITY_FLOW + VELOCITY_FLOW[:7]
FLOWS, HEATS = 19, 7
ALL = FLOWS + HEATS
RELAX_FLOW = 0.8
RELAX_HEAT = 0.9
WALL_COEFF = 0.5
METAL_GAIN = 0.5

FACE_RIGHT = [(i, 0) for i in range(ALL) if VELOCITY[i][0] >= 0] + [
    (i, 1) for i in range(ALL) if VELOCITY[i][0] == 1
]
FACE_LEFT = [(i, 0) for i in range(ALL) if VELOCITY[i][0] <= 0] + [
    (i, 1) for i in range(ALL) if VELOCITY[i][0] == -1
]
FACES = len(FACE_RIGHT)
UP = [i for i in range(ALL) if VELOCITY[i][2] == 1]
DOWN = [i for i in range(ALL) if VELOCITY[i][2] == -1]
EDGES = len(UP)
SOLID, COUNTS, LISTS = FACES, FACES + 1, FACES + 2
SIDE_PLANES = FACES + 4
LIST_ROWS = 12
LANES = 128
F32 = jnp.float32
BF16 = jnp.bfloat16


def params(mebibytes=32):
    return pltpu.CompilerParams(vmem_limit_bytes=mebibytes * 1024 * 1024)


def in_vmem(count):
    return [pl.BlockSpec(memory_space=pltpu.VMEM)] * count


def shape(*dims):
    return jax.ShapeDtypeStruct(dims, F32)


def split(value):
    high = value.astype(BF16)
    low = (value - high.astype(F32)).astype(BF16)
    return high, low


def split_three(value):
    high = value.astype(BF16)
    rest = value - high.astype(F32)
    middle = rest.astype(BF16)
    low = (rest - middle.astype(F32)).astype(BF16)
    return high, middle, low


def dot(left, right, dims):
    return lax.dot_general(left, right, (dims, ((), ())), preferred_element_type=F32)


def rows_of(row, count):
    return lax.broadcasted_iota(jnp.int32, (count, row.shape[1]), 0) == row


def hot(mask):
    return jnp.where(mask, 1.0, 0.0).astype(BF16)


def pick(rows, row_index, lane_index):
    found = jnp.zeros(lane_index.shape, F32)
    for r, row in enumerate(rows):
        whole = jnp.broadcast_to(row, lane_index.shape)
        value = jnp.take_along_axis(whole, lane_index, axis=1, mode="promise_in_bounds")
        found = jnp.where(row_index == r, value, found)
    return found


def pick_twice(rows, row_index, lane_index):
    first, second = (row_index, lane_index) if len(row_index) == 2 else (row_index * 2, lane_index * 2)
    found = pick(rows, jnp.concatenate(first, axis=0), jnp.concatenate(second, axis=0))
    return [found[4 * n : 4 * n + 4] for n in range(len(row_index))]


def add_up(values, row_mask, lane_hot):
    count = row_mask.shape[0]
    stacked = jnp.concatenate(
        [jnp.where(row_mask, part.astype(F32), 0.0) for part in split(values)], axis=0
    ).astype(BF16)
    sums = dot(stacked, lane_hot, ((1,), (1,)))
    return sums[:count] + sums[count:]


def one_row(block):
    return jnp.concatenate([block[r : r + 1] for r in range(block.shape[0])], axis=1)


def put_rows(ref, start, row):
    for r in range(row.shape[1] // LANES):
        ref[start + r : start + r + 1, :] = row[:, r * LANES : (r + 1) * LANES]


def lists_of(block):
    return [block[4 * n : 4 * n + 4].astype(jnp.int32) for n in range(3)]


def wall_temper(tempers, node):
    rows = [temper[z : z + 1] for temper in tempers for z in range(temper.shape[0])]
    return pick_twice(rows, [node >> 7], [node & 127])[0]


def pack(
    count_ref, heat_ref, metal_ref, node_ref, owner_ref, cell_ref, out_ref, list_ref, counts_ref
):
    blocks = out_ref.shape[0]
    wide, deep, lanes = heat_ref.shape[1:]
    tempers = []
    for x in range(wide):
        temper = heat_ref[0, x]
        for k in range(1, HEATS):
            temper = temper + heat_ref[k, x]
        tempers.append(temper)
    node = node_ref[...]
    cell = cell_ref[...]
    entries = node.shape[1]
    live = lax.broadcasted_iota(jnp.int32, (1, entries), 1) < count_ref[0, 0]
    owner = jnp.where(live, owner_ref[...], -1)
    list_ref[8:16, :] = jnp.zeros((8, lanes), F32)
    put_rows(list_ref, 0, owner.astype(F32))
    put_rows(list_ref, 4, cell.astype(F32))
    put_rows(list_ref, 8, node.astype(F32))
    put_rows(list_ref, LIST_ROWS, metal_ref[...])
    lane_mask = rows_of(node & 127, lanes)
    nodes = list_ref[8:12].astype(jnp.int32)
    wall = one_row(wall_temper(tempers, nodes))
    cell_hot = hot(rows_of(cell & 127, lanes))
    row_mask = rows_of(owner * 2 + (cell >> 7), 2 * blocks)
    sums = add_up(wall, row_mask, cell_hot)
    counts = dot(hot(row_mask), cell_hot, ((1,), (1,)))
    for d in range(blocks):
        put_rows(out_ref.at[d], 0, metal_ref[...])
        out_ref[d, 2:4, :] = sums[2 * d : 2 * d + 2]
        out_ref[d, 4:6, :] = counts[2 * d : 2 * d + 2]
        out_ref[d, 6:8, :] = jnp.zeros((2, lanes), F32)
    at_nodes = dot(
        hot(rows_of(jnp.where(live, node >> 7, -1), wide * deep)), hot(lane_mask), ((1,), (1,))
    )
    counts_ref[...] = at_nodes.reshape(wide, deep, lanes)


def tree(values):
    while len(values) > 1:
        values = [sum(values[n : n + 2][1:], values[n]) for n in range(0, len(values), 2)]
    return values[0]


def collide_flow(flow, solid):
    pairs = range(1, FLOWS, 2)
    gap = {i: flow[i] - flow[i + 1] for i in pairs}
    density = tree([flow[0]] + [flow[i] + flow[i + 1] for i in pairs])
    inverse = 1.0 / density
    speed = []
    for axis in range(3):
        terms = [
            gap[i] if VELOCITY[i][axis] == 1 else -gap[i] for i in pairs if VELOCITY[i][axis] != 0
        ]
        speed.append(tree(terms) * inverse)
    base = 1.0 - 1.5 * (speed[0] * speed[0] + speed[1] * speed[1] + speed[2] * speed[2])
    scaled = {w: density * (w / RELAX_FLOW) for w in sorted(set(WEIGHT_FLOW))}
    keep = 1.0 - 1.0 / RELAX_FLOW
    post = [None] * FLOWS
    rest = scaled[WEIGHT_FLOW[0]] * base + keep * flow[0]
    post[0] = jnp.where(solid, flow[0], rest)
    for i in pairs:
        along = None
        for axis in range(3):
            c = VELOCITY[i][axis]
            if c == 0:
                continue
            term = speed[axis]
            if along is None:
                along = term if c == 1 else -term
            else:
                along = along + term if c == 1 else along - term
        weight = scaled[WEIGHT_FLOW[i]]
        even = weight * (base + 4.5 * along * along)
        odd = weight * (3.0 * along)
        j = OPPOSITE[i]
        post[i] = jnp.where(solid, flow[j], even + odd + keep * flow[i])
        post[j] = jnp.where(solid, flow[i], even - odd + keep * flow[j])
    return post, speed


def collide_heat(heat, temper, speed, solid):
    keep = 1.0 - 1.0 / RELAX_HEAT
    post = [None] * HEATS
    post[0] = jnp.where(
        solid, heat[0], temper * (WEIGHT_HEAT[0] / RELAX_HEAT) + keep * heat[0]
    )
    scaled = temper * (WEIGHT_HEAT[1] / RELAX_HEAT)
    for axis in range(3):
        i = 2 * axis + 1
        j = i + 1
        odd = scaled * (4.0 * speed[axis])
        post[i] = jnp.where(solid, heat[j], scaled + odd + keep * heat[i])
        post[j] = jnp.where(solid, heat[i], scaled - odd + keep * heat[j])
    return post


def lose(post, counts, temper):
    lost = counts * temper * -WALL_COEFF
    return [post[k] + WEIGHT_HEAT[k] * lost for k in range(HEATS)]


def first_kernel(
    count_ref,
    flow_hbm,
    heat_hbm,
    solid_hbm,
    metal_hbm,
    node_hbm,
    owner_hbm,
    cell_hbm,
    chunks_ref,
    list_ref,
    counts_ref,
    solid_ref,
    postf_ref,
    posth_ref,
    senda_ref,
    sendb_ref,
    flow_ref,
    heat_ref,
    mask_ref,
    metal_ref,
    node_ref,
    owner_ref,
    cell_ref,
    sems,
):
    wide = flow_ref.shape[1]
    odd = lax.axis_index("blk") % 2 == 1
    small = [
        pltpu.make_async_copy(source, target, sems.at[n])
        for n, (source, target) in enumerate(
            (
                (heat_hbm, heat_ref),
                (node_hbm, node_ref),
                (owner_hbm, owner_ref),
                (cell_hbm, cell_ref),
                (metal_hbm, metal_ref),
                (solid_hbm, mask_ref),
            )
        )
    ]
    large = pltpu.make_async_copy(flow_hbm, flow_ref, sems.at[len(small)])
    for copy in small + [large]:
        copy.start()
    for copy in small:
        copy.wait()
    pack(
        count_ref,
        heat_ref,
        metal_ref,
        node_ref,
        owner_ref,
        cell_ref,
        chunks_ref,
        list_ref,
        counts_ref,
    )
    solid_ref[...] = mask_ref[...].astype(F32)
    large.wait()
    for x in range(wide):
        flow = [flow_ref[i, x] for i in range(FLOWS)]
        heat = [heat_ref[k, x] for k in range(HEATS)]
        solid = mask_ref[x] != 0
        temper = heat[0]
        for k in range(1, HEATS):
            temper = temper + heat[k]
        post, speed = collide_flow(flow, solid)
        posth = lose(collide_heat(heat, temper, speed, solid), counts_ref[x], temper)
        for i in range(FLOWS):
            postf_ref[i, x] = post[i]
        for k in range(HEATS):
            posth_ref[k, x] = posth[k]

    def plane(i, x):
        return postf_ref[i, x] if i < FLOWS else posth_ref[i - FLOWS, x]

    def fill(right_ref, left_ref):
        for ref, faces, edge in ((right_ref, FACE_RIGHT, wide - 1), (left_ref, FACE_LEFT, 0)):
            for n, (i, depth) in enumerate(faces):
                ref[n] = plane(i, abs(edge - depth))
            ref[SOLID] = solid_ref[edge]
            ref[COUNTS] = counts_ref[edge]
            ref[LISTS] = list_ref[0:8]
            ref[LISTS + 1] = list_ref[8:16]

    @pl.when(odd)
    def _():
        fill(sendb_ref, senda_ref)

    @pl.when(jnp.logical_not(odd))
    def _():
        fill(senda_ref, sendb_ref)


def sides(odd, a_ref, b_ref):
    def low(n):
        return jnp.where(odd, a_ref[n], b_ref[n])

    def high(n):
        return jnp.where(odd, b_ref[n], a_ref[n])

    return low, high


def side_lists(get):
    return lists_of(jnp.concatenate([get(LISTS), get(LISTS + 1)], axis=0))


def planes(postf_ref, posth_ref, low, high, wide, source_ref):
    def get(i, x):
        if x < 0:
            value = low(FACE_RIGHT.index((i, -1 - x)))
        elif x >= wide:
            value = high(FACE_LEFT.index((i, x - wide)))
        elif i < FLOWS:
            value = postf_ref[i, x]
        else:
            value = posth_ref[i - FLOWS, x]
        if i >= FLOWS and source_ref is not None:
            value = value + WEIGHT_HEAT[i - FLOWS] * source_ref[x + 2]
        return value

    return get


def metal_rows(chunks_ref, shift):
    blocks = chunks_ref.shape[0]
    return [chunks_ref[d, shift + h : shift + h + 1] for d in range(blocks) for h in range(2)]


def metal_at(rows, *lists):
    return pick_twice(
        rows,
        [owner * 2 + (cell >> 7) for owner, cell, node in lists],
        [cell & 127 for owner, cell, node in lists],
    )


def give(metal, row, node, count):
    return add_up(
        WALL_COEFF * one_row(metal),
        rows_of(one_row(row), count),
        hot(rows_of(one_row(node) & 127, LANES)),
    )


def give_planes(metal, node, first, planes, deep):
    count = planes * deep
    return give(metal, (node >> 7) - first * deep, node, count).reshape(planes, deep, LANES)


def conduct(conduction, halves):
    vector = jnp.concatenate(halves, axis=1)
    parts = split_three(vector)
    rows = lax.broadcasted_iota(jnp.int32, (16, vector.shape[1]), 0)
    stacked = jnp.zeros((16, vector.shape[1]), F32)
    for r, part in enumerate(parts):
        stacked = jnp.where(rows == r, part.astype(F32), stacked)
    stacked = stacked.astype(BF16)
    out = sum([dot(stacked, part, ((1,), (1,))) for part in split_three(conduction)])
    return out[0:1] + out[1:2] + out[2:3]


def next_metal(conduction, metal, total, count):
    gained = WALL_COEFF * (total - count * metal)
    value = metal + METAL_GAIN * gained
    return conduct(conduction, [value[0:1], value[1:2]])


def source_kernel(
    postf_ref,
    posth_ref,
    recva_ref,
    recvb_ref,
    list_ref,
    chunks_ref,
    conduction_ref,
    up_ref,
    down_ref,
    metal_ref,
    source_ref,
):
    wide, deep, lanes = postf_ref.shape[1:]
    blocks = chunks_ref.shape[0]
    sums = chunks_ref[0]
    for d in range(1, blocks):
        sums = sums + chunks_ref[d]
    count = sums[4:6]
    metal = next_metal(conduction_ref[...], list_ref[LIST_ROWS : LIST_ROWS + 2], sums[2:4], count)
    metal_ref[...] = jnp.zeros(metal_ref.shape, F32)
    put_rows(metal_ref, 0, metal)
    metal_ref[2:4, :] = count
    own = lists_of(list_ref[...])
    found = metal_at(metal_rows(chunks_ref, 0), own)[0]
    source_ref[2 : wide + 2] = give_planes(found, own[2], 0, wide, deep)
    low, high = sides(lax.axis_index("blk") % 2 == 1, recva_ref, recvb_ref)
    before, after = side_lists(low), side_lists(high)
    found = metal_at(metal_rows(chunks_ref, 0), before, after)
    source_ref[0:2] = give_planes(found[0], before[2], wide - 2, 2, deep)
    source_ref[wide + 2 :] = give_planes(found[1], after[2], 0, 2, deep)
    get = planes(postf_ref, posth_ref, low, high, wide, source_ref)

    for ref in (up_ref, down_ref):
        ref[ref.shape[0] - 8 :, :] = jnp.zeros((8, lanes), F32)
    for ref, comps, row in ((up_ref, UP, deep - 1), (down_ref, DOWN, 0)):
        for j in range(wide + 2):
            for n, i in enumerate(comps):
                value = get(i, j - 1 - VELOCITY[i][0])
                at = j * EDGES + n
                ref[at : at + 1, :] = value[row : row + 1, :]
        at = (wide + 2) * EDGES
        put_rows(ref, at, metal)
        ref[at + 2 : at + 2 + LIST_ROWS, :] = list_ref[0:LIST_ROWS]


def stream(get, edge, deep, i, x):
    cx, cy, cz = VELOCITY[i]
    value = get(i, x - cx)
    if cz != 0:
        rows = lax.broadcasted_iota(jnp.int32, value.shape, 0)
        if cz == 1:
            value = jnp.where(rows == 0, edge(i, x), pltpu.roll(value, 1, 0))
        else:
            value = jnp.where(rows == deep - 1, edge(i, x), pltpu.roll(value, deep - 1, 0))
    if cy != 0:
        value = pltpu.roll(value, cy % value.shape[1], 1)
    return value


def edge_rows(low_ref, high_ref, first):
    def edge(i, x):
        ref, comps = (low_ref, UP) if VELOCITY[i][2] == 1 else (high_ref, DOWN)
        at = (x - first) * EDGES + comps.index(i)
        return ref[at : at + 1, :]

    return edge


def step_kernel(
    postf_ref,
    posth_ref,
    recva_ref,
    recvb_ref,
    source_ref,
    low_edge_ref,
    high_edge_ref,
    list_ref,
    metal_ref,
    solid_ref,
    counts_ref,
    chunks_hbm,
    outf_ref,
    outh_ref,
    up_ref,
    down_ref,
    out_ref,
    sem,
):
    wide, deep, lanes = posth_ref.shape[1:]
    blocks = out_ref.shape[0]
    low, high = sides(lax.axis_index("blk") % 2 == 1, recva_ref, recvb_ref)
    get = planes(None, posth_ref, low, high, wide, source_ref)
    edge = edge_rows(low_edge_ref, high_edge_ref, -1)
    tempers = []
    for x in range(-1, wide + 1):
        temper = None
        for k in range(HEATS):
            value = stream(get, edge, deep, FLOWS + k, x)
            outh_ref[k, x + 1] = value
            temper = value if temper is None else temper + value
        if 0 <= x < wide:
            tempers.append(temper)
    owner, cell, node = lists_of(list_ref[...])
    wall = one_row(wall_temper(tempers, node))
    owner, cell = one_row(owner), one_row(cell)
    row_mask = rows_of(owner * 2 + (cell >> 7), 2 * blocks)
    sums = add_up(wall, row_mask, hot(rows_of(cell & 127, lanes)))
    at = (wide + 2) * EDGES
    below, above = low_edge_ref[at : at + 2, :], high_edge_ref[at : at + 2, :]
    for d in range(blocks):
        out_ref[d, 0:2, :] = metal_ref[0:2]
        out_ref[d, 2:4, :] = below
        out_ref[d, 4:6, :] = above
        out_ref[d, 6:8, :] = sums[2 * d : 2 * d + 2]
    copy = pltpu.make_async_copy(out_ref, chunks_hbm, sem)
    copy.start()
    get = planes(postf_ref, None, low, high, wide, None)
    for x in range(-1, wide + 1):
        flow = [stream(get, edge, deep, i, x) for i in range(FLOWS)]
        if x < 0:
            solid, counts = low(SOLID) != 0, low(COUNTS)
        elif x >= wide:
            solid, counts = high(SOLID) != 0, high(COUNTS)
        else:
            solid, counts = solid_ref[x] != 0, counts_ref[x]
        post, speed = collide_flow(flow, solid)
        heat = [outh_ref[k, x + 1] for k in range(HEATS)]
        temper = heat[0]
        for k in range(1, HEATS):
            temper = temper + heat[k]
        posth = lose(collide_heat(heat, temper, speed, solid), counts, temper)
        for i in range(FLOWS):
            outf_ref[i, x + 1] = post[i]
        for k in range(HEATS):
            outh_ref[k, x + 1] = posth[k]

    for ref, comps, row in ((up_ref, UP, deep - 1), (down_ref, DOWN, 0)):
        for x in range(wide):
            for n, i in enumerate(comps):
                at = x + 1 - VELOCITY[i][0]
                value = outf_ref[i, at] if i < FLOWS else outh_ref[i - FLOWS, at]
                cy = VELOCITY[i][1]
                value = pltpu.roll(value, cy % lanes, 1) if cy else value
                ref[n, x] = value[row : row + 1, :]

    copy.wait()


def shift(value, i):
    cx, cy, cz = VELOCITY[i]
    if cz != 0:
        value = pltpu.roll(value, cz % value.shape[0], 0)
    if cy != 0:
        value = pltpu.roll(value, cy % value.shape[1], 1)
    return value


def stream_kernel(postf_ref, flow_hbm, flow_ref, sems):
    wide = flow_ref.shape[1]
    copies = []
    for n, i in enumerate(range(FLOWS)):
        for x in range(wide):
            flow_ref[i, x] = shift(postf_ref[i, x + 1 - VELOCITY[i][0]], i)
        if i % 4 == 3 or i == FLOWS - 1:
            part = pl.ds(i - i % 4, i % 4 + 1)
            copy = pltpu.make_async_copy(
                flow_ref.at[part], flow_hbm.at[part], sems.at[len(copies)]
            )
            copy.start()
            copies.append(copy)
    for copy in copies:
        copy.wait()


def heat_kernel(
    posth_ref,
    recva_ref,
    recvb_ref,
    list_ref,
    chunks_ref,
    low_edge_ref,
    high_edge_ref,
    metal_ref,
    conduction_ref,
    heat_ref,
    out_ref,
    row_ref,
):
    blocks = chunks_ref.shape[0]
    wide, deep, lanes = heat_ref.shape[1:]
    sums = chunks_ref[0]
    for d in range(1, blocks):
        sums = sums + chunks_ref[d]
    out_ref[...] = next_metal(conduction_ref[...], metal_ref[0:2], sums[6:8], metal_ref[2:4])
    low, high = sides(lax.axis_index("blk") % 2 == 1, recva_ref, recvb_ref)
    own, before, after = lists_of(list_ref[...]), side_lists(low), side_lists(high)
    inner = metal_at(metal_rows(chunks_ref, 0), own)[0]
    found = metal_at(metal_rows(chunks_ref, 0), before, after)
    source = [give_planes(found[0], before[2], wide - 1, 1, deep)]
    source.append(give_planes(inner, own[2], 0, wide, deep))
    source.append(give_planes(found[1], after[2], 0, 1, deep))
    source = jnp.concatenate(source, axis=0)
    for k in range(HEATS):
        i = FLOWS + k
        for x in range(wide):
            at = x + 1 - VELOCITY[i][0]
            heat_ref[k, x] = shift(posth_ref[k, at] + WEIGHT_HEAT[k] * source[at], i)

    at = (wide + 2) * EDGES + 2
    for n, (ref, moved, z) in enumerate(((low_edge_ref, 2, deep - 1), (high_edge_ref, 4, 0))):
        lists = lists_of(ref[at : at + LIST_ROWS, :])
        column = lists[2] >> 7
        row = jnp.where(lax.rem(column, deep) == z, lax.div(column, deep), -1)
        found = metal_at(metal_rows(chunks_ref, moved), lists)[0]
        row_ref[n * wide : (n + 1) * wide] = give(found, row, lists[2], wide)


def edge_kernel(
    heat_ref,
    metal_ref,
    row_ref,
    low_ref,
    high_ref,
    flow_in,
    flow_hbm,
    heat_hbm,
    metal_hbm,
    tilted_ref,
    sems,
):
    wide, deep, lanes = flow_hbm.shape[1:]
    level = HEATS - 2
    sublane = lax.broadcasted_iota(jnp.int32, (deep, lanes), 0)

    copies = [
        pltpu.make_async_copy(
            heat_ref.at[pl.ds(0, level)], heat_hbm.at[pl.ds(0, level)], sems.at[0]
        ),
        pltpu.make_async_copy(metal_ref, metal_hbm, sems.at[1]),
    ]
    for m, (ref, comps, z) in enumerate(((low_ref, UP, 0), (high_ref, DOWN, deep - 1))):
        for n, i in enumerate(comps[:-1]):
            copies.append(
                pltpu.make_async_copy(
                    ref.at[n],
                    flow_hbm.at[i, :, z : z + 1, :],
                    sems.at[3 + m * EDGES + n],
                )
            )
    for copy in copies:
        copy.start()
    for m, (ref, comps, z) in enumerate(((low_ref, UP, 0), (high_ref, DOWN, deep - 1))):
        for x in range(wide):
            given = row_ref[m * wide + x : m * wide + x + 1, :]
            row = ref[EDGES - 1, x] + WEIGHT_HEAT[level + m] * given
            tilted_ref[m, x] = jnp.where(sublane == z, row, heat_ref[level + m, x])
    copies.append(
        pltpu.make_async_copy(tilted_ref, heat_hbm.at[pl.ds(level, 2)], sems.at[2])
    )
    copies[-1].start()
    for copy in copies:
        copy.wait()


def swap(value, axis, offset):
    count = lax.axis_size(axis)
    pairs = []
    for first in range(offset, count + offset, 2):
        one, other = first % count, (first + 1) % count
        pairs += [(one, other), (other, one)]
    return lax.ppermute(value, axis, pairs)


def shift_both(up, down, axis):
    count = lax.axis_size(axis)
    ahead = [(i, (i + 1) % count) for i in range(count)]
    return lax.ppermute(up, axis, ahead), lax.ppermute(down, axis, [(j, i) for i, j in ahead])


def local(
    populations,
    thermal,
    solid_mask,
    metal_temp,
    conduction,
    wall_count,
    wall_node,
    wall_owner,
    wall_cell,
):
    blocks = lax.axis_size("blk")
    wide, deep, lanes = solid_mask.shape
    smem = pl.BlockSpec(memory_space=pltpu.SMEM)
    hbm = pl.BlockSpec(memory_space=pltpu.HBM)
    near_spec = pl.BlockSpec(memory_space=pltpu.VMEM)

    def call(kernel, name, outs, scalars, *args, far=0, scratch=(), out_spec=None, alias=None):
        near = len(args) - far
        held = [pltpu.with_memory_space_constraint(arg, pltpu.HBM) for arg in args[near:]]
        out_spec = out_spec or jax.tree.map(lambda _: near_spec, outs)
        return pl.pallas_call(
            kernel,
            in_specs=[smem] * len(scalars) + in_vmem(near) + [hbm] * far,
            out_specs=out_spec,
            out_shape=outs,
            scratch_shapes=scratch,
            input_output_aliases=alias or {},
            compiler_params=params(),
            name=name,
        )(*scalars, *args[:near], *held)

    def to_all(chunks):
        return lax.all_to_all(chunks, "blk", 0, 0, tiled=True)

    side = shape(SIDE_PLANES, deep, lanes)
    field = shape(wide, deep, lanes)
    flows, heats = shape(FLOWS, wide, deep, lanes), shape(HEATS, wide, deep, lanes)
    chunks, lists, counts, solid, postf, posth, senda, sendb = call(
        first_kernel,
        "collide_first",
        (shape(blocks, 8, lanes), shape(16, lanes), field, field, flows, heats, side, side),
        (wall_count,),
        populations,
        thermal,
        solid_mask,
        metal_temp,
        wall_node,
        wall_owner.reshape(1, -1),
        wall_cell,
        far=7,
        scratch=[
            pltpu.VMEM(flows.shape, F32),
            pltpu.VMEM(heats.shape, F32),
            pltpu.VMEM(field.shape, jnp.int32),
            pltpu.VMEM(metal_temp.shape, F32),
            pltpu.VMEM(wall_node.shape, jnp.int32),
            pltpu.VMEM(wall_node.shape, jnp.int32),
            pltpu.VMEM(wall_node.shape, jnp.int32),
            pltpu.SemaphoreType.DMA((7,)),
        ],
    )
    chunks = to_all(chunks)
    recva = swap(senda, "blk", 0)
    recvb = swap(sendb, "blk", 1)
    edge_count = -(-((wide + 2) * EDGES + 2 + LIST_ROWS) // 8) * 8
    edges = shape(edge_count, lanes)
    up, down, metal, source = call(
        source_kernel,
        "source_first",
        (edges, edges, shape(8, lanes), shape(wide + 4, deep, lanes)),
        (),
        postf,
        posth,
        recva,
        recvb,
        lists,
        chunks,
        conduction,
    )
    low_edge, high_edge = shift_both(up, down, "span")
    edges = shape(EDGES, wide, 1, lanes)
    chunk = shape(blocks, 8, lanes)
    chunks, postf, posth, up, down = call(
        step_kernel,
        "collide_second",
        (
            chunk,
            shape(FLOWS, wide + 2, deep, lanes),
            shape(HEATS, wide + 2, deep, lanes),
            edges,
            edges,
        ),
        (),
        postf,
        posth,
        recva,
        recvb,
        source,
        low_edge,
        high_edge,
        lists,
        metal,
        solid,
        counts,
        scratch=[pltpu.VMEM(chunk.shape, F32), pltpu.SemaphoreType.DMA],
        out_spec=(hbm,) + (near_spec,) * 4,
    )
    chunks = to_all(chunks)
    low_last, high_last = shift_both(up, down, "span")
    part = call(
        stream_kernel,
        "stream_flow",
        flows,
        (),
        postf,
        scratch=[pltpu.VMEM(flows.shape, F32), pltpu.SemaphoreType.DMA((-(-FLOWS // 4),))],
        out_spec=hbm,
    )
    heat, metal, rows = call(
        heat_kernel,
        "stream_heat",
        (heats, shape(*metal_temp.shape), shape(2 * wide, lanes)),
        (),
        posth,
        recva,
        recvb,
        lists,
        chunks,
        low_edge,
        high_edge,
        metal,
        conduction,
    )
    return call(
        edge_kernel,
        "write_last",
        (flows, heats, shape(*metal_temp.shape)),
        (),
        heat,
        metal,
        rows,
        low_last,
        high_last,
        part,
        far=1,
        scratch=[
            pltpu.VMEM((2, wide, deep, lanes), F32),
            pltpu.SemaphoreType.DMA((3 + 2 * EDGES,)),
        ],
        out_spec=(hbm,) * 3,
        alias={5: 0},
    )


def solution(mesh):
    in_specs = (
        P(None, "blk", "span", None),
        P(None, "blk", "span", None),
        P("blk", "span", None),
        P("span", "blk"),
        P("span", "blk"),
        P("span", "blk"),
        P("span", "blk"),
        P("span", "blk", None),
        P("span", "blk"),
    )
    out_specs = (P(None, "blk", "span", None), P(None, "blk", "span", None), P("span", "blk"))
    return jax.shard_map(local, mesh=mesh, in_specs=in_specs, out_specs=out_specs, check_vma=False)
```

```python
import jax
import jax.numpy as jnp
from jax import lax
from jax.experimental import pallas as pl
from jax.experimental.pallas import tpu as pltpu
from jax.sharding import PartitionSpec as P

VELOCITY_FLOW = [
    (0, 0, 0),
    (1, 0, 0),
    (-1, 0, 0),
    (0, 1, 0),
    (0, -1, 0),
    (0, 0, 1),
    (0, 0, -1),
    (1, 1, 0),
    (-1, -1, 0),
    (1, -1, 0),
    (-1, 1, 0),
    (1, 0, 1),
    (-1, 0, -1),
    (1, 0, -1),
    (-1, 0, 1),
    (0, 1, 1),
    (0, -1, -1),
    (0, 1, -1),
    (0, -1, 1),
]
WEIGHT_FLOW = [1.0 / 3.0] + [1.0 / 18.0] * 6 + [1.0 / 36.0] * 12
OPPOSITE = [0, 2, 1, 4, 3, 6, 5, 8, 7, 10, 9, 12, 11, 14, 13, 16, 15, 18, 17]
WEIGHT_HEAT = [0.25] + [0.125] * 6
VELOCITY = VELOCITY_FLOW + VELOCITY_FLOW[:7]
FLOWS, HEATS = 19, 7
ALL = FLOWS + HEATS
RELAX_FLOW = 0.8
RELAX_HEAT = 0.9
WALL_COEFF = 0.5
METAL_GAIN = 0.5

FACE_RIGHT = [(i, 0) for i in range(ALL) if VELOCITY[i][0] >= 0] + [
    (i, 1) for i in range(ALL) if VELOCITY[i][0] == 1
]
FACE_LEFT = [(i, 0) for i in range(ALL) if VELOCITY[i][0] <= 0] + [
    (i, 1) for i in range(ALL) if VELOCITY[i][0] == -1
]
FACES = len(FACE_RIGHT)
UP = [i for i in range(ALL) if VELOCITY[i][2] == 1]
DOWN = [i for i in range(ALL) if VELOCITY[i][2] == -1]
EDGES = len(UP)
SOLID, COUNTS, LISTS = FACES, FACES + 1, FACES + 2
SIDE_PLANES = FACES + 4
LIST_ROWS = 12
LANES = 128
F32 = jnp.float32
BF16 = jnp.bfloat16


def params(mebibytes=32):
    return pltpu.CompilerParams(vmem_limit_bytes=mebibytes * 1024 * 1024)


def in_vmem(count):
    return [pl.BlockSpec(memory_space=pltpu.VMEM)] * count


def shape(*dims):
    return jax.ShapeDtypeStruct(dims, F32)


def split(value):
    high = value.astype(BF16)
    low = (value - high.astype(F32)).astype(BF16)
    return high, low


def split_three(value):
    high = value.astype(BF16)
    rest = value - high.astype(F32)
    middle = rest.astype(BF16)
    low = (rest - middle.astype(F32)).astype(BF16)
    return high, middle, low


def dot(left, right, dims):
    return lax.dot_general(left, right, (dims, ((), ())), preferred_element_type=F32)


def rows_of(row, count):
    return lax.broadcasted_iota(jnp.int32, (count, row.shape[1]), 0) == row


def hot(mask):
    return jnp.where(mask, 1.0, 0.0).astype(BF16)


def pick(rows, row_index, lane_index):
    found = jnp.zeros(lane_index.shape, F32)
    for r, row in enumerate(rows):
        whole = jnp.broadcast_to(row, lane_index.shape)
        value = jnp.take_along_axis(whole, lane_index, axis=1, mode="promise_in_bounds")
        found = jnp.where(row_index == r, value, found)
    return found


def pick_twice(rows, row_index, lane_index):
    first, second = (row_index, lane_index) if len(row_index) == 2 else (row_index * 2, lane_index * 2)
    found = pick(rows, jnp.concatenate(first, axis=0), jnp.concatenate(second, axis=0))
    return [found[4 * n : 4 * n + 4] for n in range(len(row_index))]


def add_up(values, row_mask, lane_hot):
    count = row_mask.shape[0]
    stacked = jnp.concatenate(
        [jnp.where(row_mask, part.astype(F32), 0.0) for part in split(values)], axis=0
    ).astype(BF16)
    sums = dot(stacked, lane_hot, ((1,), (1,)))
    return sums[:count] + sums[count:]


def one_row(block):
    return jnp.concatenate([block[r : r + 1] for r in range(block.shape[0])], axis=1)


def put_rows(ref, start, row):
    for r in range(row.shape[1] // LANES):
        ref[start + r : start + r + 1, :] = row[:, r * LANES : (r + 1) * LANES]


def lists_of(block):
    return [block[4 * n : 4 * n + 4].astype(jnp.int32) for n in range(3)]


def wall_temper(tempers, node):
    rows = [temper[z : z + 1] for temper in tempers for z in range(temper.shape[0])]
    return pick_twice(rows, [node >> 7], [node & 127])[0]


def pack(
    count_ref, heat_ref, metal_ref, node_ref, owner_ref, cell_ref, out_ref, list_ref, counts_ref
):
    blocks = out_ref.shape[0]
    wide, deep, lanes = heat_ref.shape[1:]
    tempers = []
    for x in range(wide):
        temper = heat_ref[0, x]
        for k in range(1, HEATS):
            temper = temper + heat_ref[k, x]
        tempers.append(temper)
    node = node_ref[...]
    cell = cell_ref[...]
    entries = node.shape[1]
    live = lax.broadcasted_iota(jnp.int32, (1, entries), 1) < count_ref[0, 0]
    owner = jnp.where(live, owner_ref[...], -1)
    list_ref[8:16, :] = jnp.zeros((8, lanes), F32)
    put_rows(list_ref, 0, owner.astype(F32))
    put_rows(list_ref, 4, cell.astype(F32))
    put_rows(list_ref, 8, node.astype(F32))
    put_rows(list_ref, LIST_ROWS, metal_ref[...])
    lane_mask = rows_of(node & 127, lanes)
    nodes = list_ref[8:12].astype(jnp.int32)
    wall = one_row(wall_temper(tempers, nodes))
    cell_hot = hot(rows_of(cell & 127, lanes))
    row_mask = rows_of(owner * 2 + (cell >> 7), 2 * blocks)
    sums = add_up(wall, row_mask, cell_hot)
    counts = dot(hot(row_mask), cell_hot, ((1,), (1,)))
    for d in range(blocks):
        put_rows(out_ref.at[d], 0, metal_ref[...])
        out_ref[d, 2:4, :] = sums[2 * d : 2 * d + 2]
        out_ref[d, 4:6, :] = counts[2 * d : 2 * d + 2]
        out_ref[d, 6:8, :] = jnp.zeros((2, lanes), F32)
    at_nodes = dot(
        hot(rows_of(jnp.where(live, node >> 7, -1), wide * deep)), hot(lane_mask), ((1,), (1,))
    )
    counts_ref[...] = at_nodes.reshape(wide, deep, lanes)


def tree(values):
    while len(values) > 1:
        values = [sum(values[n : n + 2][1:], values[n]) for n in range(0, len(values), 2)]
    return values[0]


def collide_flow(flow, solid):
    pairs = range(1, FLOWS, 2)
    gap = {i: flow[i] - flow[i + 1] for i in pairs}
    density = tree([flow[0]] + [flow[i] + flow[i + 1] for i in pairs])
    inverse = 1.0 / density
    speed = []
    for axis in range(3):
        terms = [
            gap[i] if VELOCITY[i][axis] == 1 else -gap[i] for i in pairs if VELOCITY[i][axis] != 0
        ]
        speed.append(tree(terms) * inverse)
    base = 1.0 - 1.5 * (speed[0] * speed[0] + speed[1] * speed[1] + speed[2] * speed[2])
    scaled = {w: density * (w / RELAX_FLOW) for w in sorted(set(WEIGHT_FLOW))}
    keep = 1.0 - 1.0 / RELAX_FLOW
    post = [None] * FLOWS
    rest = scaled[WEIGHT_FLOW[0]] * base + keep * flow[0]
    post[0] = jnp.where(solid, flow[0], rest)
    for i in pairs:
        along = None
        for axis in range(3):
            c = VELOCITY[i][axis]
            if c == 0:
                continue
            term = speed[axis]
            if along is None:
                along = term if c == 1 else -term
            else:
                along = along + term if c == 1 else along - term
        weight = scaled[WEIGHT_FLOW[i]]
        even = weight * (base + 4.5 * along * along)
        odd = weight * (3.0 * along)
        j = OPPOSITE[i]
        post[i] = jnp.where(solid, flow[j], even + odd + keep * flow[i])
        post[j] = jnp.where(solid, flow[i], even - odd + keep * flow[j])
    return post, speed


def collide_heat(heat, temper, speed, solid):
    keep = 1.0 - 1.0 / RELAX_HEAT
    post = [None] * HEATS
    post[0] = jnp.where(
        solid, heat[0], temper * (WEIGHT_HEAT[0] / RELAX_HEAT) + keep * heat[0]
    )
    scaled = temper * (WEIGHT_HEAT[1] / RELAX_HEAT)
    for axis in range(3):
        i = 2 * axis + 1
        j = i + 1
        odd = scaled * (4.0 * speed[axis])
        post[i] = jnp.where(solid, heat[j], scaled + odd + keep * heat[i])
        post[j] = jnp.where(solid, heat[i], scaled - odd + keep * heat[j])
    return post


def lose(post, counts, temper):
    lost = counts * temper * -WALL_COEFF
    return [post[k] + WEIGHT_HEAT[k] * lost for k in range(HEATS)]


def first_kernel(
    count_ref,
    flow_hbm,
    heat_hbm,
    solid_hbm,
    metal_hbm,
    node_hbm,
    owner_hbm,
    cell_hbm,
    chunks_ref,
    list_ref,
    counts_ref,
    solid_ref,
    postf_ref,
    posth_ref,
    senda_ref,
    sendb_ref,
    flow_ref,
    heat_ref,
    mask_ref,
    metal_ref,
    node_ref,
    owner_ref,
    cell_ref,
    sems,
):
    wide = flow_ref.shape[1]
    odd = lax.axis_index("blk") % 2 == 1
    small = [
        pltpu.make_async_copy(source, target, sems.at[n])
        for n, (source, target) in enumerate(
            (
                (heat_hbm, heat_ref),
                (node_hbm, node_ref),
                (owner_hbm, owner_ref),
                (cell_hbm, cell_ref),
                (metal_hbm, metal_ref),
                (solid_hbm, mask_ref),
            )
        )
    ]
    large = pltpu.make_async_copy(flow_hbm, flow_ref, sems.at[len(small)])
    for copy in small + [large]:
        copy.start()
    for copy in small:
        copy.wait()
    pack(
        count_ref,
        heat_ref,
        metal_ref,
        node_ref,
        owner_ref,
        cell_ref,
        chunks_ref,
        list_ref,
        counts_ref,
    )
    solid_ref[...] = mask_ref[...].astype(F32)
    large.wait()
    for x in range(wide):
        flow = [flow_ref[i, x] for i in range(FLOWS)]
        heat = [heat_ref[k, x] for k in range(HEATS)]
        solid = mask_ref[x] != 0
        temper = heat[0]
        for k in range(1, HEATS):
            temper = temper + heat[k]
        post, speed = collide_flow(flow, solid)
        posth = lose(collide_heat(heat, temper, speed, solid), counts_ref[x], temper)
        for i in range(FLOWS):
            postf_ref[i, x] = post[i]
        for k in range(HEATS):
            posth_ref[k, x] = posth[k]

    def plane(i, x):
        return postf_ref[i, x] if i < FLOWS else posth_ref[i - FLOWS, x]

    def fill(right_ref, left_ref):
        for ref, faces, edge in ((right_ref, FACE_RIGHT, wide - 1), (left_ref, FACE_LEFT, 0)):
            for n, (i, depth) in enumerate(faces):
                ref[n] = plane(i, abs(edge - depth))
            ref[SOLID] = solid_ref[edge]
            ref[COUNTS] = counts_ref[edge]
            ref[LISTS] = list_ref[0:8]
            ref[LISTS + 1] = list_ref[8:16]

    @pl.when(odd)
    def _():
        fill(sendb_ref, senda_ref)

    @pl.when(jnp.logical_not(odd))
    def _():
        fill(senda_ref, sendb_ref)


def sides(odd, a_ref, b_ref):
    def low(n):
        return jnp.where(odd, a_ref[n], b_ref[n])

    def high(n):
        return jnp.where(odd, b_ref[n], a_ref[n])

    return low, high


def side_lists(get):
    return lists_of(jnp.concatenate([get(LISTS), get(LISTS + 1)], axis=0))


def planes(postf_ref, posth_ref, low, high, wide, source_ref):
    def get(i, x):
        if x < 0:
            value = low(FACE_RIGHT.index((i, -1 - x)))
        elif x >= wide:
            value = high(FACE_LEFT.index((i, x - wide)))
        elif i < FLOWS:
            value = postf_ref[i, x]
        else:
            value = posth_ref[i - FLOWS, x]
        if i >= FLOWS and source_ref is not None:
            value = value + WEIGHT_HEAT[i - FLOWS] * source_ref[x + 2]
        return value

    return get


def metal_rows(chunks_ref, shift):
    blocks = chunks_ref.shape[0]
    return [chunks_ref[d, shift + h : shift + h + 1] for d in range(blocks) for h in range(2)]


def metal_at(rows, *lists):
    return pick_twice(
        rows,
        [owner * 2 + (cell >> 7) for owner, cell, node in lists],
        [cell & 127 for owner, cell, node in lists],
    )


def give(metal, row, node, count):
    return add_up(
        WALL_COEFF * one_row(metal),
        rows_of(one_row(row), count),
        hot(rows_of(one_row(node) & 127, LANES)),
    )


def give_planes(metal, node, first, planes, deep):
    count = planes * deep
    return give(metal, (node >> 7) - first * deep, node, count).reshape(planes, deep, LANES)


def conduct(conduction, halves):
    vector = jnp.concatenate(halves, axis=1)
    parts = split_three(vector)
    rows = lax.broadcasted_iota(jnp.int32, (16, vector.shape[1]), 0)
    stacked = jnp.zeros((16, vector.shape[1]), F32)
    for r, part in enumerate(parts):
        stacked = jnp.where(rows == r, part.astype(F32), stacked)
    stacked = stacked.astype(BF16)
    out = sum([dot(stacked, part, ((1,), (1,))) for part in split_three(conduction)])
    return out[0:1] + out[1:2] + out[2:3]


def next_metal(conduction, metal, total, count):
    gained = WALL_COEFF * (total - count * metal)
    value = metal + METAL_GAIN * gained
    return conduct(conduction, [value[0:1], value[1:2]])


def along_y(value, i):
    cy = VELOCITY[i][1]
    return pltpu.roll(value, cy % value.shape[1], 1) if cy else value


def shift(value, i):
    cz = VELOCITY[i][2]
    return along_y(pltpu.roll(value, cz % value.shape[0], 0) if cz else value, i)


def source_kernel(
    postf_ref,
    posth_ref,
    recvb_ref,
    recva_ref,
    list_ref,
    chunks_ref,
    conduction_ref,
    up_ref,
    down_ref,
    metal_ref,
    source_ref,
):
    wide, deep, lanes = postf_ref.shape[1:]
    blocks = chunks_ref.shape[0]
    sums = chunks_ref[0]
    for d in range(1, blocks):
        sums = sums + chunks_ref[d]
    count = sums[4:6]
    metal = next_metal(conduction_ref[...], list_ref[LIST_ROWS : LIST_ROWS + 2], sums[2:4], count)
    metal_ref[...] = jnp.zeros(metal_ref.shape, F32)
    put_rows(metal_ref, 0, metal)
    metal_ref[2:4, :] = count
    own = lists_of(list_ref[...])
    found = metal_at(metal_rows(chunks_ref, 0), own)[0]
    source_ref[2 : wide + 2] = give_planes(found, own[2], 0, wide, deep)
    low, high = sides(lax.axis_index("blk") % 2 == 1, recva_ref, recvb_ref)
    before, after = side_lists(low), side_lists(high)
    found = metal_at(metal_rows(chunks_ref, 0), before, after)
    source_ref[0:2] = give_planes(found[0], before[2], wide - 2, 2, deep)
    source_ref[wide + 2 :] = give_planes(found[1], after[2], 0, 2, deep)
    get = planes(postf_ref, posth_ref, low, high, wide, source_ref)

    for ref in (up_ref, down_ref):
        ref[ref.shape[0] - 8 :, :] = jnp.zeros((8, lanes), F32)
    for ref, comps, row in ((up_ref, UP, deep - 1), (down_ref, DOWN, 0)):
        for j in range(wide + 2):
            for n, i in enumerate(comps):
                value = along_y(get(i, j - 1 - VELOCITY[i][0]), i)
                at = j * EDGES + n
                ref[at : at + 1, :] = value[row : row + 1, :]
        at = (wide + 2) * EDGES
        put_rows(ref, at, metal)
        ref[at + 2 : at + 2 + LIST_ROWS, :] = list_ref[0:LIST_ROWS]


def early_kernel(
    postf_ref,
    posth_ref,
    recvb_ref,
    recva_ref,
    source_ref,
    list_ref,
    flow_ref,
    heat_ref,
    wall_ref,
):
    wide, deep, lanes = postf_ref.shape[1:]
    low, high = sides(lax.axis_index("blk") % 2 == 1, recva_ref, recvb_ref)
    get = planes(postf_ref, posth_ref, low, high, wide, source_ref)
    sublane = lax.broadcasted_iota(jnp.int32, (deep, lanes), 0)
    tempers = []
    for x in range(-1, wide + 1):
        temper = None
        for k in range(HEATS):
            i = FLOWS + k
            cx, cy, cz = VELOCITY[i]
            value = shift(get(i, x - cx), i)
            if cz != 0:
                value = jnp.where(sublane == (0 if cz == 1 else deep - 1), 0.0, value)
            heat_ref[k, x + 1] = value
            temper = value if temper is None else temper + value
        if 0 <= x < wide:
            tempers.append(temper)
    node = lists_of(list_ref[...])[2]
    wall_ref[4:8] = jnp.zeros((4, lanes), F32)
    wall_ref[0:4] = wall_temper(tempers, node)
    for x in range(-1, wide + 1):
        for i in range(FLOWS):
            flow_ref[i, x + 1] = shift(get(i, x - VELOCITY[i][0]), i)


def step_kernel(
    flow_ref,
    heat_ref,
    wall_ref,
    recvb_ref,
    recva_ref,
    low_edge_ref,
    high_edge_ref,
    list_ref,
    metal_ref,
    solid_ref,
    counts_ref,
    chunks_hbm,
    outf_ref,
    outh_ref,
    up_ref,
    down_ref,
    out_ref,
    sem,
):
    wide, deep, lanes = solid_ref.shape
    blocks = out_ref.shape[0]
    low, high = sides(lax.axis_index("blk") % 2 == 1, recva_ref, recvb_ref)
    owner, cell, node = lists_of(list_ref[...])
    column = node >> 7
    place, z = lax.div(column, deep), lax.rem(column, deep)
    rows = [
        ref[(x + 2) * EDGES - 1 : (x + 2) * EDGES, :]
        for ref in (low_edge_ref, high_edge_ref)
        for x in range(wide)
    ]
    row_index = jnp.where(z == 0, place, jnp.where(z == deep - 1, wide + place, -1))
    wall = one_row(wall_ref[0:4] + pick_twice(rows, [row_index], [node & 127])[0])
    owner, cell = one_row(owner), one_row(cell)
    row_mask = rows_of(owner * 2 + (cell >> 7), 2 * blocks)
    sums = add_up(wall, row_mask, hot(rows_of(cell & 127, lanes)))
    at = (wide + 2) * EDGES
    below, above = low_edge_ref[at : at + 2, :], high_edge_ref[at : at + 2, :]
    for d in range(blocks):
        out_ref[d, 0:2, :] = metal_ref[0:2]
        out_ref[d, 2:4, :] = below
        out_ref[d, 4:6, :] = above
        out_ref[d, 6:8, :] = sums[2 * d : 2 * d + 2]
    copy = pltpu.make_async_copy(out_ref, chunks_hbm, sem)
    copy.start()
    sublane = lax.broadcasted_iota(jnp.int32, (deep, lanes), 0)

    def whole(value, i, x):
        cz = VELOCITY[i][2]
        if cz == 0:
            return value
        ref, comps, row = (
            (low_edge_ref, UP, 0) if cz == 1 else (high_edge_ref, DOWN, deep - 1)
        )
        at = (x + 1) * EDGES + comps.index(i)
        return jnp.where(sublane == row, ref[at : at + 1, :], value)

    for x in range(-1, wide + 1):
        flow = [whole(flow_ref[i, x + 1], i, x) for i in range(FLOWS)]
        if x < 0:
            solid, counts = low(SOLID) != 0, low(COUNTS)
        elif x >= wide:
            solid, counts = high(SOLID) != 0, high(COUNTS)
        else:
            solid, counts = solid_ref[x] != 0, counts_ref[x]
        post, speed = collide_flow(flow, solid)
        heat = [whole(heat_ref[k, x + 1], FLOWS + k, x) for k in range(HEATS)]
        temper = heat[0]
        for k in range(1, HEATS):
            temper = temper + heat[k]
        posth = lose(collide_heat(heat, temper, speed, solid), counts, temper)
        for i in range(FLOWS):
            outf_ref[i, x + 1] = post[i]
        for k in range(HEATS):
            outh_ref[k, x + 1] = posth[k]

    for ref, comps, row in ((up_ref, UP, deep - 1), (down_ref, DOWN, 0)):
        for x in range(wide):
            for n, i in enumerate(comps):
                at = x + 1 - VELOCITY[i][0]
                value = outf_ref[i, at] if i < FLOWS else outh_ref[i - FLOWS, at]
                ref[n, x] = along_y(value, i)[row : row + 1, :]

    copy.wait()


def stream_kernel(postf_ref, flow_hbm, flow_ref, sems):
    wide = flow_ref.shape[1]
    copies = []
    for n, i in enumerate(range(FLOWS)):
        for x in range(wide):
            flow_ref[i, x] = shift(postf_ref[i, x + 1 - VELOCITY[i][0]], i)
        if i % 4 == 3 or i == FLOWS - 1:
            part = pl.ds(i - i % 4, i % 4 + 1)
            copy = pltpu.make_async_copy(
                flow_ref.at[part], flow_hbm.at[part], sems.at[len(copies)]
            )
            copy.start()
            copies.append(copy)
    for copy in copies:
        copy.wait()


def heat_kernel(
    posth_ref,
    recvb_ref,
    recva_ref,
    list_ref,
    chunks_ref,
    low_edge_ref,
    high_edge_ref,
    metal_ref,
    conduction_ref,
    heat_ref,
    out_ref,
    row_ref,
):
    blocks = chunks_ref.shape[0]
    wide, deep, lanes = heat_ref.shape[1:]
    sums = chunks_ref[0]
    for d in range(1, blocks):
        sums = sums + chunks_ref[d]
    out_ref[...] = next_metal(conduction_ref[...], metal_ref[0:2], sums[6:8], metal_ref[2:4])
    low, high = sides(lax.axis_index("blk") % 2 == 1, recva_ref, recvb_ref)
    own, before, after = lists_of(list_ref[...]), side_lists(low), side_lists(high)
    inner = metal_at(metal_rows(chunks_ref, 0), own)[0]
    found = metal_at(metal_rows(chunks_ref, 0), before, after)
    source = [give_planes(found[0], before[2], wide - 1, 1, deep)]
    source.append(give_planes(inner, own[2], 0, wide, deep))
    source.append(give_planes(found[1], after[2], 0, 1, deep))
    source = jnp.concatenate(source, axis=0)
    for k in range(HEATS):
        i = FLOWS + k
        for x in range(wide):
            at = x + 1 - VELOCITY[i][0]
            heat_ref[k, x] = shift(posth_ref[k, at] + WEIGHT_HEAT[k] * source[at], i)

    at = (wide + 2) * EDGES + 2
    for n, (ref, moved, z) in enumerate(((low_edge_ref, 2, deep - 1), (high_edge_ref, 4, 0))):
        lists = lists_of(ref[at : at + LIST_ROWS, :])
        column = lists[2] >> 7
        row = jnp.where(lax.rem(column, deep) == z, lax.div(column, deep), -1)
        found = metal_at(metal_rows(chunks_ref, moved), lists)[0]
        row_ref[n * wide : (n + 1) * wide] = give(found, row, lists[2], wide)


def edge_kernel(
    heat_ref,
    metal_ref,
    row_ref,
    low_ref,
    high_ref,
    flow_in,
    flow_hbm,
    heat_hbm,
    metal_hbm,
    tilted_ref,
    sems,
):
    wide, deep, lanes = flow_hbm.shape[1:]
    level = HEATS - 2
    sublane = lax.broadcasted_iota(jnp.int32, (deep, lanes), 0)

    copies = [
        pltpu.make_async_copy(
            heat_ref.at[pl.ds(0, level)], heat_hbm.at[pl.ds(0, level)], sems.at[0]
        ),
        pltpu.make_async_copy(metal_ref, metal_hbm, sems.at[1]),
    ]
    for m, (ref, comps, z) in enumerate(((low_ref, UP, 0), (high_ref, DOWN, deep - 1))):
        for n, i in enumerate(comps[:-1]):
            copies.append(
                pltpu.make_async_copy(
                    ref.at[n],
                    flow_hbm.at[i, :, z : z + 1, :],
                    sems.at[3 + m * EDGES + n],
                )
            )
    for copy in copies:
        copy.start()
    for m, (ref, comps, z) in enumerate(((low_ref, UP, 0), (high_ref, DOWN, deep - 1))):
        for x in range(wide):
            given = row_ref[m * wide + x : m * wide + x + 1, :]
            row = ref[EDGES - 1, x] + WEIGHT_HEAT[level + m] * given
            tilted_ref[m, x] = jnp.where(sublane == z, row, heat_ref[level + m, x])
    copies.append(
        pltpu.make_async_copy(tilted_ref, heat_hbm.at[pl.ds(level, 2)], sems.at[2])
    )
    copies[-1].start()
    for copy in copies:
        copy.wait()


def swap(value, axis, offset):
    count = lax.axis_size(axis)
    pairs = []
    for first in range(offset, count + offset, 2):
        one, other = first % count, (first + 1) % count
        pairs += [(one, other), (other, one)]
    return lax.ppermute(value, axis, pairs)


def shift_both(up, down, axis):
    count = lax.axis_size(axis)
    ahead = [(i, (i + 1) % count) for i in range(count)]
    return lax.ppermute(up, axis, ahead), lax.ppermute(down, axis, [(j, i) for i, j in ahead])


def local(
    populations,
    thermal,
    solid_mask,
    metal_temp,
    conduction,
    wall_count,
    wall_node,
    wall_owner,
    wall_cell,
):
    blocks = lax.axis_size("blk")
    wide, deep, lanes = solid_mask.shape
    smem = pl.BlockSpec(memory_space=pltpu.SMEM)
    hbm = pl.BlockSpec(memory_space=pltpu.HBM)
    near_spec = pl.BlockSpec(memory_space=pltpu.VMEM)

    def call(kernel, name, outs, scalars, *args, far=0, scratch=(), out_spec=None, alias=None):
        near = len(args) - far
        held = [pltpu.with_memory_space_constraint(arg, pltpu.HBM) for arg in args[near:]]
        out_spec = out_spec or jax.tree.map(lambda _: near_spec, outs)
        return pl.pallas_call(
            kernel,
            in_specs=[smem] * len(scalars) + in_vmem(near) + [hbm] * far,
            out_specs=out_spec,
            out_shape=outs,
            scratch_shapes=scratch,
            input_output_aliases=alias or {},
            compiler_params=params(),
            name=name,
        )(*scalars, *args[:near], *held)

    def to_all(chunks):
        return lax.all_to_all(chunks, "blk", 0, 0, tiled=True)

    side = shape(SIDE_PLANES, deep, lanes)
    field = shape(wide, deep, lanes)
    flows, heats = shape(FLOWS, wide, deep, lanes), shape(HEATS, wide, deep, lanes)
    chunks, lists, counts, solid, postf, posth, senda, sendb = call(
        first_kernel,
        "collide_first",
        (shape(blocks, 8, lanes), shape(16, lanes), field, field, flows, heats, side, side),
        (wall_count,),
        populations,
        thermal,
        solid_mask,
        metal_temp,
        wall_node,
        wall_owner.reshape(1, -1),
        wall_cell,
        far=7,
        scratch=[
            pltpu.VMEM(flows.shape, F32),
            pltpu.VMEM(heats.shape, F32),
            pltpu.VMEM(field.shape, jnp.int32),
            pltpu.VMEM(metal_temp.shape, F32),
            pltpu.VMEM(wall_node.shape, jnp.int32),
            pltpu.VMEM(wall_node.shape, jnp.int32),
            pltpu.VMEM(wall_node.shape, jnp.int32),
            pltpu.SemaphoreType.DMA((7,)),
        ],
    )
    chunks = to_all(chunks)
    recva = swap(senda, "blk", 0)
    recvb = swap(sendb, "blk", 1)
    edge_count = -(-((wide + 2) * EDGES + 2 + LIST_ROWS) // 8) * 8
    edges = shape(edge_count, lanes)
    up, down, metal, source = call(
        source_kernel,
        "source_first",
        (edges, edges, shape(8, lanes), shape(wide + 4, deep, lanes)),
        (),
        postf,
        posth,
        recvb,
        recva,
        lists,
        chunks,
        conduction,
    )
    low_edge, high_edge = shift_both(up, down, "span")
    flow, heat, wall = call(
        early_kernel,
        "stream_early",
        (
            shape(FLOWS, wide + 2, deep, lanes),
            shape(HEATS, wide + 2, deep, lanes),
            shape(8, lanes),
        ),
        (),
        postf,
        posth,
        recvb,
        recva,
        source,
        lists,
    )
    edges = shape(EDGES, wide, 1, lanes)
    chunk = shape(blocks, 8, lanes)
    chunks, postf, posth, up, down = call(
        step_kernel,
        "collide_second",
        (
            chunk,
            shape(FLOWS, wide + 2, deep, lanes),
            shape(HEATS, wide + 2, deep, lanes),
            edges,
            edges,
        ),
        (),
        flow,
        heat,
        wall,
        recvb,
        recva,
        low_edge,
        high_edge,
        lists,
        metal,
        solid,
        counts,
        scratch=[pltpu.VMEM(chunk.shape, F32), pltpu.SemaphoreType.DMA],
        out_spec=(hbm,) + (near_spec,) * 4,
    )
    chunks = to_all(chunks)
    low_last, high_last = shift_both(up, down, "span")
    part = call(
        stream_kernel,
        "stream_flow",
        flows,
        (),
        postf,
        scratch=[pltpu.VMEM(flows.shape, F32), pltpu.SemaphoreType.DMA((-(-FLOWS // 4),))],
        out_spec=hbm,
    )
    heat, metal, rows = call(
        heat_kernel,
        "stream_heat",
        (heats, shape(*metal_temp.shape), shape(2 * wide, lanes)),
        (),
        posth,
        recvb,
        recva,
        lists,
        chunks,
        low_edge,
        high_edge,
        metal,
        conduction,
    )
    return call(
        edge_kernel,
        "write_last",
        (flows, heats, shape(*metal_temp.shape)),
        (),
        heat,
        metal,
        rows,
        low_last,
        high_last,
        part,
        far=1,
        scratch=[
            pltpu.VMEM((2, wide, deep, lanes), F32),
            pltpu.SemaphoreType.DMA((3 + 2 * EDGES,)),
        ],
        out_spec=(hbm,) * 3,
        alias={5: 0},
    )


def solution(mesh):
    in_specs = (
        P(None, "blk", "span", None),
        P(None, "blk", "span", None),
        P("blk", "span", None),
        P("span", "blk"),
        P("span", "blk"),
        P("span", "blk"),
        P("span", "blk"),
        P("span", "blk", None),
        P("span", "blk"),
    )
    out_specs = (P(None, "blk", "span", None), P(None, "blk", "span", None), P("span", "blk"))
    return jax.shard_map(local, mesh=mesh, in_specs=in_specs, out_specs=out_specs, check_vma=False)
```

```python
import jax
import jax.numpy as jnp
from jax import lax
from jax.experimental import pallas as pl
from jax.experimental.pallas import tpu as pltpu
from jax.sharding import PartitionSpec as P

VELOCITY_FLOW = [
    (0, 0, 0),
    (1, 0, 0),
    (-1, 0, 0),
    (0, 1, 0),
    (0, -1, 0),
    (0, 0, 1),
    (0, 0, -1),
    (1, 1, 0),
    (-1, -1, 0),
    (1, -1, 0),
    (-1, 1, 0),
    (1, 0, 1),
    (-1, 0, -1),
    (1, 0, -1),
    (-1, 0, 1),
    (0, 1, 1),
    (0, -1, -1),
    (0, 1, -1),
    (0, -1, 1),
]
WEIGHT_FLOW = [1.0 / 3.0] + [1.0 / 18.0] * 6 + [1.0 / 36.0] * 12
OPPOSITE = [0, 2, 1, 4, 3, 6, 5, 8, 7, 10, 9, 12, 11, 14, 13, 16, 15, 18, 17]
WEIGHT_HEAT = [0.25] + [0.125] * 6
VELOCITY = VELOCITY_FLOW + VELOCITY_FLOW[:7]
FLOWS, HEATS = 19, 7
ALL = FLOWS + HEATS
RELAX_FLOW = 0.8
RELAX_HEAT = 0.9
WALL_COEFF = 0.5
METAL_GAIN = 0.5

FACE_RIGHT = [(i, 0) for i in range(ALL) if VELOCITY[i][0] >= 0] + [
    (i, 1) for i in range(ALL) if VELOCITY[i][0] == 1
]
FACE_LEFT = [(i, 0) for i in range(ALL) if VELOCITY[i][0] <= 0] + [
    (i, 1) for i in range(ALL) if VELOCITY[i][0] == -1
]
FACES = len(FACE_RIGHT)
UP = [i for i in range(ALL) if VELOCITY[i][2] == 1]
DOWN = [i for i in range(ALL) if VELOCITY[i][2] == -1]
EDGES = len(UP)
SOLID, COUNTS, LISTS = FACES, FACES + 1, FACES + 2
SIDE_PLANES = FACES + 4
LIST_ROWS = 12
LANES = 128
F32 = jnp.float32
BF16 = jnp.bfloat16


def params(mebibytes=32):
    return pltpu.CompilerParams(vmem_limit_bytes=mebibytes * 1024 * 1024)


def in_vmem(count):
    return [pl.BlockSpec(memory_space=pltpu.VMEM)] * count


def shape(*dims):
    return jax.ShapeDtypeStruct(dims, F32)


def split(value):
    high = value.astype(BF16)
    rest = value - high.astype(F32)
    middle = rest.astype(BF16)
    low = (rest - middle.astype(F32)).astype(BF16)
    return high, middle, low


def dot(left, right, dims):
    return lax.dot_general(left, right, (dims, ((), ())), preferred_element_type=F32)


def rows_of(row, count):
    return lax.broadcasted_iota(jnp.int32, (count, row.shape[1]), 0) == row


def hot(mask):
    return jnp.where(mask, 1.0, 0.0).astype(BF16)


def pick(rows, row_index, lane_index):
    found = jnp.zeros(lane_index.shape, F32)
    for r, row in enumerate(rows):
        whole = jnp.broadcast_to(row, lane_index.shape)
        value = jnp.take_along_axis(whole, lane_index, axis=1, mode="promise_in_bounds")
        found = jnp.where(row_index == r, value, found)
    return found


def pick_twice(rows, row_index, lane_index):
    first, second = (row_index, lane_index) if len(row_index) == 2 else (row_index * 2, lane_index * 2)
    found = pick(rows, jnp.concatenate(first, axis=0), jnp.concatenate(second, axis=0))
    return [found[4 * n : 4 * n + 4] for n in range(len(row_index))]


def add_up(values, row_mask, lane_hot):
    count = row_mask.shape[0]
    stacked = jnp.concatenate(
        [jnp.where(row_mask, part.astype(F32), 0.0) for part in split(values)], axis=0
    ).astype(BF16)
    sums = dot(stacked, lane_hot, ((1,), (1,)))
    return sums[:count] + sums[count : 2 * count] + sums[2 * count :]


def one_row(block):
    return jnp.concatenate([block[r : r + 1] for r in range(block.shape[0])], axis=1)


def put_rows(ref, start, row):
    for r in range(row.shape[1] // LANES):
        ref[start + r : start + r + 1, :] = row[:, r * LANES : (r + 1) * LANES]


def rows_from(ref, start, count):
    return jnp.concatenate([ref[start + r] for r in range(count)], axis=0)


def lists_of(block):
    return [block[4 * n : 4 * n + 4].astype(jnp.int32) for n in range(3)]


def wall_temper(tempers, node):
    rows = [temper[z : z + 1] for temper in tempers for z in range(temper.shape[0])]
    return pick_twice(rows, [node >> 7], [node & 127])[0]


def pack(
    count_ref, heat_ref, metal_ref, node_ref, owner_ref, cell_ref, out_ref, list_ref, counts_ref
):
    blocks = out_ref.shape[0]
    wide, deep, lanes = heat_ref.shape[1:]
    tempers = []
    for x in range(wide):
        temper = heat_ref[0, x]
        for k in range(1, HEATS):
            temper = temper + heat_ref[k, x]
        tempers.append(temper)
    node = node_ref[...]
    cell = cell_ref[...]
    entries = node.shape[1]
    live = lax.broadcasted_iota(jnp.int32, (1, entries), 1) < count_ref[0, 0]
    owner = jnp.where(live, owner_ref[...], -1)
    list_ref[8:16, :] = jnp.zeros((8, lanes), F32)
    put_rows(list_ref, 0, owner.astype(F32))
    put_rows(list_ref, 4, cell.astype(F32))
    put_rows(list_ref, 8, node.astype(F32))
    put_rows(list_ref, LIST_ROWS, metal_ref[...])
    lane_mask = rows_of(node & 127, lanes)
    nodes = list_ref[8:12].astype(jnp.int32)
    wall = one_row(wall_temper(tempers, nodes))
    cell_hot = hot(rows_of(cell & 127, lanes))
    row_mask = rows_of(owner * 2 + (cell >> 7), 2 * blocks)
    sums = add_up(wall, row_mask, cell_hot)
    counts = dot(hot(row_mask), cell_hot, ((1,), (1,)))
    for d in range(blocks):
        put_rows(out_ref.at[d], 0, metal_ref[...])
        out_ref[d, 2:4, :] = sums[2 * d : 2 * d + 2]
        out_ref[d, 4:6, :] = counts[2 * d : 2 * d + 2]
        out_ref[d, 6:8, :] = jnp.zeros((2, lanes), F32)
    at_nodes = dot(
        hot(rows_of(jnp.where(live, node >> 7, -1), wide * deep)), hot(lane_mask), ((1,), (1,))
    )
    counts_ref[...] = at_nodes.reshape(wide, deep, lanes)


def tree(values):
    while len(values) > 1:
        values = [sum(values[n : n + 2][1:], values[n]) for n in range(0, len(values), 2)]
    return values[0]


def collide_flow(flow, solid):
    pairs = range(1, FLOWS, 2)
    gap = {i: flow[i] - flow[i + 1] for i in pairs}
    density = tree([flow[0]] + [flow[i] + flow[i + 1] for i in pairs])
    inverse = 1.0 / density
    speed = []
    for axis in range(3):
        terms = [
            gap[i] if VELOCITY[i][axis] == 1 else -gap[i] for i in pairs if VELOCITY[i][axis] != 0
        ]
        speed.append(tree(terms) * inverse)
    base = 1.0 - 1.5 * (speed[0] * speed[0] + speed[1] * speed[1] + speed[2] * speed[2])
    scaled = {w: density * (w / RELAX_FLOW) for w in sorted(set(WEIGHT_FLOW))}
    keep = 1.0 - 1.0 / RELAX_FLOW
    post = [None] * FLOWS
    rest = scaled[WEIGHT_FLOW[0]] * base + keep * flow[0]
    post[0] = jnp.where(solid, flow[0], rest)
    for i in pairs:
        along = None
        for axis in range(3):
            c = VELOCITY[i][axis]
            if c == 0:
                continue
            term = speed[axis]
            if along is None:
                along = term if c == 1 else -term
            else:
                along = along + term if c == 1 else along - term
        weight = scaled[WEIGHT_FLOW[i]]
        even = weight * (base + 4.5 * along * along)
        odd = weight * (3.0 * along)
        j = OPPOSITE[i]
        post[i] = jnp.where(solid, flow[j], even + odd + keep * flow[i])
        post[j] = jnp.where(solid, flow[i], even - odd + keep * flow[j])
    return post, speed


def collide_heat(heat, temper, speed, solid):
    keep = 1.0 - 1.0 / RELAX_HEAT
    post = [None] * HEATS
    post[0] = jnp.where(
        solid, heat[0], temper * (WEIGHT_HEAT[0] / RELAX_HEAT) + keep * heat[0]
    )
    scaled = temper * (WEIGHT_HEAT[1] / RELAX_HEAT)
    for axis in range(3):
        i = 2 * axis + 1
        j = i + 1
        odd = scaled * (4.0 * speed[axis])
        post[i] = jnp.where(solid, heat[j], scaled + odd + keep * heat[i])
        post[j] = jnp.where(solid, heat[i], scaled - odd + keep * heat[j])
    return post


def lose(post, counts, temper):
    lost = counts * temper * -WALL_COEFF
    return [post[k] + WEIGHT_HEAT[k] * lost for k in range(HEATS)]


def first_kernel(
    count_ref,
    flow_hbm,
    heat_hbm,
    solid_hbm,
    metal_hbm,
    node_hbm,
    owner_hbm,
    cell_hbm,
    chunks_ref,
    list_ref,
    counts_ref,
    solid_ref,
    postf_ref,
    posth_ref,
    senda_ref,
    sendb_ref,
    flow_ref,
    heat_ref,
    mask_ref,
    metal_ref,
    node_ref,
    owner_ref,
    cell_ref,
    sems,
):
    wide = flow_ref.shape[1]
    odd = lax.axis_index("blk") % 2 == 1
    small = [
        pltpu.make_async_copy(source, target, sems.at[n])
        for n, (source, target) in enumerate(
            (
                (heat_hbm, heat_ref),
                (node_hbm, node_ref),
                (owner_hbm, owner_ref),
                (cell_hbm, cell_ref),
                (metal_hbm, metal_ref),
                (solid_hbm, mask_ref),
            )
        )
    ]
    large = pltpu.make_async_copy(flow_hbm, flow_ref, sems.at[len(small)])
    for copy in small + [large]:
        copy.start()
    for copy in small:
        copy.wait()
    pack(
        count_ref,
        heat_ref,
        metal_ref,
        node_ref,
        owner_ref,
        cell_ref,
        chunks_ref,
        list_ref,
        counts_ref,
    )
    solid_ref[...] = mask_ref[...].astype(F32)
    large.wait()
    for x in range(wide):
        flow = [flow_ref[i, x] for i in range(FLOWS)]
        heat = [heat_ref[k, x] for k in range(HEATS)]
        solid = mask_ref[x] != 0
        temper = heat[0]
        for k in range(1, HEATS):
            temper = temper + heat[k]
        post, speed = collide_flow(flow, solid)
        posth = lose(collide_heat(heat, temper, speed, solid), counts_ref[x], temper)
        for i in range(FLOWS):
            postf_ref[i, x] = post[i]
        for k in range(HEATS):
            posth_ref[k, x] = posth[k]

    def plane(i, x):
        return postf_ref[i, x] if i < FLOWS else posth_ref[i - FLOWS, x]

    def fill(right_ref, left_ref):
        for ref, faces, edge in ((right_ref, FACE_RIGHT, wide - 1), (left_ref, FACE_LEFT, 0)):
            for n, (i, depth) in enumerate(faces):
                ref[n] = plane(i, abs(edge - depth))
            ref[SOLID] = solid_ref[edge]
            ref[COUNTS] = counts_ref[edge]
            ref[LISTS] = list_ref[0:8]
            ref[LISTS + 1] = list_ref[8:16]

    @pl.when(odd)
    def _():
        fill(sendb_ref, senda_ref)

    @pl.when(jnp.logical_not(odd))
    def _():
        fill(senda_ref, sendb_ref)


def sides(odd, a_ref, b_ref):
    def low(n):
        return jnp.where(odd, a_ref[n], b_ref[n])

    def high(n):
        return jnp.where(odd, b_ref[n], a_ref[n])

    return low, high


def side_lists(get):
    return lists_of(jnp.concatenate([get(LISTS), get(LISTS + 1)], axis=0))


def planes(postf_ref, posth_ref, low, high, wide, source_ref):
    def get(i, x):
        if x < 0:
            value = low(FACE_RIGHT.index((i, -1 - x)))
        elif x >= wide:
            value = high(FACE_LEFT.index((i, x - wide)))
        elif i < FLOWS:
            value = postf_ref[i, x]
        else:
            value = posth_ref[i - FLOWS, x]
        if i >= FLOWS and source_ref is not None:
            value = value + WEIGHT_HEAT[i - FLOWS] * source_ref[x + 2]
        return value

    return get


def metal_rows(chunks_ref, shift):
    blocks = chunks_ref.shape[0]
    return [chunks_ref[d, shift + h : shift + h + 1] for d in range(blocks) for h in range(2)]


def metal_at(rows, *lists):
    return pick_twice(
        rows,
        [owner * 2 + (cell >> 7) for owner, cell, node in lists],
        [cell & 127 for owner, cell, node in lists],
    )


def give(metal, row, node, count):
    return add_up(
        WALL_COEFF * one_row(metal),
        rows_of(one_row(row), count),
        hot(rows_of(one_row(node) & 127, LANES)),
    )


def give_planes(metal, node, first, planes, deep):
    count = planes * deep
    return give(metal, (node >> 7) - first * deep, node, count).reshape(planes, deep, LANES)


def conduct(conduction, halves):
    vector = jnp.concatenate(halves, axis=1)
    parts = split(vector)
    rows = lax.broadcasted_iota(jnp.int32, (16, vector.shape[1]), 0)
    stacked = jnp.zeros((16, vector.shape[1]), F32)
    for r, part in enumerate(parts):
        stacked = jnp.where(rows == r, part.astype(F32), stacked)
    stacked = stacked.astype(BF16)
    out = sum([dot(stacked, part, ((1,), (1,))) for part in split(conduction)])
    return out[0:1] + out[1:2] + out[2:3]


def next_metal(conduction, metal, total, count):
    gained = WALL_COEFF * (total - count * metal)
    value = metal + METAL_GAIN * gained
    return conduct(conduction, [value[0:1], value[1:2]])


def along_y(value, i):
    cy = VELOCITY[i][1]
    return pltpu.roll(value, cy % value.shape[1], 1) if cy else value


def shift(value, i):
    cz = VELOCITY[i][2]
    return along_y(pltpu.roll(value, cz % value.shape[0], 0) if cz else value, i)


def source_kernel(
    postf_ref,
    posth_ref,
    recvb_ref,
    recva_ref,
    list_ref,
    chunks_ref,
    conduction_ref,
    up_ref,
    down_ref,
    metal_ref,
    source_ref,
):
    wide, deep, lanes = postf_ref.shape[1:]
    blocks = chunks_ref.shape[0]
    sums = chunks_ref[0]
    for d in range(1, blocks):
        sums = sums + chunks_ref[d]
    count = sums[4:6]
    metal = next_metal(conduction_ref[...], list_ref[LIST_ROWS : LIST_ROWS + 2], sums[2:4], count)
    metal_ref[...] = jnp.zeros(metal_ref.shape, F32)
    put_rows(metal_ref, 0, metal)
    metal_ref[2:4, :] = count
    own = lists_of(list_ref[...])
    found = metal_at(metal_rows(chunks_ref, 0), own)[0]
    source_ref[2 : wide + 2] = give_planes(found, own[2], 0, wide, deep)
    low, high = sides(lax.axis_index("blk") % 2 == 1, recva_ref, recvb_ref)
    before, after = side_lists(low), side_lists(high)
    found = metal_at(metal_rows(chunks_ref, 0), before, after)
    source_ref[0:2] = give_planes(found[0], before[2], wide - 2, 2, deep)
    source_ref[wide + 2 :] = give_planes(found[1], after[2], 0, 2, deep)
    get = planes(postf_ref, posth_ref, low, high, wide, source_ref)

    for ref, comps, row in ((up_ref, UP, deep - 1), (down_ref, DOWN, 0)):
        for j in range(wide + 2):
            for n, i in enumerate(comps):
                value = along_y(get(i, j - 1 - VELOCITY[i][0]), i)
                at = j * EDGES + n
                ref[at] = value[row : row + 1, :]
        at = (wide + 2) * EDGES
        for r in range(2):
            ref[at + r] = metal[:, r * lanes : (r + 1) * lanes]
        for r in range(LIST_ROWS):
            ref[at + 2 + r] = list_ref[r : r + 1, :]


def early_kernel(
    postf_ref,
    posth_ref,
    recvb_ref,
    recva_ref,
    source_ref,
    list_ref,
    flow_ref,
    heat_ref,
    wall_ref,
):
    wide, deep, lanes = postf_ref.shape[1:]
    low, high = sides(lax.axis_index("blk") % 2 == 1, recva_ref, recvb_ref)
    get = planes(postf_ref, posth_ref, low, high, wide, source_ref)
    sublane = lax.broadcasted_iota(jnp.int32, (deep, lanes), 0)
    tempers = []
    for x in range(-1, wide + 1):
        temper = None
        for k in range(HEATS):
            i = FLOWS + k
            cx, cy, cz = VELOCITY[i]
            value = shift(get(i, x - cx), i)
            if cz != 0:
                value = jnp.where(sublane == (0 if cz == 1 else deep - 1), 0.0, value)
            heat_ref[k, x + 1] = value
            temper = value if temper is None else temper + value
        if 0 <= x < wide:
            tempers.append(temper)
    node = lists_of(list_ref[...])[2]
    wall_ref[4:8] = jnp.zeros((4, lanes), F32)
    wall_ref[0:4] = wall_temper(tempers, node)
    for x in range(-1, wide + 1):
        for i in range(FLOWS):
            flow_ref[i, x + 1] = shift(get(i, x - VELOCITY[i][0]), i)


def step_kernel(
    flow_ref,
    heat_ref,
    wall_ref,
    recvb_ref,
    recva_ref,
    low_edge_ref,
    high_edge_ref,
    list_ref,
    metal_ref,
    solid_ref,
    counts_ref,
    chunks_hbm,
    outf_ref,
    outh_ref,
    up_ref,
    down_ref,
    out_ref,
    sem,
):
    wide, deep, lanes = solid_ref.shape
    blocks = out_ref.shape[0]
    low, high = sides(lax.axis_index("blk") % 2 == 1, recva_ref, recvb_ref)
    owner, cell, node = lists_of(list_ref[...])
    column = node >> 7
    place, z = lax.div(column, deep), lax.rem(column, deep)
    rows = [
        ref[(x + 2) * EDGES - 1]
        for ref in (low_edge_ref, high_edge_ref)
        for x in range(wide)
    ]
    row_index = jnp.where(z == 0, place, jnp.where(z == deep - 1, wide + place, -1))
    wall = one_row(wall_ref[0:4] + pick_twice(rows, [row_index], [node & 127])[0])
    owner, cell = one_row(owner), one_row(cell)
    row_mask = rows_of(owner * 2 + (cell >> 7), 2 * blocks)
    sums = add_up(wall, row_mask, hot(rows_of(cell & 127, lanes)))
    at = (wide + 2) * EDGES
    below, above = rows_from(low_edge_ref, at, 2), rows_from(high_edge_ref, at, 2)
    for d in range(blocks):
        out_ref[d, 0:2, :] = metal_ref[0:2]
        out_ref[d, 2:4, :] = below
        out_ref[d, 4:6, :] = above
        out_ref[d, 6:8, :] = sums[2 * d : 2 * d + 2]
    copy = pltpu.make_async_copy(out_ref, chunks_hbm, sem)
    copy.start()
    sublane = lax.broadcasted_iota(jnp.int32, (deep, lanes), 0)

    def whole(value, i, x):
        cz = VELOCITY[i][2]
        if cz == 0:
            return value
        ref, comps, row = (
            (low_edge_ref, UP, 0) if cz == 1 else (high_edge_ref, DOWN, deep - 1)
        )
        at = (x + 1) * EDGES + comps.index(i)
        return jnp.where(sublane == row, ref[at], value)

    for x in range(-1, wide + 1):
        flow = [whole(flow_ref[i, x + 1], i, x) for i in range(FLOWS)]
        if x < 0:
            solid, counts = low(SOLID) != 0, low(COUNTS)
        elif x >= wide:
            solid, counts = high(SOLID) != 0, high(COUNTS)
        else:
            solid, counts = solid_ref[x] != 0, counts_ref[x]
        post, speed = collide_flow(flow, solid)
        heat = [whole(heat_ref[k, x + 1], FLOWS + k, x) for k in range(HEATS)]
        temper = heat[0]
        for k in range(1, HEATS):
            temper = temper + heat[k]
        posth = lose(collide_heat(heat, temper, speed, solid), counts, temper)
        for i in range(FLOWS):
            outf_ref[i, x + 1] = post[i]
        for k in range(HEATS):
            outh_ref[k, x + 1] = posth[k]

    for ref, comps, row in ((up_ref, UP, deep - 1), (down_ref, DOWN, 0)):
        for x in range(wide):
            for n, i in enumerate(comps):
                at = x + 1 - VELOCITY[i][0]
                value = outf_ref[i, at] if i < FLOWS else outh_ref[i - FLOWS, at]
                ref[n, x] = along_y(value, i)[row : row + 1, :]

    copy.wait()


def stream_kernel(postf_ref, flow_hbm, flow_ref, sems):
    wide = flow_ref.shape[1]
    copies = []
    for n, i in enumerate(range(FLOWS)):
        for x in range(wide):
            flow_ref[i, x] = shift(postf_ref[i, x + 1 - VELOCITY[i][0]], i)
        if i % 4 == 3 or i == FLOWS - 1:
            part = pl.ds(i - i % 4, i % 4 + 1)
            copy = pltpu.make_async_copy(
                flow_ref.at[part], flow_hbm.at[part], sems.at[len(copies)]
            )
            copy.start()
            copies.append(copy)
    for copy in copies:
        copy.wait()


def heat_kernel(
    posth_ref,
    recvb_ref,
    recva_ref,
    list_ref,
    chunks_ref,
    low_edge_ref,
    high_edge_ref,
    metal_ref,
    conduction_ref,
    heat_ref,
    out_ref,
    row_ref,
):
    blocks = chunks_ref.shape[0]
    wide, deep, lanes = heat_ref.shape[1:]
    sums = chunks_ref[0]
    for d in range(1, blocks):
        sums = sums + chunks_ref[d]
    out_ref[...] = next_metal(conduction_ref[...], metal_ref[0:2], sums[6:8], metal_ref[2:4])
    low, high = sides(lax.axis_index("blk") % 2 == 1, recva_ref, recvb_ref)
    own, before, after = lists_of(list_ref[...]), side_lists(low), side_lists(high)
    inner = metal_at(metal_rows(chunks_ref, 0), own)[0]
    found = metal_at(metal_rows(chunks_ref, 0), before, after)
    source = [give_planes(found[0], before[2], wide - 1, 1, deep)]
    source.append(give_planes(inner, own[2], 0, wide, deep))
    source.append(give_planes(found[1], after[2], 0, 1, deep))
    source = jnp.concatenate(source, axis=0)
    for k in range(HEATS):
        i = FLOWS + k
        for x in range(wide):
            at = x + 1 - VELOCITY[i][0]
            heat_ref[k, x] = shift(posth_ref[k, at] + WEIGHT_HEAT[k] * source[at], i)

    at = (wide + 2) * EDGES + 2
    for n, (ref, moved, z) in enumerate(((low_edge_ref, 2, deep - 1), (high_edge_ref, 4, 0))):
        lists = lists_of(rows_from(ref, at, LIST_ROWS))
        column = lists[2] >> 7
        row = jnp.where(lax.rem(column, deep) == z, lax.div(column, deep), -1)
        found = metal_at(metal_rows(chunks_ref, moved), lists)[0]
        row_ref[n * wide : (n + 1) * wide] = give(found, row, lists[2], wide)


def runs(comps):
    starts = [n for n, i in enumerate(comps) if n == 0 or comps[n - 1] != i - 1]
    return [(n, comps[n], end - n) for n, end in zip(starts, starts[1:] + [len(comps)])]


def edge_kernel(
    heat_ref,
    metal_ref,
    row_ref,
    low_ref,
    high_ref,
    flow_in,
    flow_hbm,
    heat_hbm,
    metal_hbm,
    tilted_ref,
    sems,
):
    wide, deep, lanes = flow_hbm.shape[1:]
    level = HEATS - 2
    sublane = lax.broadcasted_iota(jnp.int32, (deep, lanes), 0)

    copies = [
        pltpu.make_async_copy(
            heat_ref.at[pl.ds(0, level)], heat_hbm.at[pl.ds(0, level)], sems.at[0]
        ),
        pltpu.make_async_copy(metal_ref, metal_hbm, sems.at[1]),
    ]
    for m, (ref, comps, z) in enumerate(((low_ref, UP, 0), (high_ref, DOWN, deep - 1))):
        for n, i, count in runs(comps[:-1]):
            copies.append(
                pltpu.make_async_copy(
                    ref.at[pl.ds(n, count)],
                    flow_hbm.at[pl.ds(i, count), :, z : z + 1, :],
                    sems.at[3 + m * EDGES + n],
                )
            )
    for copy in copies:
        copy.start()
    for m, (ref, comps, z) in enumerate(((low_ref, UP, 0), (high_ref, DOWN, deep - 1))):
        for x in range(wide):
            given = row_ref[m * wide + x : m * wide + x + 1, :]
            row = ref[EDGES - 1, x] + WEIGHT_HEAT[level + m] * given
            tilted_ref[m, x] = jnp.where(sublane == z, row, heat_ref[level + m, x])
    copies.append(
        pltpu.make_async_copy(tilted_ref, heat_hbm.at[pl.ds(level, 2)], sems.at[2])
    )
    copies[-1].start()
    for copy in copies:
        copy.wait()


def swap(value, axis, offset):
    count = lax.axis_size(axis)
    pairs = []
    for first in range(offset, count + offset, 2):
        one, other = first % count, (first + 1) % count
        pairs += [(one, other), (other, one)]
    return lax.ppermute(value, axis, pairs)


def shift_both(up, down, axis):
    count = lax.axis_size(axis)
    ahead = [(i, (i + 1) % count) for i in range(count)]
    return lax.ppermute(up, axis, ahead), lax.ppermute(down, axis, [(j, i) for i, j in ahead])


def local(
    populations,
    thermal,
    solid_mask,
    metal_temp,
    conduction,
    wall_count,
    wall_node,
    wall_owner,
    wall_cell,
):
    blocks = lax.axis_size("blk")
    wide, deep, lanes = solid_mask.shape
    smem = pl.BlockSpec(memory_space=pltpu.SMEM)
    hbm = pl.BlockSpec(memory_space=pltpu.HBM)
    near_spec = pl.BlockSpec(memory_space=pltpu.VMEM)

    def call(kernel, name, outs, scalars, *args, far=0, scratch=(), out_spec=None, alias=None):
        near = len(args) - far
        held = [pltpu.with_memory_space_constraint(arg, pltpu.HBM) for arg in args[near:]]
        out_spec = out_spec or jax.tree.map(lambda _: near_spec, outs)
        return pl.pallas_call(
            kernel,
            in_specs=[smem] * len(scalars) + in_vmem(near) + [hbm] * far,
            out_specs=out_spec,
            out_shape=outs,
            scratch_shapes=scratch,
            input_output_aliases=alias or {},
            compiler_params=params(),
            name=name,
        )(*scalars, *args[:near], *held)

    def to_all(chunks):
        return lax.all_to_all(chunks, "blk", 0, 0, tiled=True)

    side = shape(SIDE_PLANES, deep, lanes)
    field = shape(wide, deep, lanes)
    flows, heats = shape(FLOWS, wide, deep, lanes), shape(HEATS, wide, deep, lanes)
    chunks, lists, counts, solid, postf, posth, senda, sendb = call(
        first_kernel,
        "collide_first",
        (shape(blocks, 8, lanes), shape(16, lanes), field, field, flows, heats, side, side),
        (wall_count,),
        populations,
        thermal,
        solid_mask,
        metal_temp,
        wall_node,
        wall_owner.reshape(1, -1),
        wall_cell,
        far=7,
        scratch=[
            pltpu.VMEM(flows.shape, F32),
            pltpu.VMEM(heats.shape, F32),
            pltpu.VMEM(field.shape, jnp.int32),
            pltpu.VMEM(metal_temp.shape, F32),
            pltpu.VMEM(wall_node.shape, jnp.int32),
            pltpu.VMEM(wall_node.shape, jnp.int32),
            pltpu.VMEM(wall_node.shape, jnp.int32),
            pltpu.SemaphoreType.DMA((7,)),
        ],
    )
    chunks = to_all(chunks)
    recva = swap(senda, "blk", 0)
    recvb = swap(sendb, "blk", 1)
    edges = shape((wide + 2) * EDGES + 2 + LIST_ROWS, 1, lanes)
    up, down, metal, source = call(
        source_kernel,
        "source_first",
        (edges, edges, shape(8, lanes), shape(wide + 4, deep, lanes)),
        (),
        postf,
        posth,
        recvb,
        recva,
        lists,
        chunks,
        conduction,
    )
    low_edge, high_edge = shift_both(up, down, "span")
    flow, heat, wall = call(
        early_kernel,
        "stream_early",
        (
            shape(FLOWS, wide + 2, deep, lanes),
            shape(HEATS, wide + 2, deep, lanes),
            shape(8, lanes),
        ),
        (),
        postf,
        posth,
        recvb,
        recva,
        source,
        lists,
    )
    edges = shape(EDGES, wide, 1, lanes)
    chunk = shape(blocks, 8, lanes)
    chunks, postf, posth, up, down = call(
        step_kernel,
        "collide_second",
        (
            chunk,
            shape(FLOWS, wide + 2, deep, lanes),
            shape(HEATS, wide + 2, deep, lanes),
            edges,
            edges,
        ),
        (),
        flow,
        heat,
        wall,
        recvb,
        recva,
        low_edge,
        high_edge,
        lists,
        metal,
        solid,
        counts,
        scratch=[pltpu.VMEM(chunk.shape, F32), pltpu.SemaphoreType.DMA],
        out_spec=(hbm,) + (near_spec,) * 4,
    )
    chunks = to_all(chunks)
    low_last, high_last = shift_both(up, down, "span")
    part = call(
        stream_kernel,
        "stream_flow",
        flows,
        (),
        postf,
        scratch=[pltpu.VMEM(flows.shape, F32), pltpu.SemaphoreType.DMA((-(-FLOWS // 4),))],
        out_spec=hbm,
    )
    heat, metal, rows = call(
        heat_kernel,
        "stream_heat",
        (heats, shape(*metal_temp.shape), shape(2 * wide, lanes)),
        (),
        posth,
        recvb,
        recva,
        lists,
        chunks,
        low_edge,
        high_edge,
        metal,
        conduction,
    )
    return call(
        edge_kernel,
        "write_last",
        (flows, heats, shape(*metal_temp.shape)),
        (),
        heat,
        metal,
        rows,
        low_last,
        high_last,
        part,
        far=1,
        scratch=[
            pltpu.VMEM((2, wide, deep, lanes), F32),
            pltpu.SemaphoreType.DMA((3 + 2 * EDGES,)),
        ],
        out_spec=(hbm,) * 3,
        alias={5: 0},
    )


def solution(mesh):
    in_specs = (
        P(None, "blk", "span", None),
        P(None, "blk", "span", None),
        P("blk", "span", None),
        P("span", "blk"),
        P("span", "blk"),
        P("span", "blk"),
        P("span", "blk"),
        P("span", "blk", None),
        P("span", "blk"),
    )
    out_specs = (P(None, "blk", "span", None), P(None, "blk", "span", None), P("span", "blk"))
    return jax.shard_map(local, mesh=mesh, in_specs=in_specs, out_specs=out_specs, check_vma=False)
```

```python
import jax
import jax.numpy as jnp
from jax import lax
from jax.experimental import pallas as pl
from jax.experimental.pallas import tpu as pltpu
from jax.sharding import PartitionSpec as P

VELOCITY_FLOW = [
    (0, 0, 0),
    (1, 0, 0),
    (-1, 0, 0),
    (0, 1, 0),
    (0, -1, 0),
    (0, 0, 1),
    (0, 0, -1),
    (1, 1, 0),
    (-1, -1, 0),
    (1, -1, 0),
    (-1, 1, 0),
    (1, 0, 1),
    (-1, 0, -1),
    (1, 0, -1),
    (-1, 0, 1),
    (0, 1, 1),
    (0, -1, -1),
    (0, 1, -1),
    (0, -1, 1),
]
WEIGHT_FLOW = [1.0 / 3.0] + [1.0 / 18.0] * 6 + [1.0 / 36.0] * 12
OPPOSITE = [0, 2, 1, 4, 3, 6, 5, 8, 7, 10, 9, 12, 11, 14, 13, 16, 15, 18, 17]
WEIGHT_HEAT = [0.25] + [0.125] * 6
VELOCITY = VELOCITY_FLOW + VELOCITY_FLOW[:7]
FLOWS, HEATS = 19, 7
ALL = FLOWS + HEATS
RELAX_FLOW = 0.8
RELAX_HEAT = 0.9
WALL_COEFF = 0.5
METAL_GAIN = 0.5

FACE_RIGHT = [(i, 0) for i in range(ALL) if VELOCITY[i][0] >= 0] + [
    (i, 1) for i in range(ALL) if VELOCITY[i][0] == 1
]
FACE_LEFT = [(i, 0) for i in range(ALL) if VELOCITY[i][0] <= 0] + [
    (i, 1) for i in range(ALL) if VELOCITY[i][0] == -1
]
FACES = len(FACE_RIGHT)
UP = [i for i in range(ALL) if VELOCITY[i][2] == 1]
DOWN = [i for i in range(ALL) if VELOCITY[i][2] == -1]
EDGES = len(UP)
SOLID, COUNTS, LISTS = FACES, FACES + 1, FACES + 2
SIDE_PLANES = FACES + 4
LIST_ROWS = 12
LANES = 128
F32 = jnp.float32
BF16 = jnp.bfloat16


def params(mebibytes=32):
    return pltpu.CompilerParams(vmem_limit_bytes=mebibytes * 1024 * 1024)


def in_vmem(count):
    return [pl.BlockSpec(memory_space=pltpu.VMEM)] * count


def shape(*dims):
    return jax.ShapeDtypeStruct(dims, F32)


def split(value):
    high = value.astype(BF16)
    rest = value - high.astype(F32)
    middle = rest.astype(BF16)
    low = (rest - middle.astype(F32)).astype(BF16)
    return high, middle, low


def dot(left, right, dims):
    return lax.dot_general(left, right, (dims, ((), ())), preferred_element_type=F32)


def rows_of(row, count):
    return lax.broadcasted_iota(jnp.int32, (count, row.shape[1]), 0) == row


def hot(mask):
    return jnp.where(mask, 1.0, 0.0).astype(BF16)


def pick(rows, row_index, lane_index):
    found = jnp.zeros(lane_index.shape, F32)
    for r, row in enumerate(rows):
        whole = jnp.broadcast_to(row, lane_index.shape)
        value = jnp.take_along_axis(whole, lane_index, axis=1, mode="promise_in_bounds")
        found = jnp.where(row_index == r, value, found)
    return found


def pick_twice(rows, row_index, lane_index):
    first, second = (row_index, lane_index) if len(row_index) == 2 else (row_index * 2, lane_index * 2)
    found = pick(rows, jnp.concatenate(first, axis=0), jnp.concatenate(second, axis=0))
    return [found[4 * n : 4 * n + 4] for n in range(len(row_index))]


def add_up(values, row_mask, lane_hot):
    count = row_mask.shape[0]
    stacked = jnp.concatenate(
        [jnp.where(row_mask, part.astype(F32), 0.0) for part in split(values)], axis=0
    ).astype(BF16)
    sums = dot(stacked, lane_hot, ((1,), (1,)))
    return sums[:count] + sums[count : 2 * count] + sums[2 * count :]


def one_row(block):
    return jnp.concatenate([block[r : r + 1] for r in range(block.shape[0])], axis=1)


def put_rows(ref, start, row):
    for r in range(row.shape[1] // LANES):
        ref[start + r : start + r + 1, :] = row[:, r * LANES : (r + 1) * LANES]


def rows_from(ref, start, count):
    return jnp.concatenate([ref[start + r] for r in range(count)], axis=0)


def lists_of(block):
    return [block[4 * n : 4 * n + 4].astype(jnp.int32) for n in range(3)]


def wall_temper(tempers, node):
    rows = [temper[z : z + 1] for temper in tempers for z in range(temper.shape[0])]
    return pick_twice(rows, [node >> 7], [node & 127])[0]


def pack(
    arrive, count_ref, heat_ref, metal_ref, node_ref, owner_ref, cell_ref, out_ref, list_ref, counts_ref
):
    blocks = out_ref.shape[0]
    wide, deep, lanes = heat_ref.shape[1:]
    node = node_ref[...]
    cell = cell_ref[...]
    entries = node.shape[1]
    live = lax.broadcasted_iota(jnp.int32, (1, entries), 1) < count_ref[0, 0]
    owner = jnp.where(live, owner_ref[...], -1)
    list_ref[8:16, :] = jnp.zeros((8, lanes), F32)
    put_rows(list_ref, 0, owner.astype(F32))
    put_rows(list_ref, 4, cell.astype(F32))
    put_rows(list_ref, 8, node.astype(F32))
    put_rows(list_ref, LIST_ROWS, metal_ref[...])
    lane_mask = rows_of(node & 127, lanes)
    cell_hot = hot(rows_of(cell & 127, lanes))
    row_mask = rows_of(owner * 2 + (cell >> 7), 2 * blocks)
    counts = dot(hot(row_mask), cell_hot, ((1,), (1,)))
    at_nodes = dot(
        hot(rows_of(jnp.where(live, node >> 7, -1), wide * deep)), hot(lane_mask), ((1,), (1,))
    )
    counts_ref[...] = at_nodes.reshape(wide, deep, lanes)
    arrive()
    tempers = []
    for x in range(wide):
        temper = heat_ref[0, x]
        for k in range(1, HEATS):
            temper = temper + heat_ref[k, x]
        tempers.append(temper)
    nodes = list_ref[8:12].astype(jnp.int32)
    wall = one_row(wall_temper(tempers, nodes))
    sums = add_up(wall, row_mask, cell_hot)
    for d in range(blocks):
        put_rows(out_ref.at[d], 0, metal_ref[...])
        out_ref[d, 2:4, :] = sums[2 * d : 2 * d + 2]
        out_ref[d, 4:6, :] = counts[2 * d : 2 * d + 2]
        out_ref[d, 6:8, :] = jnp.zeros((2, lanes), F32)


def tree(values):
    while len(values) > 1:
        values = [sum(values[n : n + 2][1:], values[n]) for n in range(0, len(values), 2)]
    return values[0]


def collide_flow(flow, solid):
    pairs = range(1, FLOWS, 2)
    gap = {i: flow[i] - flow[i + 1] for i in pairs}
    density = tree([flow[0]] + [flow[i] + flow[i + 1] for i in pairs])
    inverse = 1.0 / density
    speed = []
    for axis in range(3):
        terms = [
            gap[i] if VELOCITY[i][axis] == 1 else -gap[i] for i in pairs if VELOCITY[i][axis] != 0
        ]
        speed.append(tree(terms) * inverse)
    base = 1.0 - 1.5 * (speed[0] * speed[0] + speed[1] * speed[1] + speed[2] * speed[2])
    scaled = {w: density * (w / RELAX_FLOW) for w in sorted(set(WEIGHT_FLOW))}
    keep = 1.0 - 1.0 / RELAX_FLOW
    post = [None] * FLOWS
    rest = scaled[WEIGHT_FLOW[0]] * base + keep * flow[0]
    post[0] = jnp.where(solid, flow[0], rest)
    for i in pairs:
        along = None
        for axis in range(3):
            c = VELOCITY[i][axis]
            if c == 0:
                continue
            term = speed[axis]
            if along is None:
                along = term if c == 1 else -term
            else:
                along = along + term if c == 1 else along - term
        weight = scaled[WEIGHT_FLOW[i]]
        even = weight * (base + 4.5 * along * along)
        odd = weight * (3.0 * along)
        j = OPPOSITE[i]
        post[i] = jnp.where(solid, flow[j], even + odd + keep * flow[i])
        post[j] = jnp.where(solid, flow[i], even - odd + keep * flow[j])
    return post, speed


def collide_heat(heat, temper, speed, solid):
    keep = 1.0 - 1.0 / RELAX_HEAT
    post = [None] * HEATS
    post[0] = jnp.where(
        solid, heat[0], temper * (WEIGHT_HEAT[0] / RELAX_HEAT) + keep * heat[0]
    )
    scaled = temper * (WEIGHT_HEAT[1] / RELAX_HEAT)
    for axis in range(3):
        i = 2 * axis + 1
        j = i + 1
        odd = scaled * (4.0 * speed[axis])
        post[i] = jnp.where(solid, heat[j], scaled + odd + keep * heat[i])
        post[j] = jnp.where(solid, heat[i], scaled - odd + keep * heat[j])
    return post


def lose(post, counts, temper):
    lost = counts * temper * -WALL_COEFF
    return [post[k] + WEIGHT_HEAT[k] * lost for k in range(HEATS)]


def first_kernel(
    count_ref,
    flow_hbm,
    heat_hbm,
    solid_hbm,
    metal_hbm,
    node_hbm,
    owner_hbm,
    cell_hbm,
    chunks_ref,
    list_ref,
    counts_ref,
    solid_ref,
    postf_ref,
    posth_ref,
    senda_ref,
    sendb_ref,
    flow_ref,
    heat_ref,
    mask_ref,
    metal_ref,
    node_ref,
    owner_ref,
    cell_ref,
    sems,
):
    wide = flow_ref.shape[1]
    odd = lax.axis_index("blk") % 2 == 1
    small = [
        pltpu.make_async_copy(source, target, sems.at[n])
        for n, (source, target) in enumerate(
            (
                (heat_hbm, heat_ref),
                (node_hbm, node_ref),
                (owner_hbm, owner_ref),
                (cell_hbm, cell_ref),
                (metal_hbm, metal_ref),
                (solid_hbm, mask_ref),
            )
        )
    ]
    strip = wide // 2
    strips = [
        pltpu.make_async_copy(
            flow_hbm.at[:, pl.ds(n * strip, strip)],
            flow_ref.at[:, pl.ds(n * strip, strip)],
            sems.at[len(small) + n],
        )
        for n in range(2)
    ]
    for copy in small[1:5] + [small[0], small[5]] + strips:
        copy.start()
    for copy in small[1:5]:
        copy.wait()
    pack(
        small[0].wait,
        count_ref,
        heat_ref,
        metal_ref,
        node_ref,
        owner_ref,
        cell_ref,
        chunks_ref,
        list_ref,
        counts_ref,
    )
    small[5].wait()
    solid_ref[...] = mask_ref[...].astype(F32)
    for x in range(wide):
        if x % strip == 0:
            strips[x // strip].wait()
        flow = [flow_ref[i, x] for i in range(FLOWS)]
        heat = [heat_ref[k, x] for k in range(HEATS)]
        solid = mask_ref[x] != 0
        temper = heat[0]
        for k in range(1, HEATS):
            temper = temper + heat[k]
        post, speed = collide_flow(flow, solid)
        posth = lose(collide_heat(heat, temper, speed, solid), counts_ref[x], temper)
        for i in range(FLOWS):
            postf_ref[i, x] = post[i]
        for k in range(HEATS):
            posth_ref[k, x] = posth[k]

    def plane(i, x):
        return postf_ref[i, x] if i < FLOWS else posth_ref[i - FLOWS, x]

    def fill(right_ref, left_ref):
        for ref, faces, edge in ((right_ref, FACE_RIGHT, wide - 1), (left_ref, FACE_LEFT, 0)):
            for n, (i, depth) in enumerate(faces):
                ref[n] = plane(i, abs(edge - depth))
            ref[SOLID] = solid_ref[edge]
            ref[COUNTS] = counts_ref[edge]
            ref[LISTS] = list_ref[0:8]
            ref[LISTS + 1] = list_ref[8:16]

    @pl.when(odd)
    def _():
        fill(sendb_ref, senda_ref)

    @pl.when(jnp.logical_not(odd))
    def _():
        fill(senda_ref, sendb_ref)


def sides(odd, a_ref, b_ref):
    def low(n):
        return jnp.where(odd, a_ref[n], b_ref[n])

    def high(n):
        return jnp.where(odd, b_ref[n], a_ref[n])

    return low, high


def side_lists(get):
    return lists_of(jnp.concatenate([get(LISTS), get(LISTS + 1)], axis=0))


def planes(postf_ref, posth_ref, low, high, wide, source_ref):
    def get(i, x):
        if x < 0:
            value = low(FACE_RIGHT.index((i, -1 - x)))
        elif x >= wide:
            value = high(FACE_LEFT.index((i, x - wide)))
        elif i < FLOWS:
            value = postf_ref[i, x]
        else:
            value = posth_ref[i - FLOWS, x]
        if i >= FLOWS and source_ref is not None:
            value = value + WEIGHT_HEAT[i - FLOWS] * source_ref[x + 2]
        return value

    return get


def metal_rows(chunks_ref, shift):
    blocks = chunks_ref.shape[0]
    return [chunks_ref[d, shift + h : shift + h + 1] for d in range(blocks) for h in range(2)]


def metal_at(rows, *lists):
    return pick_twice(
        rows,
        [owner * 2 + (cell >> 7) for owner, cell, node in lists],
        [cell & 127 for owner, cell, node in lists],
    )


def give(metal, row, node, count):
    return add_up(
        WALL_COEFF * one_row(metal),
        rows_of(one_row(row), count),
        hot(rows_of(one_row(node) & 127, LANES)),
    )


def give_planes(metal, node, first, planes, deep):
    count = planes * deep
    return give(metal, (node >> 7) - first * deep, node, count).reshape(planes, deep, LANES)


def conduct(conduction, halves):
    vector = jnp.concatenate(halves, axis=1)
    parts = split(vector)
    rows = lax.broadcasted_iota(jnp.int32, (16, vector.shape[1]), 0)
    stacked = jnp.zeros((16, vector.shape[1]), F32)
    for r, part in enumerate(parts):
        stacked = jnp.where(rows == r, part.astype(F32), stacked)
    stacked = stacked.astype(BF16)
    out = sum([dot(stacked, part, ((1,), (1,))) for part in split(conduction)])
    return out[0:1] + out[1:2] + out[2:3]


def next_metal(conduction, metal, total, count):
    gained = WALL_COEFF * (total - count * metal)
    value = metal + METAL_GAIN * gained
    return conduct(conduction, [value[0:1], value[1:2]])


def along_y(value, i):
    cy = VELOCITY[i][1]
    return pltpu.roll(value, cy % value.shape[1], 1) if cy else value


def shift(value, i):
    cz = VELOCITY[i][2]
    return along_y(pltpu.roll(value, cz % value.shape[0], 0) if cz else value, i)


def source_kernel(
    postf_ref,
    posth_ref,
    recvb_ref,
    recva_ref,
    list_ref,
    chunks_ref,
    conduction_ref,
    up_ref,
    down_ref,
    metal_ref,
    source_ref,
):
    wide, deep, lanes = postf_ref.shape[1:]
    blocks = chunks_ref.shape[0]
    sums = chunks_ref[0]
    for d in range(1, blocks):
        sums = sums + chunks_ref[d]
    count = sums[4:6]
    metal = next_metal(conduction_ref[...], list_ref[LIST_ROWS : LIST_ROWS + 2], sums[2:4], count)
    metal_ref[...] = jnp.zeros(metal_ref.shape, F32)
    put_rows(metal_ref, 0, metal)
    metal_ref[2:4, :] = count
    own = lists_of(list_ref[...])
    found = metal_at(metal_rows(chunks_ref, 0), own)[0]
    source_ref[2 : wide + 2] = give_planes(found, own[2], 0, wide, deep)
    low, high = sides(lax.axis_index("blk") % 2 == 1, recva_ref, recvb_ref)
    before, after = side_lists(low), side_lists(high)
    found = metal_at(metal_rows(chunks_ref, 0), before, after)
    source_ref[0:2] = give_planes(found[0], before[2], wide - 2, 2, deep)
    source_ref[wide + 2 :] = give_planes(found[1], after[2], 0, 2, deep)
    get = planes(postf_ref, posth_ref, low, high, wide, source_ref)

    for ref, comps, row in ((up_ref, UP, deep - 1), (down_ref, DOWN, 0)):
        for j in range(wide + 2):
            for n, i in enumerate(comps):
                value = along_y(get(i, j - 1 - VELOCITY[i][0]), i)
                at = j * EDGES + n
                ref[at] = value[row : row + 1, :]
        at = (wide + 2) * EDGES
        for r in range(2):
            ref[at + r] = metal[:, r * lanes : (r + 1) * lanes]
        for r in range(LIST_ROWS):
            ref[at + 2 + r] = list_ref[r : r + 1, :]


def early_kernel(
    postf_ref,
    posth_ref,
    recvb_ref,
    recva_ref,
    source_ref,
    list_ref,
    flow_ref,
    heat_ref,
    wall_ref,
):
    wide, deep, lanes = postf_ref.shape[1:]
    low, high = sides(lax.axis_index("blk") % 2 == 1, recva_ref, recvb_ref)
    get = planes(postf_ref, posth_ref, low, high, wide, source_ref)
    sublane = lax.broadcasted_iota(jnp.int32, (deep, lanes), 0)
    tempers = []
    for x in range(-1, wide + 1):
        temper = None
        for k in range(HEATS):
            i = FLOWS + k
            cx, cy, cz = VELOCITY[i]
            value = shift(get(i, x - cx), i)
            if cz != 0:
                value = jnp.where(sublane == (0 if cz == 1 else deep - 1), 0.0, value)
            heat_ref[k, x + 1] = value
            temper = value if temper is None else temper + value
        if 0 <= x < wide:
            tempers.append(temper)
    node = lists_of(list_ref[...])[2]
    wall_ref[4:8] = jnp.zeros((4, lanes), F32)
    wall_ref[0:4] = wall_temper(tempers, node)
    for x in range(-1, wide + 1):
        for i in range(FLOWS):
            flow_ref[i, x + 1] = shift(get(i, x - VELOCITY[i][0]), i)


def step_kernel(
    flow_ref,
    heat_ref,
    wall_ref,
    recvb_ref,
    recva_ref,
    low_edge_ref,
    high_edge_ref,
    list_ref,
    metal_ref,
    solid_ref,
    counts_ref,
    chunks_hbm,
    outf_ref,
    outh_ref,
    up_ref,
    down_ref,
    out_ref,
    sem,
):
    wide, deep, lanes = solid_ref.shape
    blocks = out_ref.shape[0]
    low, high = sides(lax.axis_index("blk") % 2 == 1, recva_ref, recvb_ref)
    owner, cell, node = lists_of(list_ref[...])
    column = node >> 7
    place, z = lax.div(column, deep), lax.rem(column, deep)
    rows = [
        ref[(x + 2) * EDGES - 1]
        for ref in (low_edge_ref, high_edge_ref)
        for x in range(wide)
    ]
    row_index = jnp.where(z == 0, place, jnp.where(z == deep - 1, wide + place, -1))
    wall = one_row(wall_ref[0:4] + pick_twice(rows, [row_index], [node & 127])[0])
    owner, cell = one_row(owner), one_row(cell)
    row_mask = rows_of(owner * 2 + (cell >> 7), 2 * blocks)
    sums = add_up(wall, row_mask, hot(rows_of(cell & 127, lanes)))
    at = (wide + 2) * EDGES
    below, above = rows_from(low_edge_ref, at, 2), rows_from(high_edge_ref, at, 2)
    for d in range(blocks):
        out_ref[d, 0:2, :] = metal_ref[0:2]
        out_ref[d, 2:4, :] = below
        out_ref[d, 4:6, :] = above
        out_ref[d, 6:8, :] = sums[2 * d : 2 * d + 2]
    copy = pltpu.make_async_copy(out_ref, chunks_hbm, sem)
    copy.start()
    sublane = lax.broadcasted_iota(jnp.int32, (deep, lanes), 0)

    def whole(value, i, x):
        cz = VELOCITY[i][2]
        if cz == 0:
            return value
        ref, comps, row = (
            (low_edge_ref, UP, 0) if cz == 1 else (high_edge_ref, DOWN, deep - 1)
        )
        at = (x + 1) * EDGES + comps.index(i)
        return jnp.where(sublane == row, ref[at], value)

    for x in range(-1, wide + 1):
        flow = [whole(flow_ref[i, x + 1], i, x) for i in range(FLOWS)]
        if x < 0:
            solid, counts = low(SOLID) != 0, low(COUNTS)
        elif x >= wide:
            solid, counts = high(SOLID) != 0, high(COUNTS)
        else:
            solid, counts = solid_ref[x] != 0, counts_ref[x]
        post, speed = collide_flow(flow, solid)
        heat = [whole(heat_ref[k, x + 1], FLOWS + k, x) for k in range(HEATS)]
        temper = heat[0]
        for k in range(1, HEATS):
            temper = temper + heat[k]
        posth = lose(collide_heat(heat, temper, speed, solid), counts, temper)
        for i in range(FLOWS):
            outf_ref[i, x + 1] = post[i]
        for k in range(HEATS):
            outh_ref[k, x + 1] = posth[k]

    for ref, comps, row in ((up_ref, UP, deep - 1), (down_ref, DOWN, 0)):
        for x in range(wide):
            for n, i in enumerate(comps):
                at = x + 1 - VELOCITY[i][0]
                value = outf_ref[i, at] if i < FLOWS else outh_ref[i - FLOWS, at]
                ref[n, x] = along_y(value, i)[row : row + 1, :]

    copy.wait()


def stream_kernel(postf_ref, flow_hbm, flow_ref, sems):
    wide = flow_ref.shape[1]
    copies = []
    for n, i in enumerate(range(FLOWS)):
        for x in range(wide):
            flow_ref[i, x] = shift(postf_ref[i, x + 1 - VELOCITY[i][0]], i)
        if i % 4 == 3 or i == FLOWS - 1:
            part = pl.ds(i - i % 4, i % 4 + 1)
            copy = pltpu.make_async_copy(
                flow_ref.at[part], flow_hbm.at[part], sems.at[len(copies)]
            )
            copy.start()
            copies.append(copy)
    for copy in copies:
        copy.wait()


def heat_kernel(
    posth_ref,
    recvb_ref,
    recva_ref,
    list_ref,
    chunks_ref,
    low_edge_ref,
    high_edge_ref,
    metal_ref,
    conduction_ref,
    heat_ref,
    out_ref,
    row_ref,
):
    blocks = chunks_ref.shape[0]
    wide, deep, lanes = heat_ref.shape[1:]
    sums = chunks_ref[0]
    for d in range(1, blocks):
        sums = sums + chunks_ref[d]
    out_ref[...] = next_metal(conduction_ref[...], metal_ref[0:2], sums[6:8], metal_ref[2:4])
    low, high = sides(lax.axis_index("blk") % 2 == 1, recva_ref, recvb_ref)
    own, before, after = lists_of(list_ref[...]), side_lists(low), side_lists(high)
    inner = metal_at(metal_rows(chunks_ref, 0), own)[0]
    found = metal_at(metal_rows(chunks_ref, 0), before, after)
    source = [give_planes(found[0], before[2], wide - 1, 1, deep)]
    source.append(give_planes(inner, own[2], 0, wide, deep))
    source.append(give_planes(found[1], after[2], 0, 1, deep))
    source = jnp.concatenate(source, axis=0)
    for k in range(HEATS):
        i = FLOWS + k
        for x in range(wide):
            at = x + 1 - VELOCITY[i][0]
            heat_ref[k, x] = shift(posth_ref[k, at] + WEIGHT_HEAT[k] * source[at], i)

    at = (wide + 2) * EDGES + 2
    for n, (ref, moved, z) in enumerate(((low_edge_ref, 2, deep - 1), (high_edge_ref, 4, 0))):
        lists = lists_of(rows_from(ref, at, LIST_ROWS))
        column = lists[2] >> 7
        row = jnp.where(lax.rem(column, deep) == z, lax.div(column, deep), -1)
        found = metal_at(metal_rows(chunks_ref, moved), lists)[0]
        row_ref[n * wide : (n + 1) * wide] = give(found, row, lists[2], wide)


def runs(comps):
    starts = [n for n, i in enumerate(comps) if n == 0 or comps[n - 1] != i - 1]
    return [(n, comps[n], end - n) for n, end in zip(starts, starts[1:] + [len(comps)])]


def edge_kernel(
    heat_ref,
    metal_ref,
    row_ref,
    low_ref,
    high_ref,
    flow_in,
    flow_hbm,
    heat_hbm,
    metal_hbm,
    tilted_ref,
    sems,
):
    wide, deep, lanes = flow_hbm.shape[1:]
    level = HEATS - 2
    sublane = lax.broadcasted_iota(jnp.int32, (deep, lanes), 0)

    copies = [
        pltpu.make_async_copy(
            heat_ref.at[pl.ds(0, level)], heat_hbm.at[pl.ds(0, level)], sems.at[0]
        ),
        pltpu.make_async_copy(metal_ref, metal_hbm, sems.at[1]),
    ]
    for m, (ref, comps, z) in enumerate(((low_ref, UP, 0), (high_ref, DOWN, deep - 1))):
        for n, i, count in runs(comps[:-1]):
            copies.append(
                pltpu.make_async_copy(
                    ref.at[pl.ds(n, count)],
                    flow_hbm.at[pl.ds(i, count), :, z : z + 1, :],
                    sems.at[3 + m * EDGES + n],
                )
            )
    for copy in copies:
        copy.start()
    for m, (ref, comps, z) in enumerate(((low_ref, UP, 0), (high_ref, DOWN, deep - 1))):
        for x in range(wide):
            given = row_ref[m * wide + x : m * wide + x + 1, :]
            row = ref[EDGES - 1, x] + WEIGHT_HEAT[level + m] * given
            tilted_ref[m, x] = jnp.where(sublane == z, row, heat_ref[level + m, x])
    copies.append(
        pltpu.make_async_copy(tilted_ref, heat_hbm.at[pl.ds(level, 2)], sems.at[2])
    )
    copies[-1].start()
    for copy in copies:
        copy.wait()


def swap(value, axis, offset):
    count = lax.axis_size(axis)
    pairs = []
    for first in range(offset, count + offset, 2):
        one, other = first % count, (first + 1) % count
        pairs += [(one, other), (other, one)]
    return lax.ppermute(value, axis, pairs)


def shift_both(up, down, axis):
    count = lax.axis_size(axis)
    ahead = [(i, (i + 1) % count) for i in range(count)]
    return lax.ppermute(up, axis, ahead), lax.ppermute(down, axis, [(j, i) for i, j in ahead])


def local(
    populations,
    thermal,
    solid_mask,
    metal_temp,
    conduction,
    wall_count,
    wall_node,
    wall_owner,
    wall_cell,
):
    blocks = lax.axis_size("blk")
    wide, deep, lanes = solid_mask.shape
    smem = pl.BlockSpec(memory_space=pltpu.SMEM)
    hbm = pl.BlockSpec(memory_space=pltpu.HBM)
    near_spec = pl.BlockSpec(memory_space=pltpu.VMEM)

    def call(kernel, name, outs, scalars, *args, far=0, scratch=(), out_spec=None, alias=None):
        near = len(args) - far
        held = [pltpu.with_memory_space_constraint(arg, pltpu.HBM) for arg in args[near:]]
        out_spec = out_spec or jax.tree.map(lambda _: near_spec, outs)
        return pl.pallas_call(
            kernel,
            in_specs=[smem] * len(scalars) + in_vmem(near) + [hbm] * far,
            out_specs=out_spec,
            out_shape=outs,
            scratch_shapes=scratch,
            input_output_aliases=alias or {},
            compiler_params=params(),
            name=name,
        )(*scalars, *args[:near], *held)

    def to_all(chunks):
        return lax.all_to_all(chunks, "blk", 0, 0, tiled=True)

    side = shape(SIDE_PLANES, deep, lanes)
    field = shape(wide, deep, lanes)
    flows, heats = shape(FLOWS, wide, deep, lanes), shape(HEATS, wide, deep, lanes)
    chunks, lists, counts, solid, postf, posth, senda, sendb = call(
        first_kernel,
        "collide_first",
        (shape(blocks, 8, lanes), shape(16, lanes), field, field, flows, heats, side, side),
        (wall_count,),
        populations,
        thermal,
        solid_mask,
        metal_temp,
        wall_node,
        wall_owner.reshape(1, -1),
        wall_cell,
        far=7,
        scratch=[
            pltpu.VMEM(flows.shape, F32),
            pltpu.VMEM(heats.shape, F32),
            pltpu.VMEM(field.shape, jnp.int32),
            pltpu.VMEM(metal_temp.shape, F32),
            pltpu.VMEM(wall_node.shape, jnp.int32),
            pltpu.VMEM(wall_node.shape, jnp.int32),
            pltpu.VMEM(wall_node.shape, jnp.int32),
            pltpu.SemaphoreType.DMA((8,)),
        ],
    )
    chunks = to_all(chunks)
    recva = swap(senda, "blk", 0)
    recvb = swap(sendb, "blk", 1)
    edges = shape((wide + 2) * EDGES + 2 + LIST_ROWS, 1, lanes)
    up, down, metal, source = call(
        source_kernel,
        "source_first",
        (edges, edges, shape(8, lanes), shape(wide + 4, deep, lanes)),
        (),
        postf,
        posth,
        recvb,
        recva,
        lists,
        chunks,
        conduction,
    )
    low_edge, high_edge = shift_both(up, down, "span")
    flow, heat, wall = call(
        early_kernel,
        "stream_early",
        (
            shape(FLOWS, wide + 2, deep, lanes),
            shape(HEATS, wide + 2, deep, lanes),
            shape(8, lanes),
        ),
        (),
        postf,
        posth,
        recvb,
        recva,
        source,
        lists,
    )
    edges = shape(EDGES, wide, 1, lanes)
    chunk = shape(blocks, 8, lanes)
    chunks, postf, posth, up, down = call(
        step_kernel,
        "collide_second",
        (
            chunk,
            shape(FLOWS, wide + 2, deep, lanes),
            shape(HEATS, wide + 2, deep, lanes),
            edges,
            edges,
        ),
        (),
        flow,
        heat,
        wall,
        recvb,
        recva,
        low_edge,
        high_edge,
        lists,
        metal,
        solid,
        counts,
        scratch=[pltpu.VMEM(chunk.shape, F32), pltpu.SemaphoreType.DMA],
        out_spec=(hbm,) + (near_spec,) * 4,
    )
    chunks = to_all(chunks)
    low_last, high_last = shift_both(up, down, "span")
    part = call(
        stream_kernel,
        "stream_flow",
        flows,
        (),
        postf,
        scratch=[pltpu.VMEM(flows.shape, F32), pltpu.SemaphoreType.DMA((-(-FLOWS // 4),))],
        out_spec=hbm,
    )
    heat, metal, rows = call(
        heat_kernel,
        "stream_heat",
        (heats, shape(*metal_temp.shape), shape(2 * wide, lanes)),
        (),
        posth,
        recvb,
        recva,
        lists,
        chunks,
        low_edge,
        high_edge,
        metal,
        conduction,
    )
    return call(
        edge_kernel,
        "write_last",
        (flows, heats, shape(*metal_temp.shape)),
        (),
        heat,
        metal,
        rows,
        low_last,
        high_last,
        part,
        far=1,
        scratch=[
            pltpu.VMEM((2, wide, deep, lanes), F32),
            pltpu.SemaphoreType.DMA((3 + 2 * EDGES,)),
        ],
        out_spec=(hbm,) * 3,
        alias={5: 0},
    )


def solution(mesh):
    in_specs = (
        P(None, "blk", "span", None),
        P(None, "blk", "span", None),
        P("blk", "span", None),
        P("span", "blk"),
        P("span", "blk"),
        P("span", "blk"),
        P("span", "blk"),
        P("span", "blk", None),
        P("span", "blk"),
    )
    out_specs = (P(None, "blk", "span", None), P(None, "blk", "span", None), P("span", "blk"))
    return jax.shard_map(local, mesh=mesh, in_specs=in_specs, out_specs=out_specs, check_vma=False)
```

```python
import jax
import jax.numpy as jnp
from jax import lax
from jax.experimental import pallas as pl
from jax.experimental.pallas import tpu as pltpu
from jax.sharding import PartitionSpec as P

VELOCITY_FLOW = [
    (0, 0, 0),
    (1, 0, 0),
    (-1, 0, 0),
    (0, 1, 0),
    (0, -1, 0),
    (0, 0, 1),
    (0, 0, -1),
    (1, 1, 0),
    (-1, -1, 0),
    (1, -1, 0),
    (-1, 1, 0),
    (1, 0, 1),
    (-1, 0, -1),
    (1, 0, -1),
    (-1, 0, 1),
    (0, 1, 1),
    (0, -1, -1),
    (0, 1, -1),
    (0, -1, 1),
]
WEIGHT_FLOW = [1.0 / 3.0] + [1.0 / 18.0] * 6 + [1.0 / 36.0] * 12
OPPOSITE = [0, 2, 1, 4, 3, 6, 5, 8, 7, 10, 9, 12, 11, 14, 13, 16, 15, 18, 17]
WEIGHT_HEAT = [0.25] + [0.125] * 6
VELOCITY = VELOCITY_FLOW + VELOCITY_FLOW[:7]
FLOWS, HEATS = 19, 7
ALL = FLOWS + HEATS
RELAX_FLOW = 0.8
RELAX_HEAT = 0.9
WALL_COEFF = 0.5
METAL_GAIN = 0.5

FACE_RIGHT = [(i, 0) for i in range(ALL) if VELOCITY[i][0] >= 0] + [
    (i, 1) for i in range(ALL) if VELOCITY[i][0] == 1
]
FACE_LEFT = [(i, 0) for i in range(ALL) if VELOCITY[i][0] <= 0] + [
    (i, 1) for i in range(ALL) if VELOCITY[i][0] == -1
]
FACES = len(FACE_RIGHT)
UP = [i for i in range(ALL) if VELOCITY[i][2] == 1]
DOWN = [i for i in range(ALL) if VELOCITY[i][2] == -1]
EDGES = len(UP)
SOLID, COUNTS, LISTS = FACES, FACES + 1, FACES + 2
SIDE_PLANES = FACES + 4
LIST_ROWS = 12
LANES = 128
F32 = jnp.float32
BF16 = jnp.bfloat16


def params(mebibytes=32):
    return pltpu.CompilerParams(vmem_limit_bytes=mebibytes * 1024 * 1024)


def in_vmem(count):
    return [pl.BlockSpec(memory_space=pltpu.VMEM)] * count


def shape(*dims):
    return jax.ShapeDtypeStruct(dims, F32)


def split(value):
    high = value.astype(BF16)
    rest = value - high.astype(F32)
    middle = rest.astype(BF16)
    low = (rest - middle.astype(F32)).astype(BF16)
    return high, middle, low


def dot(left, right, dims):
    return lax.dot_general(left, right, (dims, ((), ())), preferred_element_type=F32)


def rows_of(row, count):
    return lax.broadcasted_iota(jnp.int32, (count, row.shape[1]), 0) == row


def hot(mask):
    return jnp.where(mask, 1.0, 0.0).astype(BF16)


def pick(rows, row_index, lane_index):
    found = jnp.zeros(lane_index.shape, F32)
    for r, row in enumerate(rows):
        whole = jnp.broadcast_to(row, lane_index.shape)
        value = jnp.take_along_axis(whole, lane_index, axis=1, mode="promise_in_bounds")
        found = jnp.where(row_index == r, value, found)
    return found


def pick_twice(rows, row_index, lane_index):
    first, second = (row_index, lane_index) if len(row_index) == 2 else (row_index * 2, lane_index * 2)
    found = pick(rows, jnp.concatenate(first, axis=0), jnp.concatenate(second, axis=0))
    return [found[4 * n : 4 * n + 4] for n in range(len(row_index))]


def add_up(values, row_mask, lane_hot):
    count = row_mask.shape[0]
    stacked = jnp.concatenate(
        [jnp.where(row_mask, part.astype(F32), 0.0) for part in split(values)], axis=0
    ).astype(BF16)
    sums = dot(stacked, lane_hot, ((1,), (1,)))
    return sums[:count] + sums[count : 2 * count] + sums[2 * count :]


def one_row(block):
    return jnp.concatenate([block[r : r + 1] for r in range(block.shape[0])], axis=1)


def put_rows(ref, start, row):
    for r in range(row.shape[1] // LANES):
        ref[start + r : start + r + 1, :] = row[:, r * LANES : (r + 1) * LANES]


def rows_from(ref, start, count):
    return jnp.concatenate([ref[start + r] for r in range(count)], axis=0)


def lists_of(block):
    return [block[4 * n : 4 * n + 4].astype(jnp.int32) for n in range(3)]


def wall_temper(tempers, node):
    rows = [temper[z : z + 1] for temper in tempers for z in range(temper.shape[0])]
    return pick_twice(rows, [node >> 7], [node & 127])[0]


def pack(
    count_ref, heat_ref, metal_ref, node_ref, owner_ref, cell_ref, out_ref, list_ref, counts_ref
):
    blocks = out_ref.shape[0]
    wide, deep, lanes = heat_ref.shape[1:]
    tempers = []
    for x in range(wide):
        temper = heat_ref[0, x]
        for k in range(1, HEATS):
            temper = temper + heat_ref[k, x]
        tempers.append(temper)
    node = node_ref[...]
    cell = cell_ref[...]
    entries = node.shape[1]
    live = lax.broadcasted_iota(jnp.int32, (1, entries), 1) < count_ref[0, 0]
    owner = jnp.where(live, owner_ref[...], -1)
    list_ref[8:16, :] = jnp.zeros((8, lanes), F32)
    put_rows(list_ref, 0, owner.astype(F32))
    put_rows(list_ref, 4, cell.astype(F32))
    put_rows(list_ref, 8, node.astype(F32))
    put_rows(list_ref, LIST_ROWS, metal_ref[...])
    lane_mask = rows_of(node & 127, lanes)
    nodes = list_ref[8:12].astype(jnp.int32)
    wall = one_row(wall_temper(tempers, nodes))
    cell_hot = hot(rows_of(cell & 127, lanes))
    row_mask = rows_of(owner * 2 + (cell >> 7), 2 * blocks)
    sums = add_up(wall, row_mask, cell_hot)
    counts = dot(hot(row_mask), cell_hot, ((1,), (1,)))
    for d in range(blocks):
        put_rows(out_ref.at[d], 0, metal_ref[...])
        out_ref[d, 2:4, :] = sums[2 * d : 2 * d + 2]
        out_ref[d, 4:6, :] = counts[2 * d : 2 * d + 2]
        out_ref[d, 6:8, :] = jnp.zeros((2, lanes), F32)
    at_nodes = dot(
        hot(rows_of(jnp.where(live, node >> 7, -1), wide * deep)), hot(lane_mask), ((1,), (1,))
    )
    counts_ref[...] = at_nodes.reshape(wide, deep, lanes)


def tree(values):
    while len(values) > 1:
        values = [sum(values[n : n + 2][1:], values[n]) for n in range(0, len(values), 2)]
    return values[0]


def collide_flow(flow, solid):
    pairs = range(1, FLOWS, 2)
    gap = {i: flow[i] - flow[i + 1] for i in pairs}
    density = tree([flow[0]] + [flow[i] + flow[i + 1] for i in pairs])
    inverse = 1.0 / density
    speed = []
    for axis in range(3):
        terms = [
            gap[i] if VELOCITY[i][axis] == 1 else -gap[i] for i in pairs if VELOCITY[i][axis] != 0
        ]
        speed.append(tree(terms) * inverse)
    base = 1.0 - 1.5 * (speed[0] * speed[0] + speed[1] * speed[1] + speed[2] * speed[2])
    scaled = {w: density * (w / RELAX_FLOW) for w in sorted(set(WEIGHT_FLOW))}
    keep = 1.0 - 1.0 / RELAX_FLOW
    post = [None] * FLOWS
    rest = scaled[WEIGHT_FLOW[0]] * base + keep * flow[0]
    post[0] = jnp.where(solid, flow[0], rest)
    for i in pairs:
        along = None
        for axis in range(3):
            c = VELOCITY[i][axis]
            if c == 0:
                continue
            term = speed[axis]
            if along is None:
                along = term if c == 1 else -term
            else:
                along = along + term if c == 1 else along - term
        weight = scaled[WEIGHT_FLOW[i]]
        even = weight * (base + 4.5 * along * along)
        odd = weight * (3.0 * along)
        j = OPPOSITE[i]
        post[i] = jnp.where(solid, flow[j], even + odd + keep * flow[i])
        post[j] = jnp.where(solid, flow[i], even - odd + keep * flow[j])
    return post, speed


def collide_heat(heat, temper, speed, solid):
    keep = 1.0 - 1.0 / RELAX_HEAT
    post = [None] * HEATS
    post[0] = jnp.where(
        solid, heat[0], temper * (WEIGHT_HEAT[0] / RELAX_HEAT) + keep * heat[0]
    )
    scaled = temper * (WEIGHT_HEAT[1] / RELAX_HEAT)
    for axis in range(3):
        i = 2 * axis + 1
        j = i + 1
        odd = scaled * (4.0 * speed[axis])
        post[i] = jnp.where(solid, heat[j], scaled + odd + keep * heat[i])
        post[j] = jnp.where(solid, heat[i], scaled - odd + keep * heat[j])
    return post


def lose(post, counts, temper):
    lost = counts * temper * -WALL_COEFF
    return [post[k] + WEIGHT_HEAT[k] * lost for k in range(HEATS)]


def first_kernel(
    count_ref,
    flow_hbm,
    heat_hbm,
    solid_hbm,
    metal_hbm,
    node_hbm,
    owner_hbm,
    cell_hbm,
    chunks_ref,
    list_ref,
    counts_ref,
    solid_ref,
    postf_ref,
    posth_ref,
    senda_ref,
    sendb_ref,
    flow_ref,
    heat_ref,
    mask_ref,
    metal_ref,
    node_ref,
    owner_ref,
    cell_ref,
    sems,
):
    wide = flow_ref.shape[1]
    odd = lax.axis_index("blk") % 2 == 1
    small = [
        pltpu.make_async_copy(source, target, sems.at[n])
        for n, (source, target) in enumerate(
            (
                (heat_hbm, heat_ref),
                (node_hbm, node_ref),
                (owner_hbm, owner_ref),
                (cell_hbm, cell_ref),
                (metal_hbm, metal_ref),
                (solid_hbm, mask_ref),
            )
        )
    ]
    large = pltpu.make_async_copy(flow_hbm, flow_ref, sems.at[len(small)])
    for copy in small + [large]:
        copy.start()
    for copy in small:
        copy.wait()
    pack(
        count_ref,
        heat_ref,
        metal_ref,
        node_ref,
        owner_ref,
        cell_ref,
        chunks_ref,
        list_ref,
        counts_ref,
    )
    solid_ref[...] = mask_ref[...].astype(F32)
    large.wait()
    for x in range(wide):
        flow = [flow_ref[i, x] for i in range(FLOWS)]
        heat = [heat_ref[k, x] for k in range(HEATS)]
        solid = mask_ref[x] != 0
        temper = heat[0]
        for k in range(1, HEATS):
            temper = temper + heat[k]
        post, speed = collide_flow(flow, solid)
        posth = lose(collide_heat(heat, temper, speed, solid), counts_ref[x], temper)
        for i in range(FLOWS):
            postf_ref[i, x] = post[i]
        for k in range(HEATS):
            posth_ref[k, x] = posth[k]

    def plane(i, x):
        return postf_ref[i, x] if i < FLOWS else posth_ref[i - FLOWS, x]

    def fill(right_ref, left_ref):
        for ref, faces, edge in ((right_ref, FACE_RIGHT, wide - 1), (left_ref, FACE_LEFT, 0)):
            for n, (i, depth) in enumerate(faces):
                ref[n] = plane(i, abs(edge - depth))
            ref[SOLID] = solid_ref[edge]
            ref[COUNTS] = counts_ref[edge]
            ref[LISTS] = list_ref[0:8]
            ref[LISTS + 1] = list_ref[8:16]

    @pl.when(odd)
    def _():
        fill(sendb_ref, senda_ref)

    @pl.when(jnp.logical_not(odd))
    def _():
        fill(senda_ref, sendb_ref)


def sides(odd, a_ref, b_ref):
    def low(n):
        return jnp.where(odd, a_ref[n], b_ref[n])

    def high(n):
        return jnp.where(odd, b_ref[n], a_ref[n])

    return low, high


def side_lists(get):
    return lists_of(jnp.concatenate([get(LISTS), get(LISTS + 1)], axis=0))


def planes(postf_ref, posth_ref, low, high, wide, source_ref):
    def get(i, x):
        if x < 0:
            value = low(FACE_RIGHT.index((i, -1 - x)))
        elif x >= wide:
            value = high(FACE_LEFT.index((i, x - wide)))
        elif i < FLOWS:
            value = postf_ref[i, x]
        else:
            value = posth_ref[i - FLOWS, x]
        if i >= FLOWS and source_ref is not None:
            value = value + WEIGHT_HEAT[i - FLOWS] * source_ref[x + 2]
        return value

    return get


def metal_rows(chunks_ref, shift):
    blocks = chunks_ref.shape[0]
    return [chunks_ref[d, shift + h : shift + h + 1] for d in range(blocks) for h in range(2)]


def metal_at(rows, *lists):
    return pick_twice(
        rows,
        [owner * 2 + (cell >> 7) for owner, cell, node in lists],
        [cell & 127 for owner, cell, node in lists],
    )


def give(metal, row, node, count):
    return add_up(
        WALL_COEFF * one_row(metal),
        rows_of(one_row(row), count),
        hot(rows_of(one_row(node) & 127, LANES)),
    )


def give_planes(metal, node, first, planes, deep):
    count = planes * deep
    return give(metal, (node >> 7) - first * deep, node, count).reshape(planes, deep, LANES)


def conduct(conduction, halves):
    vector = jnp.concatenate(halves, axis=1)
    parts = split(vector)
    rows = lax.broadcasted_iota(jnp.int32, (16, vector.shape[1]), 0)
    stacked = jnp.zeros((16, vector.shape[1]), F32)
    for r, part in enumerate(parts):
        stacked = jnp.where(rows == r, part.astype(F32), stacked)
    stacked = stacked.astype(BF16)
    out = sum([dot(stacked, part, ((1,), (1,))) for part in split(conduction)])
    return out[0:1] + out[1:2] + out[2:3]


def next_metal(conduction, metal, total, count):
    gained = WALL_COEFF * (total - count * metal)
    value = metal + METAL_GAIN * gained
    return conduct(conduction, [value[0:1], value[1:2]])


def along_y(value, i):
    cy = VELOCITY[i][1]
    return pltpu.roll(value, cy % value.shape[1], 1) if cy else value


def shift(value, i):
    cz = VELOCITY[i][2]
    return along_y(pltpu.roll(value, cz % value.shape[0], 0) if cz else value, i)


def source_kernel(
    postf_ref,
    posth_ref,
    recvb_ref,
    recva_ref,
    list_ref,
    chunks_ref,
    conduction_ref,
    up_ref,
    down_ref,
    metal_ref,
    source_ref,
):
    wide, deep, lanes = postf_ref.shape[1:]
    blocks = chunks_ref.shape[0]
    own = lists_of(list_ref[...])
    found = metal_at(metal_rows(chunks_ref, 0), own)[0]
    source_ref[2 : wide + 2] = give_planes(found, own[2], 0, wide, deep)
    low, high = sides(lax.axis_index("blk") % 2 == 1, recva_ref, recvb_ref)
    before, after = side_lists(low), side_lists(high)
    found = metal_at(metal_rows(chunks_ref, 0), before, after)
    source_ref[0:2] = give_planes(found[0], before[2], wide - 2, 2, deep)
    source_ref[wide + 2 :] = give_planes(found[1], after[2], 0, 2, deep)
    sums = chunks_ref[0]
    for d in range(1, blocks):
        sums = sums + chunks_ref[d]
    count = sums[4:6]
    metal = next_metal(conduction_ref[...], list_ref[LIST_ROWS : LIST_ROWS + 2], sums[2:4], count)
    metal_ref[...] = jnp.zeros(metal_ref.shape, F32)
    put_rows(metal_ref, 0, metal)
    metal_ref[2:4, :] = count
    get = planes(postf_ref, posth_ref, low, high, wide, source_ref)

    for ref, comps, row in ((up_ref, UP, deep - 1), (down_ref, DOWN, 0)):
        for j in range(wide + 2):
            for n, i in enumerate(comps):
                value = along_y(get(i, j - 1 - VELOCITY[i][0]), i)
                at = j * EDGES + n
                ref[at] = value[row : row + 1, :]
        at = (wide + 2) * EDGES
        for r in range(2):
            ref[at + r] = metal[:, r * lanes : (r + 1) * lanes]
        for r in range(LIST_ROWS):
            ref[at + 2 + r] = list_ref[r : r + 1, :]


def early_kernel(
    postf_ref,
    posth_ref,
    recvb_ref,
    recva_ref,
    source_ref,
    list_ref,
    flow_ref,
    heat_ref,
    wall_ref,
):
    wide, deep, lanes = postf_ref.shape[1:]
    low, high = sides(lax.axis_index("blk") % 2 == 1, recva_ref, recvb_ref)
    get = planes(postf_ref, posth_ref, low, high, wide, source_ref)
    sublane = lax.broadcasted_iota(jnp.int32, (deep, lanes), 0)
    tempers = []
    for x in range(-1, wide + 1):
        temper = None
        for k in range(HEATS):
            i = FLOWS + k
            cx, cy, cz = VELOCITY[i]
            value = shift(get(i, x - cx), i)
            if cz != 0:
                value = jnp.where(sublane == (0 if cz == 1 else deep - 1), 0.0, value)
            heat_ref[k, x + 1] = value
            temper = value if temper is None else temper + value
        if 0 <= x < wide:
            tempers.append(temper)
    node = lists_of(list_ref[...])[2]
    wall_ref[4:8] = jnp.zeros((4, lanes), F32)
    wall_ref[0:4] = wall_temper(tempers, node)
    for x in range(-1, wide + 1):
        for i in range(FLOWS):
            flow_ref[i, x + 1] = shift(get(i, x - VELOCITY[i][0]), i)


def step_kernel(
    flow_ref,
    heat_ref,
    wall_ref,
    recvb_ref,
    recva_ref,
    low_edge_ref,
    high_edge_ref,
    list_ref,
    metal_ref,
    solid_ref,
    counts_ref,
    chunks_hbm,
    outf_ref,
    outh_ref,
    up_ref,
    down_ref,
    out_ref,
    sem,
):
    wide, deep, lanes = solid_ref.shape
    blocks = out_ref.shape[0]
    low, high = sides(lax.axis_index("blk") % 2 == 1, recva_ref, recvb_ref)
    owner, cell, node = lists_of(list_ref[...])
    column = node >> 7
    place, z = lax.div(column, deep), lax.rem(column, deep)
    rows = [
        ref[(x + 2) * EDGES - 1]
        for ref in (low_edge_ref, high_edge_ref)
        for x in range(wide)
    ]
    row_index = jnp.where(z == 0, place, jnp.where(z == deep - 1, wide + place, -1))
    wall = one_row(wall_ref[0:4] + pick_twice(rows, [row_index], [node & 127])[0])
    owner, cell = one_row(owner), one_row(cell)
    row_mask = rows_of(owner * 2 + (cell >> 7), 2 * blocks)
    sums = add_up(wall, row_mask, hot(rows_of(cell & 127, lanes)))
    at = (wide + 2) * EDGES
    below, above = rows_from(low_edge_ref, at, 2), rows_from(high_edge_ref, at, 2)
    for d in range(blocks):
        out_ref[d, 0:2, :] = metal_ref[0:2]
        out_ref[d, 2:4, :] = below
        out_ref[d, 4:6, :] = above
        out_ref[d, 6:8, :] = sums[2 * d : 2 * d + 2]
    copy = pltpu.make_async_copy(out_ref, chunks_hbm, sem)
    copy.start()
    sublane = lax.broadcasted_iota(jnp.int32, (deep, lanes), 0)

    def whole(value, i, x):
        cz = VELOCITY[i][2]
        if cz == 0:
            return value
        ref, comps, row = (
            (low_edge_ref, UP, 0) if cz == 1 else (high_edge_ref, DOWN, deep - 1)
        )
        at = (x + 1) * EDGES + comps.index(i)
        return jnp.where(sublane == row, ref[at], value)

    for x in range(-1, wide + 1):
        flow = [whole(flow_ref[i, x + 1], i, x) for i in range(FLOWS)]
        if x < 0:
            solid, counts = low(SOLID) != 0, low(COUNTS)
        elif x >= wide:
            solid, counts = high(SOLID) != 0, high(COUNTS)
        else:
            solid, counts = solid_ref[x] != 0, counts_ref[x]
        post, speed = collide_flow(flow, solid)
        heat = [whole(heat_ref[k, x + 1], FLOWS + k, x) for k in range(HEATS)]
        temper = heat[0]
        for k in range(1, HEATS):
            temper = temper + heat[k]
        posth = lose(collide_heat(heat, temper, speed, solid), counts, temper)
        for i in range(FLOWS):
            outf_ref[i, x + 1] = post[i]
        for k in range(HEATS):
            outh_ref[k, x + 1] = posth[k]

    for ref, comps, row in ((up_ref, UP, deep - 1), (down_ref, DOWN, 0)):
        for x in range(wide):
            for n, i in enumerate(comps):
                at = x + 1 - VELOCITY[i][0]
                value = outf_ref[i, at] if i < FLOWS else outh_ref[i - FLOWS, at]
                ref[n, x] = along_y(value, i)[row : row + 1, :]

    copy.wait()


def stream_kernel(postf_ref, flow_hbm, flow_ref, sems):
    wide = flow_ref.shape[1]
    copies = []
    for n, i in enumerate(range(FLOWS)):
        for x in range(wide):
            flow_ref[i, x] = shift(postf_ref[i, x + 1 - VELOCITY[i][0]], i)
        if i % 4 == 3 or i == FLOWS - 1:
            part = pl.ds(i - i % 4, i % 4 + 1)
            copy = pltpu.make_async_copy(
                flow_ref.at[part], flow_hbm.at[part], sems.at[len(copies)]
            )
            copy.start()
            copies.append(copy)
    for copy in copies:
        copy.wait()


def heat_kernel(
    posth_ref,
    recvb_ref,
    recva_ref,
    list_ref,
    chunks_ref,
    low_edge_ref,
    high_edge_ref,
    metal_ref,
    conduction_ref,
    heat_ref,
    out_ref,
    row_ref,
):
    blocks = chunks_ref.shape[0]
    wide, deep, lanes = heat_ref.shape[1:]
    sums = chunks_ref[0]
    for d in range(1, blocks):
        sums = sums + chunks_ref[d]
    out_ref[...] = next_metal(conduction_ref[...], metal_ref[0:2], sums[6:8], metal_ref[2:4])
    low, high = sides(lax.axis_index("blk") % 2 == 1, recva_ref, recvb_ref)
    own, before, after = lists_of(list_ref[...]), side_lists(low), side_lists(high)
    inner = metal_at(metal_rows(chunks_ref, 0), own)[0]
    found = metal_at(metal_rows(chunks_ref, 0), before, after)
    source = [give_planes(found[0], before[2], wide - 1, 1, deep)]
    source.append(give_planes(inner, own[2], 0, wide, deep))
    source.append(give_planes(found[1], after[2], 0, 1, deep))
    source = jnp.concatenate(source, axis=0)
    for k in range(HEATS):
        i = FLOWS + k
        for x in range(wide):
            at = x + 1 - VELOCITY[i][0]
            heat_ref[k, x] = shift(posth_ref[k, at] + WEIGHT_HEAT[k] * source[at], i)

    at = (wide + 2) * EDGES + 2
    for n, (ref, moved, z) in enumerate(((low_edge_ref, 2, deep - 1), (high_edge_ref, 4, 0))):
        lists = lists_of(rows_from(ref, at, LIST_ROWS))
        column = lists[2] >> 7
        row = jnp.where(lax.rem(column, deep) == z, lax.div(column, deep), -1)
        found = metal_at(metal_rows(chunks_ref, moved), lists)[0]
        row_ref[n * wide : (n + 1) * wide] = give(found, row, lists[2], wide)


def runs(comps):
    starts = [n for n, i in enumerate(comps) if n == 0 or comps[n - 1] != i - 1]
    return [(n, comps[n], end - n) for n, end in zip(starts, starts[1:] + [len(comps)])]


def edge_kernel(
    heat_ref,
    metal_ref,
    row_ref,
    low_ref,
    high_ref,
    flow_in,
    flow_hbm,
    heat_hbm,
    metal_hbm,
    tilted_ref,
    sems,
):
    wide, deep, lanes = flow_hbm.shape[1:]
    level = HEATS - 2
    sublane = lax.broadcasted_iota(jnp.int32, (deep, lanes), 0)

    copies = [
        pltpu.make_async_copy(
            heat_ref.at[pl.ds(0, level)], heat_hbm.at[pl.ds(0, level)], sems.at[0]
        ),
        pltpu.make_async_copy(metal_ref, metal_hbm, sems.at[1]),
    ]
    for m, (ref, comps, z) in enumerate(((low_ref, UP, 0), (high_ref, DOWN, deep - 1))):
        for n, i, count in runs(comps[:-1]):
            copies.append(
                pltpu.make_async_copy(
                    ref.at[pl.ds(n, count)],
                    flow_hbm.at[pl.ds(i, count), :, z : z + 1, :],
                    sems.at[3 + m * EDGES + n],
                )
            )
    for copy in copies:
        copy.start()
    for m, (ref, comps, z) in enumerate(((low_ref, UP, 0), (high_ref, DOWN, deep - 1))):
        for x in range(wide):
            given = row_ref[m * wide + x : m * wide + x + 1, :]
            row = ref[EDGES - 1, x] + WEIGHT_HEAT[level + m] * given
            tilted_ref[m, x] = jnp.where(sublane == z, row, heat_ref[level + m, x])
    copies.append(
        pltpu.make_async_copy(tilted_ref, heat_hbm.at[pl.ds(level, 2)], sems.at[2])
    )
    copies[-1].start()
    for copy in copies:
        copy.wait()


def swap(value, axis, offset):
    count = lax.axis_size(axis)
    pairs = []
    for first in range(offset, count + offset, 2):
        one, other = first % count, (first + 1) % count
        pairs += [(one, other), (other, one)]
    return lax.ppermute(value, axis, pairs)


def shift_both(up, down, axis):
    count = lax.axis_size(axis)
    ahead = [(i, (i + 1) % count) for i in range(count)]
    return lax.ppermute(up, axis, ahead), lax.ppermute(down, axis, [(j, i) for i, j in ahead])


def local(
    populations,
    thermal,
    solid_mask,
    metal_temp,
    conduction,
    wall_count,
    wall_node,
    wall_owner,
    wall_cell,
):
    blocks = lax.axis_size("blk")
    wide, deep, lanes = solid_mask.shape
    smem = pl.BlockSpec(memory_space=pltpu.SMEM)
    hbm = pl.BlockSpec(memory_space=pltpu.HBM)
    near_spec = pl.BlockSpec(memory_space=pltpu.VMEM)

    def call(kernel, name, outs, scalars, *args, far=0, scratch=(), out_spec=None, alias=None):
        near = len(args) - far
        held = [pltpu.with_memory_space_constraint(arg, pltpu.HBM) for arg in args[near:]]
        out_spec = out_spec or jax.tree.map(lambda _: near_spec, outs)
        return pl.pallas_call(
            kernel,
            in_specs=[smem] * len(scalars) + in_vmem(near) + [hbm] * far,
            out_specs=out_spec,
            out_shape=outs,
            scratch_shapes=scratch,
            input_output_aliases=alias or {},
            compiler_params=params(),
            name=name,
        )(*scalars, *args[:near], *held)

    def to_all(chunks):
        return lax.all_to_all(chunks, "blk", 0, 0, tiled=True)

    side = shape(SIDE_PLANES, deep, lanes)
    field = shape(wide, deep, lanes)
    flows, heats = shape(FLOWS, wide, deep, lanes), shape(HEATS, wide, deep, lanes)
    chunks, lists, counts, solid, postf, posth, senda, sendb = call(
        first_kernel,
        "collide_first",
        (shape(blocks, 8, lanes), shape(16, lanes), field, field, flows, heats, side, side),
        (wall_count,),
        populations,
        thermal,
        solid_mask,
        metal_temp,
        wall_node,
        wall_owner.reshape(1, -1),
        wall_cell,
        far=7,
        scratch=[
            pltpu.VMEM(flows.shape, F32),
            pltpu.VMEM(heats.shape, F32),
            pltpu.VMEM(field.shape, jnp.int32),
            pltpu.VMEM(metal_temp.shape, F32),
            pltpu.VMEM(wall_node.shape, jnp.int32),
            pltpu.VMEM(wall_node.shape, jnp.int32),
            pltpu.VMEM(wall_node.shape, jnp.int32),
            pltpu.SemaphoreType.DMA((7,)),
        ],
    )
    chunks = to_all(chunks)
    recva = swap(senda, "blk", 0)
    recvb = swap(sendb, "blk", 1)
    edges = shape((wide + 2) * EDGES + 2 + LIST_ROWS, 1, lanes)
    up, down, metal, source = call(
        source_kernel,
        "source_first",
        (edges, edges, shape(8, lanes), shape(wide + 4, deep, lanes)),
        (),
        postf,
        posth,
        recvb,
        recva,
        lists,
        chunks,
        conduction,
    )
    low_edge, high_edge = shift_both(up, down, "span")
    flow, heat, wall = call(
        early_kernel,
        "stream_early",
        (
            shape(FLOWS, wide + 2, deep, lanes),
            shape(HEATS, wide + 2, deep, lanes),
            shape(8, lanes),
        ),
        (),
        postf,
        posth,
        recvb,
        recva,
        source,
        lists,
    )
    edges = shape(EDGES, wide, 1, lanes)
    chunk = shape(blocks, 8, lanes)
    chunks, postf, posth, up, down = call(
        step_kernel,
        "collide_second",
        (
            chunk,
            shape(FLOWS, wide + 2, deep, lanes),
            shape(HEATS, wide + 2, deep, lanes),
            edges,
            edges,
        ),
        (),
        flow,
        heat,
        wall,
        recvb,
        recva,
        low_edge,
        high_edge,
        lists,
        metal,
        solid,
        counts,
        scratch=[pltpu.VMEM(chunk.shape, F32), pltpu.SemaphoreType.DMA],
        out_spec=(hbm,) + (near_spec,) * 4,
    )
    chunks = to_all(chunks)
    low_last, high_last = shift_both(up, down, "span")
    part = call(
        stream_kernel,
        "stream_flow",
        flows,
        (),
        postf,
        scratch=[pltpu.VMEM(flows.shape, F32), pltpu.SemaphoreType.DMA((-(-FLOWS // 4),))],
        out_spec=hbm,
    )
    heat, metal, rows = call(
        heat_kernel,
        "stream_heat",
        (heats, shape(*metal_temp.shape), shape(2 * wide, lanes)),
        (),
        posth,
        recvb,
        recva,
        lists,
        chunks,
        low_edge,
        high_edge,
        metal,
        conduction,
    )
    return call(
        edge_kernel,
        "write_last",
        (flows, heats, shape(*metal_temp.shape)),
        (),
        heat,
        metal,
        rows,
        low_last,
        high_last,
        part,
        far=1,
        scratch=[
            pltpu.VMEM((2, wide, deep, lanes), F32),
            pltpu.SemaphoreType.DMA((3 + 2 * EDGES,)),
        ],
        out_spec=(hbm,) * 3,
        alias={5: 0},
    )


def solution(mesh):
    in_specs = (
        P(None, "blk", "span", None),
        P(None, "blk", "span", None),
        P("blk", "span", None),
        P("span", "blk"),
        P("span", "blk"),
        P("span", "blk"),
        P("span", "blk"),
        P("span", "blk", None),
        P("span", "blk"),
    )
    out_specs = (P(None, "blk", "span", None), P(None, "blk", "span", None), P("span", "blk"))
    return jax.shard_map(local, mesh=mesh, in_specs=in_specs, out_specs=out_specs, check_vma=False)
```
